32 devices in a mesh: dp: 16 (over z, x, core), tensor: 2 (over y).
Axes of the slice: x: 2, y: 2, z: 4, core: 2. Of those that a mesh axis runs over, the one named last changes fastest.
Arguments:
- block_input: bfloat16 [2, 64, 197, 768], P(None, 'dp'), may hold values from -6 to 6
- norm_gain: float32 [2, 2, 768], replicated, may hold values from 0.5 to 1.5
- row_bias: float32 [2, 3, 768], replicated, may hold values from -2 to 2
- qkv_weight: bfloat16 [2, 768, 3, 768], P(None, 'dp', None, 'tensor'), may hold values from -0.21875 to 0.21875
- qkv_bias: float32 [2, 2, 768], P(None, None, 'tensor'), may hold values from -2 to 2
- out_weight: bfloat16 [2, 768, 768], P(None, 'dp', 'tensor'), may hold values from -1.25 to 1.25
- mlp_in: bfloat16 [768, 3072], P('dp', 'tensor'), may hold values from -0.21875 to 0.21875
- mlp_in_bias: float32 [3072], P('tensor'), may hold values from -2 to 2
- mlp_out: bfloat16 [768, 3072], P('dp', 'tensor'), may hold values from -0.15625 to 0.15625
- mlp_out_bias: float32 [768], replicated, may hold values from -2 to 2
- router: float32 [768, 4], replicated, may hold values from -0.2 to 0.2
- expert_in: bfloat16 [768, 4, 3072], P('dp', None, 'tensor'), may hold values from -0.21875 to 0.21875
- expert_in_bias: float32 [4, 3072], P(None, 'tensor'), may hold values from -1.5 to 1.5
- expert_out: bfloat16 [768, 4, 3072], P('dp', None, 'tensor'), may hold values from -0.21875 to 0.21875
- expert_out_bias: float32 [4, 768], replicated, may hold values from -1.5 to 1.5
- routes: int32 [2, 64, 197, 2], P(None, 'dp'), may hold values from 0 to 3, as said below
- slot_index: int32 [2, 64, 197, 2], P(None, 'dp'), may hold values from 0 to 393, as said below
- out_grad: bfloat16 [2, 64, 197, 768], P(None, 'dp'), may hold values from -6 to 6
Outputs:
- block_output: bfloat16 [2, 64, 197, 768], P(None, 'dp')
- input_grad: float32 [2, 64, 197, 768], P(None, 'dp')
- norm_gain_grad: float32 [2, 2, 768], replicated
- row_bias_grad: float32 [2, 3, 768], replicated
- qkv_weight_grad: float32 [2, 768, 3, 768], P(None, 'dp', None, 'tensor')
- qkv_bias_grad: float32 [2, 2, 768], P(None, None, 'tensor')
- out_weight_grad: float32 [2, 768, 768], P(None, 'dp', 'tensor')
- mlp_in_grad: float32 [768, 3072], P('dp', 'tensor')
- mlp_in_bias_grad: float32 [3072], P('tensor')
- mlp_out_grad: float32 [768, 3072], P('dp', 'tensor')
- mlp_out_bias_grad: float32 [768], replicated
- router_grad: float32 [768, 4], replicated
- expert_in_grad: float32 [768, 4, 3072], P('dp', None, 'tensor')
- expert_in_bias_grad: float32 [4, 3072], P(None, 'tensor')
- expert_out_grad: float32 [768, 4, 3072], P('dp', None, 'tensor')
- expert_out_bias_grad: float32 [4, 768], replicated
The draws below stay inside these ranges and needn't reach their ends.
Inputs may be any that keep to these rules, and one draw needn't show every extreme that they name: `routes`: in each micro-batch, the 4 images of each index of dp name every expert exactly 394 times, and a token's two experts differ. `slot_index`: in each micro-batch and each index of dp, the routes to one expert carry the slot numbers 0 to 393, each once.
All inputs are finite; a program needn't handle non-finite values.
Results may differ from the reference program's by a relative error of at most 0.018.
Values may be sent and summed in bfloat16 or wider, within the bound.
No kernel may reach another device: no remote copies, remote signals or barrier semaphores. Data moves between devices by JAX's collectives and lax.ppermute only.
A program may use at most 448 MiB of HBM per device.

```python
import jax
import jax.numpy as jnp
from jax import lax

D = 768
HEADS = 12
HD = 64
FF = 3072
EXPERTS = 4
LEN = 197
MICRO = 2
IMGS_DEV = 4
IMAGES = 64
LOAD = 394
CAP = 295
N_DP = 16


def draw_plan(key):
    token_count = IMGS_DEV * LEN
    blocks = MICRO * (IMAGES // IMGS_DEV)

    def draw_block(block_key):
        key_turn, key_swap, key_order, key_ranks = jax.random.split(block_key, 4)
        first_pick = jnp.arange(token_count, dtype=jnp.int32) % EXPERTS
        shift_draw = jax.random.randint(key_turn, (token_count // EXPERTS,), 1, EXPERTS).astype(jnp.int32)
        second = (first_pick + jnp.repeat(shift_draw, EXPERTS)) % EXPERTS
        expert_pair = jnp.stack([first_pick, second], axis=1)
        swap_draw = jax.random.randint(key_swap, (token_count,), 0, 2)
        expert_pair = jnp.where(swap_draw[:, None] == 1, expert_pair[:, ::-1], expert_pair)
        token_order = jax.random.permutation(key_order, token_count)
        expert_pair = expert_pair[token_order].astype(jnp.int32)
        tie_ranks = jax.random.permutation(key_ranks, 2 * token_count).astype(jnp.int32)
        flat_experts = expert_pair.reshape(-1)
        sort_score = flat_experts * (2 * token_count) + tie_ranks
        sorted_at = jnp.argsort(sort_score, stable=True)
        position = jnp.zeros((2 * token_count,), jnp.int32).at[sorted_at].set(jnp.arange(2 * token_count, dtype=jnp.int32))
        slot_numbers = position - flat_experts * LOAD
        return (expert_pair, slot_numbers.reshape(token_count, 2).astype(jnp.int32))
    block_keys = jax.random.split(key, blocks)
    expert_pairs, slot_numbers = jax.vmap(draw_block)(block_keys)
    full_shape = (MICRO, IMAGES, LEN, 2)
    return (expert_pairs.reshape(full_shape), slot_numbers.reshape(full_shape))


def draw_routes(key, part):
    return draw_plan(key)[0]


def draw_slot_index(key, part):
    return draw_plan(key)[1]


def spiked(array, stream_key, source, target, blocks, factor):
    def block_of(axis_at):
        return (jnp.arange(array.shape[axis_at]) // (array.shape[axis_at] // blocks)).reshape((-1,) + (1,) * (array.ndim - 1 - axis_at))

    first = jax.random.permutation(stream_key, blocks)[block_of(target)]
    far = (block_of(target) + blocks // 2) % blocks
    return jnp.where((block_of(source) == first) | (block_of(source) == far), factor * array, array)


def block_levels(own_key, extent, pieces, smallest, high):
    factor_of = 1.0
    for dim, parts in pieces:
        draws = jax.random.uniform(jax.random.fold_in(jax.random.fold_in(own_key, 6), dim), (parts,), jnp.float32, smallest / len(pieces), high / len(pieces))
        factor_of = factor_of * jnp.repeat(jnp.exp(draws), extent[dim] // parts).reshape((-1,) + (1,) * (len(extent) - 1 - dim))
    return factor_of


def scatter_about(stream_key, dims, scale, most, shards=(), kind=jnp.bfloat16):
    values = scale * jax.random.normal(stream_key, dims, jnp.float32)
    if shards:
        values = values * block_levels(stream_key, dims, shards, -0.22, 0.18)
    return jnp.clip(values, -most, most).astype(kind)


def bell_draw_with(rng, dims, scale, limit, cuts, heavy, kind=jnp.bfloat16):
    values = scale * jax.random.normal(rng, dims, jnp.float32)
    if cuts:
        values = values * block_levels(rng, dims, cuts, -0.22, 0.18)
    return jnp.clip(spiked(values, jax.random.fold_in(rng, 3), *heavy), -limit, limit).astype(kind)


def setup_inputs(seed: int = 0) -> dict:
    streams_of = jax.random.split(jax.random.key(seed), 19)
    return {
        "block_input": bell_draw_with(streams_of[0], (MICRO, IMAGES, LEN, D), 1.0, 6.0, ((1, 16),), (1, 3, 16, 2.0)),
        "norm_gain": jnp.clip(1.0 + 0.1 * jax.random.normal(streams_of[1], (2, 2, D), jnp.float32), 0.5, 1.5),
        "row_bias": scatter_about(streams_of[2], (2, 3, D), 0.3, 2.0, (), jnp.float32),
        "qkv_weight": scatter_about(streams_of[3], (2, D, 3, D), D ** -0.5, 0.21875, ((1, 16), (3, 2))),
        "qkv_bias": scatter_about(streams_of[4], (2, 2, D), 0.3, 2.0, ((2, 2),), jnp.float32),
        "out_weight": bell_draw_with(streams_of[5], (2, D, D), (D // 16) ** -0.5, 1.25, ((1, 16), (2, 2)), (2, 1, 16, 2.0)),
        "mlp_in": scatter_about(streams_of[6], (D, FF), D ** -0.5, 0.21875, ((0, 16), (1, 2))),
        "mlp_in_bias": scatter_about(streams_of[7], (FF,), 0.3, 2.0, ((0, 2),), jnp.float32),
        "mlp_out": scatter_about(streams_of[8], (D, FF), (FF // 2) ** -0.5, 0.15625, ((0, 16), (1, 2))),
        "mlp_out_bias": scatter_about(streams_of[9], (D,), 0.3, 2.0, (), jnp.float32),
        "router": scatter_about(streams_of[10], (D, EXPERTS), 0.03, 0.2, (), jnp.float32),
        "expert_in": scatter_about(streams_of[11], (D, EXPERTS, FF), D ** -0.5, 0.21875, ((0, 16), (2, 2))),
        "expert_in_bias": scatter_about(streams_of[12], (EXPERTS, FF), 0.2, 1.5, ((1, 2),), jnp.float32),
        "expert_out": scatter_about(streams_of[13], (D, EXPERTS, FF), (FF // 4) ** -0.5, 0.21875, ((0, 16), (2, 2))),
        "expert_out_bias": scatter_about(streams_of[14], (EXPERTS, D), 0.2, 1.5, (), jnp.float32),
        "routes": draw_routes(jax.random.fold_in(streams_of[18], 71), 0),
        "slot_index": draw_slot_index(jax.random.fold_in(streams_of[18], 71), 0),
        "out_grad": bell_draw_with(streams_of[17], (MICRO, IMAGES, LEN, D), 1.0, 6.0, ((1, 16),), (1, 3, 16, 2.0)),
    }


NORM_EPS = 1e-06
EXACT = lax.Precision.HIGHEST

@jax.custom_vjp
def low(v):
    return lax.optimization_barrier(v.astype(jnp.bfloat16)).astype(jnp.float32)

@jax.custom_vjp
def low_back(v):
    return v

def low_keep(v):
    return (low(v), None)

def low_pass(kept, grad):
    return (grad,)

def back_keep(v):
    return (v, None)

def back_low(kept, grad):
    return (low(grad),)
low.defvjp(low_keep, low_pass)
low_back.defvjp(back_keep, back_low)

def layer_norm(hidden, norm_gain, norm_shift):
    center = lax.optimization_barrier(jnp.mean(hidden, axis=-1, keepdims=True))
    centred = hidden - center
    spread = lax.optimization_barrier(jnp.mean(centred * centred, axis=-1, keepdims=True))
    return centred * lax.rsqrt(spread + NORM_EPS) * norm_gain + norm_shift

def attention(hidden, norm_gain, norm_shift, qkv_weights, qkv_biases, out_matrix, out_biases):
    images = hidden.shape[0] // LEN
    normed = low(layer_norm(hidden, norm_gain, norm_shift))
    projected = jnp.einsum('td,dkf->tkf', normed, qkv_weights, precision=EXACT)
    queries = low(low_back(projected[:, 0] + qkv_biases[0]))
    key_rows = low(low_back(projected[:, 1]))
    values = low(low_back(projected[:, 2] + qkv_biases[1]))
    head_shape = (images, LEN, HEADS, HD)
    scores = jnp.einsum('bqhe,bkhe->bhqk', queries.reshape(head_shape), key_rows.reshape(head_shape), precision=EXACT)
    scores = low_back(scores * HD ** (-0.5))
    row_max = lax.optimization_barrier(jnp.max(scores, axis=-1, keepdims=True))
    weights = jnp.exp(scores - row_max)
    attn_probs = low(weights / lax.optimization_barrier(jnp.sum(weights, axis=-1, keepdims=True)))
    mixed_rows = jnp.einsum('bhqk,bkhe->bqhe', attn_probs, values.reshape(head_shape), precision=EXACT)
    mixed_rows = low(low_back(mixed_rows.reshape(hidden.shape[0], D)))
    branch = jnp.einsum('tf,of->to', mixed_rows, out_matrix, precision=EXACT) + out_biases
    return hidden + low_back(branch)

def feed_forward(hidden, norm_gain, norm_shift, in_matrix, in_biases, out_matrix, out_biases):
    normed = low(layer_norm(hidden, norm_gain, norm_shift))
    preact = low_back(jnp.dot(normed, in_matrix, precision=EXACT) + in_biases)
    active = low(jax.nn.gelu(preact))
    branch = jnp.einsum('tf,df->td', active, out_matrix, precision=EXACT) + out_biases
    return hidden + low_back(branch)

def mixture(hidden, norm_gain, norm_shift, router_matrix, in_matrix, in_biases, out_matrix, out_biases, route_ids, slot_ids):
    token_count = hidden.shape[0]
    normed = layer_norm(hidden, norm_gain, norm_shift)
    logits = jnp.dot(normed, router_matrix, precision=EXACT)
    logits = logits - lax.optimization_barrier(jnp.max(logits, axis=-1, keepdims=True))
    weights = jnp.exp(logits)
    gate_probs = weights / lax.optimization_barrier(jnp.sum(weights, axis=-1, keepdims=True))
    kept_mask = slot_ids < CAP
    chosen = jnp.take_along_axis(gate_probs, route_ids, axis=1) * kept_mask.astype(jnp.float32)
    place_index = jnp.where(kept_mask, route_ids * CAP + slot_ids, EXPERTS * CAP).astype(jnp.int32)
    token_ids = jnp.broadcast_to(jnp.arange(token_count, dtype=jnp.int32)[:, None], (token_count, 2))
    owner_row = jnp.zeros((EXPERTS * CAP,), jnp.int32).at[place_index.reshape(-1)].set(token_ids.reshape(-1), mode='drop')
    token_rows = low(normed)[owner_row].reshape(EXPERTS, CAP, D)
    preact = low_back(jnp.einsum('ecd,def->ecf', token_rows, in_matrix, precision=EXACT) + in_biases[:, None, :])
    active = low(jax.nn.gelu(preact))
    result = jnp.einsum('ecf,def->ecd', active, out_matrix, precision=EXACT) + out_biases[:, None, :]
    result = low_back(result).reshape(EXPERTS * CAP, D)
    safe_place = jnp.where(kept_mask, place_index, 0).astype(jnp.int32)
    combined = lax.optimization_barrier(jnp.sum(chosen[:, :, None] * result[safe_place], axis=1))
    return hidden + combined

def layer_pair(hidden, weight_list, route_ids, slot_ids):
    gain_all, bias_all, qkv_all, qkv_bias_all, out_all, first_in, first_in_bias, first_out, first_out_bias, router_matrix, second_in, second_in_bias, second_out, second_out_bias = weight_list
    hidden = attention(hidden, gain_all[0, 0], bias_all[0, 0], qkv_all[0], qkv_bias_all[0], out_all[0], bias_all[0, 2])
    hidden = feed_forward(hidden, gain_all[0, 1], bias_all[0, 1], first_in, first_in_bias, first_out, first_out_bias)
    hidden = attention(hidden, gain_all[1, 0], bias_all[1, 0], qkv_all[1], qkv_bias_all[1], out_all[1], bias_all[1, 2])
    return mixture(hidden, gain_all[1, 1], bias_all[1, 1], router_matrix, second_in, second_in_bias, second_out, second_out_bias, route_ids, slot_ids)

def reference(block_input, norm_gain, row_bias, qkv_weight, qkv_bias, out_weight, mlp_in, mlp_in_bias, mlp_out, mlp_out_bias, router, expert_in, expert_in_bias, expert_out, expert_out_bias, routes, slot_index, out_grad):
    params = tuple((piece.astype(jnp.float32) for piece in (norm_gain, row_bias, qkv_weight, qkv_bias, out_weight, mlp_in, mlp_in_bias, mlp_out, mlp_out_bias, router, expert_in, expert_in_bias, expert_out, expert_out_bias)))
    blocks = MICRO * N_DP
    token_count = IMGS_DEV * LEN
    inputs = block_input.astype(jnp.float32).reshape(blocks, token_count, D)
    cotangents = out_grad.astype(jnp.float32).reshape(blocks, token_count, D)
    route_blocks = routes.reshape(blocks, token_count, 2)
    slot_blocks = slot_index.reshape(blocks, token_count, 2)

    def block_step(totals, block_items):
        hidden, cotangent, route_ids, slot_ids = block_items

        def forward(hidden_in, *weight_list):
            return layer_pair(hidden_in, weight_list, route_ids, slot_ids)
        layer_out, pullback = jax.vjp(forward, hidden, *params)
        weight_grads = pullback(cotangent)
        totals = tuple((left + right for left, right in zip(totals, weight_grads[1:])))
        return (totals, (layer_out.astype(jnp.bfloat16), weight_grads[0]))
    zero_grads = tuple((jnp.zeros_like(piece) for piece in params))
    totals, (outputs, d_inputs) = lax.scan(block_step, zero_grads, (inputs, cotangents, route_blocks, slot_blocks))
    full_shape = (MICRO, N_DP * IMGS_DEV, LEN, D)
    return (outputs.reshape(full_shape), d_inputs.reshape(full_shape), totals[0], totals[1], totals[2], totals[3], totals[4], totals[5], totals[6], totals[7], totals[8], totals[9], totals[10], totals[11], totals[12], totals[13])
```

```python
import functools

import jax
import jax.numpy as jnp
from jax import lax
from jax.experimental import pallas as pl
from jax.experimental.pallas import tpu as pltpu
from jax.sharding import PartitionSpec as P

HD = 64
CAP = 295
NORM_EPS = 1e-06
EXACT = lax.Precision.HIGHEST
BF = jnp.bfloat16
F32 = jnp.float32
VMEM_LIMIT = 58 * 1024 * 1024
FF_BLOCK = 512
ROW_PAD = 16
GELU_SLOPE = 0.7978845608028654
GELU_CUBE = 0.044715


def round_up(value, unit):
    return -(-value // unit) * unit


def mm(left, right):
    return jnp.dot(left, right, preferred_element_type=F32)


def mm_bt(left, right):
    return lax.dot_general(left, right, (((1,), (1,)), ((), ())), preferred_element_type=F32)


def mm_at(left, right):
    return lax.dot_general(left, right, (((0,), (0,)), ((), ())), preferred_element_type=F32)


def norm_parts(hidden):
    center = jnp.mean(hidden, axis=-1, keepdims=True)
    centred = hidden - center
    spread = jnp.mean(centred * centred, axis=-1, keepdims=True)
    scale = lax.rsqrt(spread + NORM_EPS)
    return centred * scale, scale


def norm_pull(unit, scale, gain, incoming):
    wide = incoming * gain
    mean_wide = jnp.mean(wide, axis=-1, keepdims=True)
    mean_dot = jnp.mean(wide * unit, axis=-1, keepdims=True)
    hidden_grad = scale * (wide - mean_wide - unit * mean_dot)
    gain_grad = jnp.sum(incoming * unit, axis=0, keepdims=True)
    shift_grad = jnp.sum(incoming, axis=0, keepdims=True)
    return hidden_grad, gain_grad, shift_grad


def gelu_pair(preact):
    square = preact * preact
    inner = GELU_SLOPE * preact * (1.0 + GELU_CUBE * square)
    bend = jnp.tanh(inner)
    half = 0.5 * (1.0 + bend)
    active = preact * half
    slope = half + 0.5 * preact * (1.0 - bend * bend) * (
        GELU_SLOPE * (1.0 + 3.0 * GELU_CUBE * square)
    )
    return active, slope


def gelu_value(preact):
    square = preact * preact
    inner = GELU_SLOPE * preact * (1.0 + GELU_CUBE * square)
    return 0.5 * preact * (1.0 + jnp.tanh(inner))


def call(kernel, grid, in_specs, out_specs, out_shape, scratch, flops, traffic, name):
    return pl.pallas_call(
        kernel,
        grid=grid,
        in_specs=in_specs,
        out_specs=out_specs,
        out_shape=out_shape,
        scratch_shapes=scratch,
        name=name,
        compiler_params=pltpu.CompilerParams(
            vmem_limit_bytes=VMEM_LIMIT,
            dimension_semantics=("arbitrary",) * len(grid),
        ),
        cost_estimate=pl.CostEstimate(
            flops=int(flops), bytes_accessed=int(traffic), transcendentals=0
        ),
    )


def whole(shape):
    zeros = (0,) * len(shape)
    return pl.BlockSpec(shape, lambda *_: zeros, pipeline_mode=pl.Buffered(1))


def rows_of(block, width):
    return pl.BlockSpec((block, width), lambda step: (step, 0))


def attn_fwd_kernel(
    length, pad, heads, router_on,
    h_ref, g_ref, b_ref, w_ref, qb_ref, ob_ref, *rest,
):
    if router_on:
        g2_ref, b2_ref, rt_ref, sel_ref = rest[:4]
        qkv_ref, lse_ref, o_ref, a_ref, rb_ref, gp_ref, wt_ref = rest[4:]
    else:
        qkv_ref, lse_ref, o_ref, a_ref = rest
    width = h_ref.shape[1]
    images = h_ref.shape[0] // pad
    hidden = h_ref[...]
    unit, _ = norm_parts(hidden)
    normed = (unit * g_ref[...] + b_ref[...]).astype(BF)
    for part in range(3):
        cols = slice(part * width, (part + 1) * width)
        qkv_ref[:, cols] = (mm(normed, w_ref[:, cols]) + qb_ref[:, cols]).astype(BF)
    pairs = heads // 2
    lane = lax.broadcasted_iota(jnp.int32, (pad, 2 * HD), 1)
    key_row = lax.broadcasted_iota(jnp.int32, (pad, pad), 0)

    def pair_step(step, carry):
        image = step // pairs
        pair = step % pairs
        rows = pl.ds(pl.multiple_of(image * pad, ROW_PAD), pad)

        def col(part):
            return pl.ds(pl.multiple_of(part * width + pair * 2 * HD, 2 * HD), 2 * HD)

        query = qkv_ref[rows, col(0)] * HD ** (-0.5)
        key = qkv_ref[rows, col(1)]
        value = qkv_ref[rows, col(2)]
        mixed = []
        for half in range(2):
            mine = (lane >= HD) if half else (lane < HD)
            scores = mm_bt(key, jnp.where(mine, query, 0).astype(BF))
            scores = jnp.where(key_row < length, scores, -1e30)
            top = jnp.max(scores, axis=0, keepdims=True)
            weights = jnp.exp(scores - top)
            total = jnp.sum(weights, axis=0, keepdims=True)
            probs = (weights * (1.0 / total)).astype(BF)
            mixed.append(mm_at(probs, value))
            lse_ref[image, pl.ds(pair * 2 + half, 1), :] = top + jnp.log(total)
        o_ref[rows, col(0)] = jnp.where(lane < HD, mixed[0], mixed[1]).astype(BF)
        return carry

    lax.fori_loop(0, images * pairs, pair_step, 0)
    after = hidden + mm_bt(o_ref[...], w_ref[:, 3 * width :]) + ob_ref[...]
    a_ref[...] = after
    if router_on:
        unit2, _ = norm_parts(after)
        normed2 = unit2 * g2_ref[...] + b2_ref[...]
        rb_ref[...] = normed2.astype(BF)
        logits = jnp.dot(normed2, rt_ref[...], precision=EXACT, preferred_element_type=F32)
        lanes = lax.broadcasted_iota(jnp.int32, logits.shape, 1)
        live = lanes < router_on
        logits = jnp.where(live, logits, -1e30)
        gates = jnp.exp(logits - jnp.max(logits, axis=-1, keepdims=True))
        gates = gates / jnp.sum(gates, axis=-1, keepdims=True)
        gates = jnp.where(live, gates, 0.0)
        gp_ref[...] = gates
        first = jnp.sum(jnp.where(lanes == sel_ref[:, 0:1], gates, 0.0), axis=-1, keepdims=True)
        second = jnp.sum(jnp.where(lanes == sel_ref[:, 1:2], gates, 0.0), axis=-1, keepdims=True)
        wt_ref[...] = jnp.where(lanes == 0, first, jnp.where(lanes == 1, second, 0.0))


def attention_forward(hidden, gain, shift, weights, qkv_bias, out_bias, length, pad, router=None):
    rows, width = hidden.shape
    heads = width // HD
    block = rows // 2
    lse_rows = round_up(heads, 8)
    images = block // pad
    in_specs = [
        rows_of(block, width), whole((1, width)), whole((1, width)), whole((width, 4 * width)),
        whole((1, 3 * width)), whole((1, width)),
    ]
    args = [hidden, gain, shift, weights, qkv_bias, out_bias]
    out_specs = [
        rows_of(block, 3 * width),
        pl.BlockSpec((images, lse_rows, pad), lambda step: (step, 0, 0)),
        rows_of(block, width),
        rows_of(block, width),
    ]
    out_shape = [
        jax.ShapeDtypeStruct((rows, 3 * width), BF),
        jax.ShapeDtypeStruct((2 * images, lse_rows, pad), F32),
        jax.ShapeDtypeStruct((rows, width), BF),
        jax.ShapeDtypeStruct((rows, width), F32),
    ]
    router_on = 0
    if router is not None:
        gain2, shift2, router_wide, select, router_on = router
        lanes = router_wide.shape[1]
        in_specs += [whole((1, width)), whole((1, width)), whole((width, lanes)), rows_of(block, 2)]
        args += [gain2, shift2, router_wide, select]
        out_specs += [rows_of(block, width), rows_of(block, lanes), rows_of(block, lanes)]
        out_shape += [
            jax.ShapeDtypeStruct((rows, width), BF),
            jax.ShapeDtypeStruct((rows, lanes), F32),
            jax.ShapeDtypeStruct((rows, lanes), F32),
        ]
    return call(
        functools.partial(attn_fwd_kernel, length, pad, heads, router_on),
        (2,), in_specs, out_specs, out_shape, [],
        8.0 * rows * width * width + 16.0 * rows * pad * width, 12.0e6, "attn_fwd",
    )(*args)


def attn_bwd_kernel(
    length, pad, heads,
    da_ref, h_ref, g_ref, b_ref, w_ref, qkv_ref, lse_ref, o_ref,
    dh_ref, dwq_ref, dwo_ref, dqb_ref, dob_ref, dg_ref, db_ref,
    grad_sc, dqkv_sc, wq_acc, wo_acc,
):
    step_id = pl.program_id(0)
    last = pl.num_programs(0) - 1
    width = h_ref.shape[1]
    images = h_ref.shape[0] // pad
    pairs = heads // 2
    incoming = da_ref[...]
    low = incoming.astype(BF)
    out_bias_grad = jnp.sum(low.astype(F32), axis=0, keepdims=True)
    out_grad_part = mm_at(low, o_ref[...])
    grad_sc[...] = mm(low, w_ref[:, 3 * width :]).astype(BF)
    lane = lax.broadcasted_iota(jnp.int32, (pad, 2 * HD), 1)
    key_row = lax.broadcasted_iota(jnp.int32, (pad, pad), 0)

    def pair_step(step, carry):
        image = step // pairs
        pair = step % pairs
        rows = pl.ds(pl.multiple_of(image * pad, ROW_PAD), pad)

        def col(part):
            return pl.ds(pl.multiple_of(part * width + pair * 2 * HD, 2 * HD), 2 * HD)

        query = (qkv_ref[rows, col(0)] * HD ** (-0.5)).astype(BF)
        key = qkv_ref[rows, col(1)]
        value = qkv_ref[rows, col(2)]
        mixed = grad_sc[rows, col(0)]
        parts = []
        for half in range(2):
            mine = (lane >= HD) if half else (lane < HD)
            scores = mm_bt(key, jnp.where(mine, query, 0).astype(BF))
            total = lse_ref[image, pl.ds(pair * 2 + half, 1), :]
            probs = jnp.where(key_row < length, jnp.exp(scores - total), 0.0)
            probs_grad = mm_bt(value, jnp.where(mine, mixed, 0).astype(BF))
            product = probs * probs_grad
            delta = jnp.sum(product, axis=0, keepdims=True)
            score_grad = (product - probs * delta).astype(BF)
            parts.append((
                mm_at(score_grad, key) * HD ** (-0.5),
                mm(score_grad, query),
                mm(probs.astype(BF), mixed),
            ))
        for part in range(3):
            dqkv_sc[rows, col(part)] = jnp.where(
                lane < HD, parts[0][part], parts[1][part]
            ).astype(BF)
        return carry

    lax.fori_loop(0, images * pairs, pair_step, 0)
    unit, scale = norm_parts(h_ref[...])
    normed = (unit * g_ref[...] + b_ref[...]).astype(BF)
    normed_grad = None
    bias_parts = []
    first = step_id == 0
    for part in range(3):
        cols = slice(part * width, (part + 1) * width)
        grads = dqkv_sc[:, cols]
        term = mm_bt(grads, w_ref[:, cols])
        normed_grad = term if normed_grad is None else normed_grad + term
        piece = mm_at(normed, grads)
        bias_parts.append(jnp.sum(grads.astype(F32), axis=0, keepdims=True))

        @pl.when(first)
        def _():
            wq_acc[:, cols] = piece

        @pl.when(step_id == last)
        def _():
            dwq_ref[:, cols] = (wq_acc[:, cols] + piece).astype(BF)

    hidden_grad, gain_grad, shift_grad = norm_pull(unit, scale, g_ref[...], normed_grad)
    dh_ref[...] = incoming + hidden_grad

    @pl.when(first)
    def _():
        wo_acc[...] = out_grad_part
        dob_ref[...] = out_bias_grad
        dg_ref[...] = gain_grad
        db_ref[...] = shift_grad
        for part in range(3):
            dqb_ref[:, part * width : (part + 1) * width] = bias_parts[part]

    @pl.when(step_id == last)
    def _():
        dwo_ref[...] = (wo_acc[...] + out_grad_part).astype(BF)
        dob_ref[...] += out_bias_grad
        dg_ref[...] += gain_grad
        db_ref[...] += shift_grad
        for part in range(3):
            dqb_ref[:, part * width : (part + 1) * width] += bias_parts[part]


def attention_back(incoming, hidden, gain, shift, weights, stored, length, pad):
    qkv, lse, mixed = stored
    rows, width = hidden.shape
    heads = width // HD
    block = rows // 2
    images = block // pad
    lse_rows = lse.shape[1]
    return call(
        functools.partial(attn_bwd_kernel, length, pad, heads),
        (2,),
        [
            rows_of(block, width), rows_of(block, width), whole((1, width)), whole((1, width)),
            whole((width, 4 * width)), rows_of(block, 3 * width),
            pl.BlockSpec((images, lse_rows, pad), lambda step: (step, 0, 0)),
            rows_of(block, width),
        ],
        [
            rows_of(block, width), whole((width, 3 * width)), whole((width, width)),
            whole((1, 3 * width)), whole((1, width)), whole((1, width)), whole((1, width)),
        ],
        [
            jax.ShapeDtypeStruct((rows, width), F32),
            jax.ShapeDtypeStruct((width, 3 * width), BF),
            jax.ShapeDtypeStruct((width, width), BF),
            jax.ShapeDtypeStruct((1, 3 * width), F32),
            jax.ShapeDtypeStruct((1, width), F32),
            jax.ShapeDtypeStruct((1, width), F32),
            jax.ShapeDtypeStruct((1, width), F32),
        ],
        [
            pltpu.VMEM((block, width), BF),
            pltpu.VMEM((block, 3 * width), BF),
            pltpu.VMEM((width, 3 * width), F32),
            pltpu.VMEM((width, width), F32),
        ],
        16.0 * rows * width * width + 40.0 * rows * pad * width, 25.0e6, "attn_bwd",
    )(incoming, hidden, gain, shift, weights, qkv, lse, mixed)


def dense_fwd_kernel(a_ref, g_ref, b_ref, win_ref, wout_ref, bin_ref, bout_ref, x_ref, m_sc, acc):
    step = pl.program_id(0)

    @pl.when(step == 0)
    def _():
        unit, _ = norm_parts(a_ref[...])
        m_sc[...] = (unit * g_ref[...] + b_ref[...]).astype(BF)
        acc[...] = a_ref[...] + bout_ref[...]

    preact = mm(m_sc[...], win_ref[...]) + bin_ref[...]
    active = gelu_value(preact).astype(BF)
    acc[...] += mm_bt(active, wout_ref[...])

    @pl.when(step == pl.num_programs(0) - 1)
    def _():
        x_ref[...] = acc[...]


def dense_forward(hidden, gain, shift, weights, in_bias, out_bias):
    rows, width = hidden.shape
    ff = in_bias.shape[1]
    steps = ff // FF_BLOCK
    return call(
        dense_fwd_kernel, (steps,),
        [
            whole((rows, width)), whole((1, width)), whole((1, width)),
            pl.BlockSpec((width, FF_BLOCK), lambda c: (0, c)),
            pl.BlockSpec((width, FF_BLOCK), lambda c: (0, steps + c)),
            pl.BlockSpec((1, FF_BLOCK), lambda c: (0, c)),
            whole((1, width)),
        ],
        whole((rows, width)),
        jax.ShapeDtypeStruct((rows, width), F32),
        [pltpu.VMEM((rows, width), BF), pltpu.VMEM((rows, width), F32)],
        4.0 * rows * width * ff, 15.0e6, "dense_fwd",
    )(hidden, gain, shift, weights, weights, in_bias, out_bias)


def dense_bwd_kernel(
    dx_ref, a_ref, g_ref, b_ref, win_ref, wout_ref, bin_ref,
    da_ref, dwin_ref, dwout_ref, dbin_ref, dbout_ref, dg_ref, db_ref,
    m_sc, low_sc, acc,
):
    step = pl.program_id(0)

    @pl.when(step == 0)
    def _():
        unit, _ = norm_parts(a_ref[...])
        m_sc[...] = (unit * g_ref[...] + b_ref[...]).astype(BF)
        low = dx_ref[...].astype(BF)
        low_sc[...] = low
        dbout_ref[...] = jnp.sum(low.astype(F32), axis=0, keepdims=True)
        acc[...] = jnp.zeros_like(acc)

    normed = m_sc[...]
    low = low_sc[...]
    preact = mm(normed, win_ref[...]) + bin_ref[...]
    active, slope = gelu_pair(preact)
    preact_grad = (slope * mm(low, wout_ref[...])).astype(BF)
    dbin_ref[...] = jnp.sum(preact_grad.astype(F32), axis=0, keepdims=True)
    dwout_ref[...] = mm_at(low, active.astype(BF)).astype(BF)
    dwin_ref[...] = mm_at(normed, preact_grad).astype(BF)
    acc[...] += mm_bt(preact_grad, win_ref[...])

    @pl.when(step == pl.num_programs(0) - 1)
    def _():
        unit, scale = norm_parts(a_ref[...])
        hidden_grad, gain_grad, shift_grad = norm_pull(unit, scale, g_ref[...], acc[...])
        da_ref[...] = dx_ref[...] + hidden_grad
        dg_ref[...] = gain_grad
        db_ref[...] = shift_grad


def dense_back(incoming, hidden, gain, shift, weights, in_bias):
    rows, width = hidden.shape
    ff = in_bias.shape[1]
    steps = ff // FF_BLOCK
    col_block = pl.BlockSpec((width, FF_BLOCK), lambda c: (0, c))
    return call(
        dense_bwd_kernel, (steps,),
        [
            whole((rows, width)), whole((rows, width)), whole((1, width)), whole((1, width)),
            col_block,
            pl.BlockSpec((width, FF_BLOCK), lambda c: (0, steps + c)),
            pl.BlockSpec((1, FF_BLOCK), lambda c: (0, c)),
        ],
        [
            whole((rows, width)), col_block, col_block,
            pl.BlockSpec((1, FF_BLOCK), lambda c: (0, c)),
            whole((1, width)), whole((1, width)), whole((1, width)),
        ],
        [
            jax.ShapeDtypeStruct((rows, width), F32),
            jax.ShapeDtypeStruct((width, ff), BF),
            jax.ShapeDtypeStruct((width, ff), BF),
            jax.ShapeDtypeStruct((1, ff), F32),
            jax.ShapeDtypeStruct((1, width), F32),
            jax.ShapeDtypeStruct((1, width), F32),
            jax.ShapeDtypeStruct((1, width), F32),
        ],
        [
            pltpu.VMEM((rows, width), BF), pltpu.VMEM((rows, width), BF),
            pltpu.VMEM((rows, width), F32),
        ],
        10.0 * rows * width * ff, 35.0e6, "dense_bwd",
    )(incoming, hidden, gain, shift, weights, weights, in_bias)


def moe_kernel(
    micro, capp,
    rb_own, rb_oth, og_own, og_oth, dr_ref, dc_own, dc_oth, w_ref,
    win_ref, wout_ref, bin_ref, bout_ref,
    yc_own, yc_oth, rc_own, rc_oth, dg_own, dg_oth,
    dwin_ref, dwout_ref, dbin_ref, dbout_ref,
    b_sc, og_sc, dy_sc, w_sc, y_acc, r_acc, yo_acc, yt_acc, ro_acc, rt_acc,
):
    expert = pl.program_id(0)
    chunk = pl.program_id(1)
    last_expert = expert == pl.num_programs(0) - 1
    last_chunk = chunk == pl.num_programs(1) - 1
    half = rb_own.shape[1]

    @pl.when(chunk == 0)
    def _():
        for m in range(micro):
            slots = slice(m * capp, (m + 1) * capp)
            ids = lax.broadcasted_iota(jnp.int32, (capp, half), 0) + expert * capp
            tokens = None
            for side, (rb, og) in enumerate(((rb_own, og_own), (rb_oth, og_oth))):
                hit0 = dr_ref[m, 2 * side : 2 * side + 1, :] == ids
                hit1 = dr_ref[m, 2 * side + 1 : 2 * side + 2, :] == ids
                pick = jnp.where(hit0 | hit1, 1.0, 0.0).astype(BF)
                gate = jnp.sum(
                    jnp.where(hit0, w_ref[m, 2 * side : 2 * side + 1, :], 0.0)
                    + jnp.where(hit1, w_ref[m, 2 * side + 1 : 2 * side + 2, :], 0.0),
                    axis=-1, keepdims=True,
                )
                found = (mm(pick, rb[m]), mm(pick, og[m]), gate)
                tokens = found if tokens is None else tuple(
                    one + two for one, two in zip(tokens, found)
                )
            b_sc[slots, :] = tokens[0].astype(BF)
            og_sc[slots, :] = tokens[1].astype(BF)
            dy_sc[slots, :] = (tokens[1] * tokens[2]).astype(BF)
            w_sc[slots, :] = jnp.broadcast_to(tokens[2], (capp, w_sc.shape[1]))
        y_acc[...] = jnp.zeros_like(y_acc)
        r_acc[...] = jnp.zeros_like(r_acc)

    tokens = b_sc[...]
    low = dy_sc[...]
    preact = mm(tokens, win_ref[...]) + bin_ref[0]
    active, slope = gelu_pair(preact)
    active = active.astype(BF)
    preact_grad = (slope * mm(low, wout_ref[...])).astype(BF)
    dbin_ref[0] = jnp.sum(preact_grad.astype(F32), axis=0, keepdims=True)
    y_acc[...] += mm_bt(active, wout_ref[...])
    r_acc[...] += mm_bt(preact_grad, win_ref[...])
    dwout_ref[...] = mm_at(low, active).astype(BF)
    dwin_ref[...] = mm_at(tokens, preact_grad).astype(BF)

    @pl.when(last_chunk)
    def _():
        dbout_ref[0] = jnp.sum(dy_sc[...].astype(F32), axis=0, keepdims=True)
        for m in range(micro):
            slots = slice(m * capp, (m + 1) * capp)
            result = y_acc[slots, :] + 0.5 * bout_ref[0]
            dots = jnp.sum(og_sc[slots, :].astype(F32) * result, axis=-1, keepdims=True)
            lanes = lax.broadcasted_iota(jnp.int32, (capp, dg_own.shape[2]), 1)
            dots = jnp.where(lanes == expert, dots, 0.0)
            weighted = (w_sc[slots, 0:1] * result).astype(BF)
            rows_grad = r_acc[slots, :].astype(BF)
            ids = lax.broadcasted_iota(jnp.int32, (half, capp), 1) + expert * capp
            for dc, yc, rc, dg in (
                (dc_own, yo_acc, ro_acc, dg_own), (dc_oth, yt_acc, rt_acc, dg_oth)
            ):
                hit = (dc[m, :, 0:1] == ids) | (dc[m, :, 1:2] == ids)
                pick = jnp.where(hit, 1.0, 0.0)
                low_pick = pick.astype(BF)
                y_new = mm(low_pick, weighted)
                r_new = mm(low_pick, rows_grad)
                d_new = jnp.dot(pick, dots, precision=EXACT, preferred_element_type=F32)

                @pl.when(expert == 0)
                def _():
                    yc[m] = y_new
                    rc[m] = r_new
                    dg[m] = d_new

                @pl.when(expert > 0)
                def _():
                    yc[m] += y_new
                    rc[m] += r_new
                    dg[m] += d_new

    @pl.when(last_chunk & last_expert)
    def _():
        yc_own[...] = yo_acc[...].astype(BF)
        yc_oth[...] = yt_acc[...].astype(BF)
        rc_own[...] = ro_acc[...].astype(BF)
        rc_oth[...] = rt_acc[...].astype(BF)


def mixture(rows_own, rows_oth, grad_own, grad_oth, place_rows, place_own, place_oth, gates,
            weights, in_bias, out_bias, capp):
    micro, half, width = rows_own.shape
    experts, _, ff = in_bias.shape
    steps = ff // FF_BLOCK
    blocks = experts * steps
    lanes = 128
    slots = micro * capp
    w_block = (width, FF_BLOCK)
    group = (micro, half, width)
    return call(
        functools.partial(moe_kernel, micro, capp),
        (experts, steps),
        [
            whole(group), whole(group), whole(group), whole(group),
            whole(place_rows.shape), whole(place_own.shape), whole(place_oth.shape),
            whole(gates.shape),
            pl.BlockSpec(w_block, lambda e, c: (0, e * steps + c)),
            pl.BlockSpec(w_block, lambda e, c: (0, blocks + e * steps + c)),
            pl.BlockSpec((1, 1, FF_BLOCK), lambda e, c: (e, 0, c)),
            pl.BlockSpec((1, 1, width), lambda e, c: (e, 0, 0)),
        ],
        [
            whole(group), whole(group), whole(group), whole(group),
            whole((micro, half, lanes)), whole((micro, half, lanes)),
            pl.BlockSpec(w_block, lambda e, c: (0, e * steps + c)),
            pl.BlockSpec(w_block, lambda e, c: (0, e * steps + c)),
            pl.BlockSpec((1, 1, FF_BLOCK), lambda e, c: (e, 0, c)),
            pl.BlockSpec((1, 1, width), lambda e, c: (e, 0, 0)),
        ],
        [
            jax.ShapeDtypeStruct(group, BF), jax.ShapeDtypeStruct(group, BF),
            jax.ShapeDtypeStruct(group, BF), jax.ShapeDtypeStruct(group, BF),
            jax.ShapeDtypeStruct((micro, half, lanes), F32),
            jax.ShapeDtypeStruct((micro, half, lanes), F32),
            jax.ShapeDtypeStruct((width, experts * ff), BF),
            jax.ShapeDtypeStruct((width, experts * ff), BF),
            jax.ShapeDtypeStruct((experts, 1, ff), F32),
            jax.ShapeDtypeStruct((experts, 1, width), F32),
        ],
        [
            pltpu.VMEM((slots, width), BF), pltpu.VMEM((slots, width), BF),
            pltpu.VMEM((slots, width), BF), pltpu.VMEM((slots, 128), F32),
            pltpu.VMEM((slots, width), F32), pltpu.VMEM((slots, width), F32),
            pltpu.VMEM(group, F32), pltpu.VMEM(group, F32),
            pltpu.VMEM(group, F32), pltpu.VMEM(group, F32),
        ],
        12.0 * slots * experts * width * ff + 16.0 * experts * micro * capp * half * width,
        60.0e6, "experts",
    )(rows_own, rows_oth, grad_own, grad_oth, place_rows, place_own, place_oth, gates,
      weights, weights, in_bias, out_bias)


def gate_bwd_kernel(
    a_ref, og_ref, yo_ref, yr_ref, ro_ref, rr_ref, do_ref, dr_ref, gp_ref, rt_ref, g_ref, b_ref,
    out_ref, da_ref, drt_ref, dg_ref, db_ref,
):
    step = pl.program_id(0)
    after = a_ref[...]
    incoming = og_ref[...].astype(F32)
    out_ref[...] = (after + (yo_ref[...].astype(F32) + yr_ref[...].astype(F32))).astype(BF)
    gates = gp_ref[...]
    gate_grad = do_ref[...] + dr_ref[...]
    logit_grad = gates * (gate_grad - jnp.sum(gates * gate_grad, axis=-1, keepdims=True))
    unit, scale = norm_parts(after)
    normed = unit * g_ref[...] + b_ref[...]
    router_grad = lax.dot_general(
        logit_grad, normed, (((0,), (0,)), ((), ())), precision=EXACT, preferred_element_type=F32
    )
    normed_grad = ro_ref[...].astype(F32) + rr_ref[...].astype(F32)
    normed_grad += lax.dot_general(
        logit_grad, rt_ref[...], (((1,), (1,)), ((), ())), precision=EXACT,
        preferred_element_type=F32,
    )
    hidden_grad, gain_grad, shift_grad = norm_pull(unit, scale, g_ref[...], normed_grad)
    da_ref[...] = incoming + hidden_grad

    @pl.when(step == 0)
    def _():
        drt_ref[...] = router_grad
        dg_ref[...] = gain_grad
        db_ref[...] = shift_grad

    @pl.when(step > 0)
    def _():
        drt_ref[...] += router_grad
        dg_ref[...] += gain_grad
        db_ref[...] += shift_grad


def gate_back(after, incoming, y_own, y_got, r_own, r_got, d_own, d_got, gates, router, gain, shift):
    rows, width = after.shape
    lanes = gates.shape[1]
    block = rows // 2
    row = rows_of(block, width)
    row_low = rows_of(block, lanes)
    return call(
        gate_bwd_kernel, (2,),
        [
            row, row, row, row, row, row, row_low, row_low, row_low,
            whole((width, lanes)), whole((1, width)), whole((1, width)),
        ],
        [row, row, whole((lanes, width)), whole((1, width)), whole((1, width))],
        [
            jax.ShapeDtypeStruct((rows, width), BF),
            jax.ShapeDtypeStruct((rows, width), F32),
            jax.ShapeDtypeStruct((lanes, width), F32),
            jax.ShapeDtypeStruct((1, width), F32),
            jax.ShapeDtypeStruct((1, width), F32),
        ],
        [], 4.0 * rows * width * lanes, 14.0e6, "gate_bwd",
    )(after, incoming, y_own, y_got, r_own, r_got, d_own, d_got, gates, router, gain, shift)


def swap(value):
    return lax.ppermute(value, "tensor", [(0, 1), (1, 0)])


def in_order(mine, other, axis):
    first = lax.axis_index("tensor") == 0
    return jnp.stack([jnp.where(first, mine, other), jnp.where(first, other, mine)], axis=axis)


def gather_rows(share):
    return lax.all_gather(share, "dp", axis=0, tiled=True)


def scatter_rows(grad):
    return lax.psum_scatter(grad, "dp", scatter_dimension=0, tiled=True).astype(F32)


def join_halves(grad, parts):
    rows, total = grad.shape
    width = total // parts // 2
    halves = grad.reshape(rows, parts, 2, width)
    mine = lax.axis_index("tensor")
    kept = lax.dynamic_index_in_dim(halves, mine, 2, keepdims=False)
    sent = lax.dynamic_index_in_dim(halves, 1 - mine, 2, keepdims=False)
    return kept + swap(sent)


def own_half(value, axis):
    size = value.shape[axis] // 2
    return lax.dynamic_slice_in_dim(value, lax.axis_index("tensor") * size, size, axis)


def local(
    block_input, norm_gain, row_bias, qkv_weight, qkv_bias, out_weight, mlp_in, mlp_in_bias,
    mlp_out, mlp_out_bias, router, expert_in, expert_in_bias, expert_out, expert_out_bias,
    routes, slot_index, out_grad,
):
    micro, images, length, width = block_input.shape
    experts = router.shape[1]
    share_rows = mlp_in.shape[0]
    own_images = images // 2
    pad = round_up(length, ROW_PAD)
    half = own_images * pad
    rows = micro * half
    capp = round_up(CAP, ROW_PAD)
    side = lax.axis_index("tensor")

    def attn_share(layer):
        return jnp.concatenate(
            [qkv_weight[layer].reshape(share_rows, -1), out_weight[layer]], axis=1
        )

    def attn_full(layer):
        mine = attn_share(layer)
        other = swap(mine)
        full = in_order(mine.reshape(share_rows, 4, -1), other.reshape(share_rows, 4, -1), 2)
        return gather_rows(full.reshape(share_rows, -1))

    attn_one = attn_full(0)
    dense_mine = jnp.stack([mlp_in, mlp_out], axis=1)
    dense_full = in_order(dense_mine, swap(dense_mine), 2)
    dense_w = gather_rows(dense_full.reshape(share_rows, -1))
    attn_two = attn_full(1)
    expert_w = gather_rows(
        jnp.concatenate(
            [expert_in.reshape(share_rows, -1), expert_out.reshape(share_rows, -1)], axis=1
        )
    )

    def both(vector):
        joined = in_order(vector, swap(vector), vector.ndim - 1)
        return joined.reshape(vector.shape[:-1] + (-1,))

    biases = jnp.concatenate([qkv_bias.reshape(-1), mlp_in_bias])
    biases_other = swap(biases)
    bias_pair = in_order(biases, biases_other, 0)
    split = qkv_bias.size
    qkv_bias_full = jnp.moveaxis(
        bias_pair[:, :split].reshape((2,) + qkv_bias.shape), 0, 2
    ).reshape(qkv_bias.shape[:2] + (width,))
    mlp_bias_full = bias_pair[:, split:].reshape(1, -1)

    def qkv_bias_row(layer):
        zero = jnp.zeros((width,), F32)
        return jnp.concatenate(
            [qkv_bias_full[layer, 0], zero, qkv_bias_full[layer, 1]]
        ).reshape(1, -1)

    def padded(value, start):
        part = lax.dynamic_slice_in_dim(value, start, own_images, 1)
        return jnp.pad(part, ((0, 0), (0, 0), (0, pad - length), (0, 0)))

    mine_at = side * own_images
    other_at = (1 - side) * own_images
    hidden = padded(block_input, mine_at).astype(F32).reshape(rows, width)
    grad_own = padded(out_grad, mine_at).reshape(micro, half, width)
    grad_oth = padded(out_grad, other_at).reshape(micro, half, width)

    kept = slot_index < CAP
    place = jnp.where(kept, routes * capp + slot_index, -1)
    pick = jnp.where(kept, routes, -1)

    def lay(value, start):
        part = lax.dynamic_slice_in_dim(value, start, own_images, 1)
        part = jnp.pad(
            part, ((0, 0), (0, 0), (0, pad - length), (0, 0)), constant_values=-1
        )
        return part.reshape(micro, half, 2)

    place_own, place_oth = lay(place, mine_at), lay(place, other_at)
    place_rows = jnp.concatenate(
        [jnp.swapaxes(place_own, 1, 2), jnp.swapaxes(place_oth, 1, 2)], axis=1
    )
    select = lay(pick, mine_at).reshape(rows, 2)
    router_wide = jnp.pad(router, ((0, 0), (0, 128 - experts)))

    def row(vector):
        return vector.reshape(1, -1)

    qkv_one, lse_one, mix_one, after_one = attention_forward(
        hidden, row(norm_gain[0, 0]), row(row_bias[0, 0]), attn_one, qkv_bias_row(0),
        row(row_bias[0, 2]), length, pad,
    )
    after_ffn = dense_forward(
        after_one, row(norm_gain[0, 1]), row(row_bias[0, 1]), dense_w, mlp_bias_full,
        row(mlp_out_bias),
    )
    qkv_two, lse_two, mix_two, after_two, rows_own, gates, chosen = attention_forward(
        after_ffn, row(norm_gain[1, 0]), row(row_bias[1, 0]), attn_two, qkv_bias_row(1),
        row(row_bias[1, 2]), length, pad,
        (row(norm_gain[1, 1]), row(row_bias[1, 1]), router_wide, select, experts),
    )
    rows_oth = swap(rows_own)
    gate_own = jnp.swapaxes(chosen[:, :2].reshape(micro, half, 2), 1, 2)
    gate_oth = swap(gate_own)
    (
        y_own, y_oth, r_own, r_oth, d_own, d_oth, ein_grad, eout_grad, ein_bias, eout_bias,
    ) = mixture(
        rows_own.reshape(micro, half, width), rows_oth.reshape(micro, half, width),
        grad_own, grad_oth, place_rows, place_own, place_oth,
        jnp.concatenate([gate_own, gate_oth], axis=1),
        expert_w, expert_in_bias.reshape(experts, 1, -1), expert_out_bias.reshape(experts, 1, -1),
        capp,
    )
    y_got, r_got, d_got = swap(y_oth), swap(r_oth), swap(d_oth)

    def flat(value):
        return value.reshape(rows, value.shape[-1])

    out_own, grad_two, router_grad, gain_moe, shift_moe = gate_back(
        after_two, flat(grad_own), flat(y_own), flat(y_got), flat(r_own), flat(r_got),
        flat(d_own), flat(d_got), gates, router_wide,
        row(norm_gain[1, 1]), row(row_bias[1, 1]),
    )
    grad_ffn, wq_two, wo_two, qb_two, ob_two, gain_two, shift_two = attention_back(
        grad_two, after_ffn, row(norm_gain[1, 0]), row(row_bias[1, 0]), attn_two,
        (qkv_two, lse_two, mix_two), length, pad,
    )
    grad_one, win_grad, wout_grad, in_bias_grad, out_bias_grad, gain_ffn, shift_ffn = dense_back(
        grad_ffn, after_one, row(norm_gain[0, 1]), row(row_bias[0, 1]), dense_w, mlp_bias_full
    )
    grad_zero, wq_one, wo_one, qb_one, ob_one, gain_one, shift_one = attention_back(
        grad_one, hidden, row(norm_gain[0, 0]), row(row_bias[0, 0]), attn_one,
        (qkv_one, lse_one, mix_one), length, pad,
    )

    def images_of(value):
        value = value.astype(BF).reshape(micro, own_images, pad, width)[:, :, :length]
        return in_order(value, swap(value), 1).reshape(block_input.shape)

    block_output = images_of(out_own)
    input_grad = images_of(grad_zero).astype(F32)

    ein_done = scatter_rows(ein_grad).reshape(expert_in.shape)
    eout_done = scatter_rows(eout_grad).reshape(expert_out.shape)
    wq_two_done = join_halves(scatter_rows(wq_two), 3)
    wo_two_done = join_halves(scatter_rows(wo_two), 1)
    win_done = join_halves(scatter_rows(win_grad), 1).reshape(mlp_in.shape)
    wout_done = join_halves(scatter_rows(wout_grad), 1).reshape(mlp_out.shape)
    wq_one_done = join_halves(scatter_rows(wq_one), 3)
    wo_one_done = join_halves(scatter_rows(wo_one), 1)

    place_in = (side == jnp.arange(2)).astype(F32)
    ein_bias_wide = place_in[:, None, None] * ein_bias.reshape(1, experts, -1)
    small = lax.psum(
        (
            jnp.concatenate([gain_one, gain_ffn, gain_two, gain_moe]),
            jnp.concatenate([shift_one, shift_ffn, ob_one, shift_two, shift_moe, ob_two]),
            jnp.concatenate([qb_one, qb_two]),
            in_bias_grad,
            out_bias_grad,
            router_grad[:experts],
            ein_bias_wide,
            0.5 * eout_bias,
        ),
        ("dp", "tensor"),
    )
    gain_sum, shift_sum, qb_sum, in_bias_sum, out_bias_sum, router_sum, ein_sum, eout_sum = small
    qb_sum = own_half(qb_sum.reshape(2, 3, width), 2)
    return (
        block_output,
        input_grad,
        gain_sum.reshape(norm_gain.shape),
        shift_sum.reshape(row_bias.shape),
        jnp.stack([wq_one_done, wq_two_done]).reshape(qkv_weight.shape),
        jnp.stack([qb_sum[:, 0], qb_sum[:, 2]], axis=1),
        jnp.stack([wo_one_done, wo_two_done]).reshape(out_weight.shape),
        win_done,
        own_half(in_bias_sum.reshape(-1), 0),
        wout_done,
        out_bias_sum.reshape(-1),
        router_sum.T,
        ein_done,
        lax.dynamic_index_in_dim(ein_sum, side, 0, keepdims=False),
        eout_done,
        eout_sum.reshape(experts, width),
    )


def solution(mesh):
    return jax.shard_map(
        local,
        mesh=mesh,
        in_specs=(
            P(None, "dp", None, None), P(), P(), P(None, "dp", None, "tensor"),
            P(None, None, "tensor"), P(None, "dp", "tensor"), P("dp", "tensor"), P("tensor"),
            P("dp", "tensor"), P(), P(), P("dp", None, "tensor"), P(None, "tensor"),
            P("dp", None, "tensor"), P(), P(None, "dp", None, None), P(None, "dp", None, None),
            P(None, "dp", None, None),
        ),
        out_specs=(
            P(None, "dp", None, None), P(None, "dp", None, None), P(), P(),
            P(None, "dp", None, "tensor"), P(None, None, "tensor"), P(None, "dp", "tensor"),
            P("dp", "tensor"), P("tensor"), P("dp", "tensor"), P(), P(),
            P("dp", None, "tensor"), P(None, "tensor"), P("dp", None, "tensor"), P(),
        ),
        check_vma=False,
    )
```

```python
import functools

import jax
import jax.numpy as jnp
from jax import lax
from jax.experimental import pallas as pl
from jax.experimental.pallas import tpu as pltpu
from jax.sharding import PartitionSpec as P

HD = 64
CAP = 295
NORM_EPS = 1e-06
EXACT = lax.Precision.HIGHEST
BF = jnp.bfloat16
F32 = jnp.float32
VMEM_LIMIT = 58 * 1024 * 1024
FF_BLOCK = 512
ROW_PAD = 16
GELU_SLOPE = 0.7978845608028654
GELU_CUBE = 0.044715


def round_up(value, unit):
    return -(-value // unit) * unit


def mm(left, right):
    return jnp.dot(left, right, preferred_element_type=F32)


def mm_bt(left, right):
    return lax.dot_general(left, right, (((1,), (1,)), ((), ())), preferred_element_type=F32)


def mm_at(left, right):
    return lax.dot_general(left, right, (((0,), (0,)), ((), ())), preferred_element_type=F32)


def norm_parts(hidden):
    center = jnp.mean(hidden, axis=-1, keepdims=True)
    centred = hidden - center
    spread = jnp.mean(centred * centred, axis=-1, keepdims=True)
    scale = lax.rsqrt(spread + NORM_EPS)
    return centred * scale, scale


def norm_pull(unit, scale, gain, incoming):
    wide = incoming * gain
    mean_wide = jnp.mean(wide, axis=-1, keepdims=True)
    mean_dot = jnp.mean(wide * unit, axis=-1, keepdims=True)
    hidden_grad = scale * (wide - mean_wide - unit * mean_dot)
    gain_grad = jnp.sum(incoming * unit, axis=0, keepdims=True)
    shift_grad = jnp.sum(incoming, axis=0, keepdims=True)
    return hidden_grad, gain_grad, shift_grad


def gelu_pair(preact):
    square = preact * preact
    inner = GELU_SLOPE * preact * (1.0 + GELU_CUBE * square)
    bend = jnp.tanh(inner)
    half = 0.5 * (1.0 + bend)
    active = preact * half
    slope = half + 0.5 * preact * (1.0 - bend * bend) * (
        GELU_SLOPE * (1.0 + 3.0 * GELU_CUBE * square)
    )
    return active, slope


def gelu_value(preact):
    square = preact * preact
    inner = GELU_SLOPE * preact * (1.0 + GELU_CUBE * square)
    return 0.5 * preact * (1.0 + jnp.tanh(inner))


def call(kernel, grid, in_specs, out_specs, out_shape, scratch, flops, traffic, name,
         after=(), prefetch=0):
    taken = prefetch + len(in_specs)
    skipped = len(after)

    def body(*refs):
        kernel(*refs[:taken], *refs[taken + skipped :])

    made = pl.pallas_call(
        body,
        grid_spec=pltpu.PrefetchScalarGridSpec(
            num_scalar_prefetch=prefetch,
            grid=grid,
            in_specs=list(in_specs) + [pl.BlockSpec(memory_space=pl.ANY)] * skipped,
            out_specs=out_specs,
            scratch_shapes=scratch,
        ),
        out_shape=out_shape,
        name=name,
        compiler_params=pltpu.CompilerParams(
            vmem_limit_bytes=VMEM_LIMIT,
            dimension_semantics=("arbitrary",) * len(grid),
        ),
        cost_estimate=pl.CostEstimate(
            flops=int(flops), bytes_accessed=int(traffic), transcendentals=0
        ),
    )
    return lambda *args: made(*args, *after)


def grad_shape(devices, width, columns):
    rows = width // devices
    if rows % ROW_PAD:
        return (2, width, columns)
    return (devices, 2, rows, columns)


def grad_block(shape, columns, index):
    block = shape[:-1] + (columns,)
    zeros = (0,) * (len(shape) - 1)
    return pl.BlockSpec(block, lambda *at: zeros + (index(*at),))


def put_grad(ref, part, cols, value):
    if len(ref.shape) == 3:
        ref[part, :, cols] = value
    else:
        ref[:, part, :, cols] = value.reshape(ref.shape[0], ref.shape[2], value.shape[1])


def whole(shape):
    zeros = (0,) * len(shape)
    return pl.BlockSpec(shape, lambda *_: zeros, pipeline_mode=pl.Buffered(1))


def rows_of(block, width):
    return pl.BlockSpec((block, width), lambda step: (step, 0))


def attn_fwd_kernel(
    length, pad, heads, router_on,
    h_ref, g_ref, b_ref, w_ref, qb_ref, ob_ref, *rest,
):
    if router_on:
        g2_ref, b2_ref, rt_ref, sel_ref = rest[:4]
        qkv_ref, lse_ref, o_ref, a_ref, rb_ref, gp_ref, wt_ref = rest[4:]
    else:
        qkv_ref, lse_ref, o_ref, a_ref = rest
    width = h_ref.shape[1]
    images = h_ref.shape[0] // pad
    hidden = h_ref[...]
    unit, _ = norm_parts(hidden)
    normed = (unit * g_ref[...] + b_ref[...]).astype(BF)
    for part in range(3):
        cols = slice(part * width, (part + 1) * width)
        qkv_ref[:, cols] = (mm(normed, w_ref[:, cols]) + qb_ref[:, cols]).astype(BF)
    pairs = heads // 2
    lane = lax.broadcasted_iota(jnp.int32, (pad, 2 * HD), 1)
    key_row = lax.broadcasted_iota(jnp.int32, (pad, pad), 0)

    def pair_step(step, carry):
        image = step // pairs
        pair = step % pairs
        rows = pl.ds(pl.multiple_of(image * pad, ROW_PAD), pad)

        def col(part):
            return pl.ds(pl.multiple_of(part * width + pair * 2 * HD, 2 * HD), 2 * HD)

        query = qkv_ref[rows, col(0)] * HD ** (-0.5)
        key = qkv_ref[rows, col(1)]
        value = qkv_ref[rows, col(2)]
        mixed = []
        for half in range(2):
            mine = (lane >= HD) if half else (lane < HD)
            scores = mm_bt(key, jnp.where(mine, query, 0).astype(BF))
            scores = jnp.where(key_row < length, scores, -1e30)
            top = jnp.max(scores, axis=0, keepdims=True)
            weights = jnp.exp(scores - top)
            total = jnp.sum(weights, axis=0, keepdims=True)
            probs = (weights * (1.0 / total)).astype(BF)
            mixed.append(mm_at(probs, value))
            lse_ref[image, pl.ds(pair * 2 + half, 1), :] = top + jnp.log(total)
        o_ref[rows, col(0)] = jnp.where(lane < HD, mixed[0], mixed[1]).astype(BF)
        return carry

    lax.fori_loop(0, images * pairs, pair_step, 0)
    after = hidden + mm_bt(o_ref[...], w_ref[:, 3 * width :]) + ob_ref[...]
    a_ref[...] = after
    if router_on:
        unit2, _ = norm_parts(after)
        normed2 = unit2 * g2_ref[...] + b2_ref[...]
        rb_ref[...] = normed2.astype(BF)
        logits = jnp.dot(normed2, rt_ref[...], precision=EXACT, preferred_element_type=F32)
        lanes = lax.broadcasted_iota(jnp.int32, logits.shape, 1)
        live = lanes < router_on
        logits = jnp.where(live, logits, -1e30)
        gates = jnp.exp(logits - jnp.max(logits, axis=-1, keepdims=True))
        gates = gates / jnp.sum(gates, axis=-1, keepdims=True)
        gates = jnp.where(live, gates, 0.0)
        gp_ref[...] = gates
        first = jnp.sum(jnp.where(lanes == sel_ref[:, 0:1], gates, 0.0), axis=-1, keepdims=True)
        second = jnp.sum(jnp.where(lanes == sel_ref[:, 1:2], gates, 0.0), axis=-1, keepdims=True)
        wt_ref[...] = jnp.where(lanes == 0, first, jnp.where(lanes == 1, second, 0.0))


def layer_block(width, layer):
    return pl.BlockSpec(
        (width, 4 * width), lambda *_: (0, layer), pipeline_mode=pl.Buffered(1)
    )


def attention_forward(
    hidden, gain, shift, weights, layer, qkv_bias, out_bias, length, pad, router=None
):
    rows, width = hidden.shape
    heads = width // HD
    block = rows // 2
    lse_rows = round_up(heads, 8)
    images = block // pad
    in_specs = [
        rows_of(block, width), whole((1, width)), whole((1, width)), layer_block(width, layer),
        whole((1, 3 * width)), whole((1, width)),
    ]
    args = [hidden, gain, shift, weights, qkv_bias, out_bias]
    out_specs = [
        rows_of(block, 3 * width),
        pl.BlockSpec((images, lse_rows, pad), lambda step: (step, 0, 0)),
        rows_of(block, width),
        rows_of(block, width),
    ]
    out_shape = [
        jax.ShapeDtypeStruct((rows, 3 * width), BF),
        jax.ShapeDtypeStruct((2 * images, lse_rows, pad), F32),
        jax.ShapeDtypeStruct((rows, width), BF),
        jax.ShapeDtypeStruct((rows, width), F32),
    ]
    router_on = 0
    if router is not None:
        gain2, shift2, router_wide, select, router_on = router
        lanes = router_wide.shape[1]
        in_specs += [whole((1, width)), whole((1, width)), whole((width, lanes)), rows_of(block, 2)]
        args += [gain2, shift2, router_wide, select]
        out_specs += [rows_of(block, width), rows_of(block, lanes), rows_of(block, lanes)]
        out_shape += [
            jax.ShapeDtypeStruct((rows, width), BF),
            jax.ShapeDtypeStruct((rows, lanes), F32),
            jax.ShapeDtypeStruct((rows, lanes), F32),
        ]
    return call(
        functools.partial(attn_fwd_kernel, length, pad, heads, router_on),
        (2,), in_specs, out_specs, out_shape, [],
        8.0 * rows * width * width + 16.0 * rows * pad * width, 12.0e6, "attn_fwd",
    )(*args)


def attn_core_kernel(
    length, pad, heads, da_ref, wo_ref, qkv_ref, lse_ref, dqkv_ref, low_ref, grad_sc,
):
    width = da_ref.shape[1]
    images = da_ref.shape[0] // pad
    pairs = heads // 2
    low = da_ref[...].astype(BF)
    low_ref[...] = low
    grad_sc[...] = mm(low, wo_ref[...]).astype(BF)
    lane = lax.broadcasted_iota(jnp.int32, (pad, 2 * HD), 1)
    key_row = lax.broadcasted_iota(jnp.int32, (pad, pad), 0)

    def pair_step(step, carry):
        image = step // pairs
        pair = step % pairs
        rows = pl.ds(pl.multiple_of(image * pad, ROW_PAD), pad)

        def col(part):
            return pl.ds(pl.multiple_of(part * width + pair * 2 * HD, 2 * HD), 2 * HD)

        query = (qkv_ref[rows, col(0)] * HD ** (-0.5)).astype(BF)
        key = qkv_ref[rows, col(1)]
        value = qkv_ref[rows, col(2)]
        mixed = grad_sc[rows, col(0)]
        parts = []
        for half in range(2):
            mine = (lane >= HD) if half else (lane < HD)
            scores = mm_bt(key, jnp.where(mine, query, 0).astype(BF))
            total = lse_ref[image, pl.ds(pair * 2 + half, 1), :]
            probs = jnp.where(key_row < length, jnp.exp(scores - total), 0.0)
            probs_grad = mm_bt(value, jnp.where(mine, mixed, 0).astype(BF))
            product = probs * probs_grad
            delta = jnp.sum(product, axis=0, keepdims=True)
            score_grad = (product - probs * delta).astype(BF)
            parts.append((
                mm_at(score_grad, key) * HD ** (-0.5),
                mm(score_grad, query),
                mm(probs.astype(BF), mixed),
            ))
        for part in range(3):
            dqkv_ref[rows, col(part)] = jnp.where(
                lane < HD, parts[0][part], parts[1][part]
            ).astype(BF)
        return carry

    lax.fori_loop(0, images * pairs, pair_step, 0)


def attention_core_back(incoming, weights, layer, stored, length, pad, which, after=()):
    qkv, lse, _ = stored
    rows, width = incoming.shape
    heads = width // HD
    block = rows // 2
    images = block // pad
    lse_rows = lse.shape[1]
    return call(
        functools.partial(attn_core_kernel, length, pad, heads),
        (1,),
        [
            pl.BlockSpec((block, width), lambda step: (which, 0)),
            pl.BlockSpec((width, width), lambda step: (0, 4 * layer + 3)),
            pl.BlockSpec((block, 3 * width), lambda step: (which, 0)),
            pl.BlockSpec((images, lse_rows, pad), lambda step: (which, 0, 0)),
        ],
        [whole((block, 3 * width)), whole((block, width))],
        [
            jax.ShapeDtypeStruct((block, 3 * width), BF),
            jax.ShapeDtypeStruct((block, width), BF),
        ],
        [pltpu.VMEM((block, width), BF)],
        2.0 * block * width * width + 20.0 * block * pad * width * 4, 8.0e6, "attn_core",
        after,
    )(incoming, weights, qkv, lse)


def attn_grad_kernel(
    da_ref, h_ref, g_ref, b_ref, w_ref, dq0_ref, dq1_ref, low0_ref, low1_ref, o_ref,
    dh_ref, dw_ref, dqb_ref, dob_ref, dg_ref, db_ref,
):
    width = h_ref.shape[1]
    block = dq0_ref.shape[0]
    gain = g_ref[...]
    unit, scale = norm_parts(h_ref[...])
    normed = (unit * gain + b_ref[...]).astype(BF)
    half = (slice(0, block), slice(block, 2 * block))
    normed_grad = [None, None]
    for part in range(3):
        cols = slice(part * width, (part + 1) * width)
        piece = None
        sums = None
        for side, ref in enumerate((dq0_ref, dq1_ref)):
            grads = ref[:, cols]
            term = mm_bt(grads, w_ref[:, cols])
            normed_grad[side] = term if part == 0 else normed_grad[side] + term
            outer = mm_at(normed[half[side]], grads)
            total = jnp.sum(grads.astype(F32), axis=0, keepdims=True)
            piece = outer if side == 0 else piece + outer
            sums = total if side == 0 else sums + total
        at = (part % 2) * width
        put_grad(dw_ref, part // 2, slice(at, at + width), piece.astype(BF))
        dqb_ref[:, cols] = sums
    low0, low1 = low0_ref[...], low1_ref[...]
    piece = mm_at(low0, o_ref[half[0], :]) + mm_at(low1, o_ref[half[1], :])
    put_grad(dw_ref, 1, slice(width, 2 * width), piece.astype(BF))
    dob_ref[...] = jnp.sum(low0.astype(F32), axis=0, keepdims=True) + jnp.sum(
        low1.astype(F32), axis=0, keepdims=True
    )
    for side in range(2):
        hidden_grad, gain_grad, shift_grad = norm_pull(
            unit[half[side]], scale[half[side]], gain, normed_grad[side]
        )
        dh_ref[half[side], :] = da_ref[half[side], :] + hidden_grad
        if side == 0:
            dg_ref[...] = gain_grad
            db_ref[...] = shift_grad
        else:
            dg_ref[...] += gain_grad
            db_ref[...] += shift_grad


def attention_grad(
    incoming, hidden, gain, shift, weights, layer, cores, mixed, devices, after=()
):
    rows, width = hidden.shape
    shape = grad_shape(devices, width, 2 * width)
    block = rows // 2
    return call(
        attn_grad_kernel, (1,),
        [
            whole((rows, width)), whole((rows, width)), whole((1, width)), whole((1, width)),
            layer_block(width, layer), whole((block, 3 * width)), whole((block, 3 * width)),
            whole((block, width)), whole((block, width)), whole((rows, width)),
        ],
        [
            whole((rows, width)), whole(shape), whole((1, 3 * width)),
            whole((1, width)), whole((1, width)), whole((1, width)),
        ],
        [
            jax.ShapeDtypeStruct((rows, width), F32),
            jax.ShapeDtypeStruct(shape, BF),
            jax.ShapeDtypeStruct((1, 3 * width), F32),
            jax.ShapeDtypeStruct((1, width), F32),
            jax.ShapeDtypeStruct((1, width), F32),
            jax.ShapeDtypeStruct((1, width), F32),
        ],
        [],
        14.0 * rows * width * width, 25.0e6, "attn_grad", after,
    )(incoming, hidden, gain, shift, weights, cores[0][0], cores[1][0], cores[0][1],
      cores[1][1], mixed)


def dense_fwd_kernel(a_ref, g_ref, b_ref, win_ref, wout_ref, bin_ref, bout_ref, x_ref, m_sc, acc):
    step = pl.program_id(0)

    @pl.when(step == 0)
    def _():
        unit, _ = norm_parts(a_ref[...])
        m_sc[...] = (unit * g_ref[...] + b_ref[...]).astype(BF)
        acc[...] = a_ref[...] + bout_ref[...]

    preact = mm(m_sc[...], win_ref[...]) + bin_ref[...]
    active = gelu_value(preact).astype(BF)
    acc[...] += mm_bt(active, wout_ref[...])

    @pl.when(step == pl.num_programs(0) - 1)
    def _():
        x_ref[...] = acc[...]


def dense_forward(hidden, gain, shift, weights, at, in_bias, out_bias):
    rows, width = hidden.shape
    ff = in_bias.shape[1]
    steps = ff // FF_BLOCK
    start = at // FF_BLOCK
    return call(
        dense_fwd_kernel, (steps,),
        [
            whole((rows, width)), whole((1, width)), whole((1, width)),
            pl.BlockSpec((width, FF_BLOCK), lambda c: (0, start + c)),
            pl.BlockSpec((width, FF_BLOCK), lambda c: (0, start + steps + c)),
            pl.BlockSpec((1, FF_BLOCK), lambda c: (0, c)),
            whole((1, width)),
        ],
        whole((rows, width)),
        jax.ShapeDtypeStruct((rows, width), F32),
        [pltpu.VMEM((rows, width), BF), pltpu.VMEM((rows, width), F32)],
        4.0 * rows * width * ff, 15.0e6, "dense_fwd",
    )(hidden, gain, shift, weights, weights, in_bias, out_bias)


def dense_bwd_kernel(
    last_call, dx_ref, a_ref, g_ref, b_ref, win_ref, wout_ref, bin_ref, *rest,
):
    if last_call:
        part_ref, da_ref, dw_ref, dbin_ref, dbout_ref, dg_ref, db_ref, m_sc, low_sc, acc = rest
    else:
        part_ref, dw_ref, dbin_ref, m_sc, low_sc, acc = rest
    step = pl.program_id(0)

    @pl.when(step == 0)
    def _():
        unit, _ = norm_parts(a_ref[...])
        m_sc[...] = (unit * g_ref[...] + b_ref[...]).astype(BF)
        low_sc[...] = dx_ref[...].astype(BF)
        if last_call:
            acc[...] = part_ref[...]
        else:
            acc[...] = jnp.zeros_like(acc)

    normed = m_sc[...]
    low = low_sc[...]
    preact = mm(normed, win_ref[...]) + bin_ref[...]
    active, slope = gelu_pair(preact)
    preact_grad = (slope * mm(low, wout_ref[...])).astype(BF)
    dbin_ref[...] = jnp.sum(preact_grad.astype(F32), axis=0, keepdims=True)
    every = slice(None)
    put_grad(dw_ref, 1, every, mm_at(low, active.astype(BF)).astype(BF))
    put_grad(dw_ref, 0, every, mm_at(normed, preact_grad).astype(BF))
    acc[...] += mm_bt(preact_grad, win_ref[...])

    @pl.when(step == pl.num_programs(0) - 1)
    def _():
        if not last_call:
            part_ref[...] = acc[...]
            return
        unit, scale = norm_parts(a_ref[...])
        hidden_grad, gain_grad, shift_grad = norm_pull(unit, scale, g_ref[...], acc[...])
        da_ref[...] = dx_ref[...] + hidden_grad
        dbout_ref[...] = jnp.sum(low_sc[...].astype(F32), axis=0, keepdims=True)
        dg_ref[...] = gain_grad
        db_ref[...] = shift_grad


def dense_back(incoming, hidden, gain, shift, weights, at, in_bias, devices, part, after=()):
    rows, width = hidden.shape
    ff = in_bias.shape[1]
    steps = ff // FF_BLOCK // 2
    last_call = part is not None
    first = steps if last_call else 0
    shape = grad_shape(devices, width, ff // 2)
    start = at // FF_BLOCK + first
    in_specs = [
        whole((rows, width)), whole((rows, width)), whole((1, width)), whole((1, width)),
        pl.BlockSpec((width, FF_BLOCK), lambda c: (0, start + c)),
        pl.BlockSpec((width, FF_BLOCK), lambda c: (0, start + 2 * steps + c)),
        pl.BlockSpec((1, FF_BLOCK), lambda c: (0, first + c)),
    ]
    wide = jax.ShapeDtypeStruct((rows, width), F32)
    short = jax.ShapeDtypeStruct((1, width), F32)
    grads = [
        jax.ShapeDtypeStruct(shape, BF), jax.ShapeDtypeStruct((1, ff // 2), F32),
    ]
    grad_specs = [
        grad_block(shape, FF_BLOCK, lambda c: c), pl.BlockSpec((1, FF_BLOCK), lambda c: (0, c)),
    ]
    args = [incoming, hidden, gain, shift, weights, weights, in_bias]
    if last_call:
        in_specs.append(whole((rows, width)))
        args.append(part)
        out_specs = [whole((rows, width))] + grad_specs + [whole((1, width))] * 3
        out_shape = [wide] + grads + [short] * 3
    else:
        out_specs = [whole((rows, width))] + grad_specs
        out_shape = [wide] + grads
    return call(
        functools.partial(dense_bwd_kernel, last_call), (steps,), in_specs, out_specs, out_shape,
        [
            pltpu.VMEM((rows, width), BF), pltpu.VMEM((rows, width), BF),
            pltpu.VMEM((rows, width), F32),
        ],
        5.0 * rows * width * ff, 25.0e6, "dense_bwd", after,
    )(*args)


def moe_kernel(
    micro, capp, base, resumed,
    rb_own, rb_oth, og_own, og_oth, dr_ref, dc_own, dc_oth, w_ref,
    win_ref, wout_ref, bin_ref, bout_ref, *rest,
):
    before = rest[:6] if resumed else ()
    (
        yc_own, yc_oth, rc_own, rc_oth, dg_own, dg_oth,
        dw_ref, dbin_ref, dbout_ref,
        b_sc, og_sc, dy_sc, w_sc, y_acc, r_acc, yo_acc, yt_acc, ro_acc, rt_acc,
    ) = rest[len(before):]
    expert = pl.program_id(0) + base
    fresh = pl.program_id(0) == 0
    chunk = pl.program_id(1)
    last_expert = pl.program_id(0) == pl.num_programs(0) - 1
    last_chunk = chunk == pl.num_programs(1) - 1
    half = rb_own.shape[1]

    @pl.when(chunk == 0)
    def _():
        for m in range(micro):
            slots = slice(m * capp, (m + 1) * capp)
            ids = lax.broadcasted_iota(jnp.int32, (capp, half), 0) + expert * capp
            tokens = None
            for side, (rb, og) in enumerate(((rb_own, og_own), (rb_oth, og_oth))):
                hit0 = dr_ref[m, 2 * side : 2 * side + 1, :] == ids
                hit1 = dr_ref[m, 2 * side + 1 : 2 * side + 2, :] == ids
                pick = jnp.where(hit0 | hit1, 1.0, 0.0).astype(BF)
                gate = jnp.sum(
                    jnp.where(hit0, w_ref[m, 2 * side : 2 * side + 1, :], 0.0)
                    + jnp.where(hit1, w_ref[m, 2 * side + 1 : 2 * side + 2, :], 0.0),
                    axis=-1, keepdims=True,
                )
                found = (mm(pick, rb[m]), mm(pick, og[m]), gate)
                tokens = found if tokens is None else tuple(
                    one + two for one, two in zip(tokens, found)
                )
            b_sc[slots, :] = tokens[0].astype(BF)
            og_sc[slots, :] = tokens[1].astype(BF)
            dy_sc[slots, :] = (tokens[1] * tokens[2]).astype(BF)
            w_sc[slots, :] = jnp.broadcast_to(tokens[2], (capp, w_sc.shape[1]))
        y_acc[...] = jnp.zeros_like(y_acc)
        r_acc[...] = jnp.zeros_like(r_acc)

    tokens = b_sc[...]
    low = dy_sc[...]
    preact = mm(tokens, win_ref[...]) + bin_ref[0]
    active, slope = gelu_pair(preact)
    active = active.astype(BF)
    preact_grad = (slope * mm(low, wout_ref[...])).astype(BF)
    dbin_ref[0] = jnp.sum(preact_grad.astype(F32), axis=0, keepdims=True)
    y_acc[...] += mm_bt(active, wout_ref[...])
    r_acc[...] += mm_bt(preact_grad, win_ref[...])
    every = slice(None)
    put_grad(dw_ref, 1, every, mm_at(low, active).astype(BF))
    put_grad(dw_ref, 0, every, mm_at(tokens, preact_grad).astype(BF))

    if resumed:
        @pl.when(fresh & (chunk == 0))
        def _():
            yo_acc[...] = before[0][...].astype(F32)
            yt_acc[...] = before[1][...].astype(F32)
            ro_acc[...] = before[2][...].astype(F32)
            rt_acc[...] = before[3][...].astype(F32)
            dg_own[...] = before[4][...]
            dg_oth[...] = before[5][...]

    @pl.when(last_chunk)
    def _():
        dbout_ref[0] = jnp.sum(dy_sc[...].astype(F32), axis=0, keepdims=True)
        for m in range(micro):
            slots = slice(m * capp, (m + 1) * capp)
            result = y_acc[slots, :] + 0.5 * bout_ref[0]
            dots = jnp.sum(og_sc[slots, :].astype(F32) * result, axis=-1, keepdims=True)
            lanes = lax.broadcasted_iota(jnp.int32, (capp, dg_own.shape[2]), 1)
            dots = jnp.where(lanes == expert, dots, 0.0)
            weighted = (w_sc[slots, 0:1] * result).astype(BF)
            rows_grad = r_acc[slots, :].astype(BF)
            ids = lax.broadcasted_iota(jnp.int32, (half, capp), 1) + expert * capp
            for dc, yc, rc, dg in (
                (dc_own, yo_acc, ro_acc, dg_own), (dc_oth, yt_acc, rt_acc, dg_oth)
            ):
                hit = (dc[m, :, 0:1] == ids) | (dc[m, :, 1:2] == ids)
                pick = jnp.where(hit, 1.0, 0.0)
                low_pick = pick.astype(BF)
                y_new = mm(low_pick, weighted)
                r_new = mm(low_pick, rows_grad)
                d_new = jnp.dot(pick, dots, precision=EXACT, preferred_element_type=F32)

                if resumed:
                    yc[m] += y_new
                    rc[m] += r_new
                    dg[m] += d_new
                    continue

                @pl.when(fresh)
                def _():
                    yc[m] = y_new
                    rc[m] = r_new
                    dg[m] = d_new

                @pl.when(jnp.logical_not(fresh))
                def _():
                    yc[m] += y_new
                    rc[m] += r_new
                    dg[m] += d_new

    @pl.when(last_chunk & last_expert)
    def _():
        yc_own[...] = yo_acc[...].astype(BF)
        yc_oth[...] = yt_acc[...].astype(BF)
        rc_own[...] = ro_acc[...].astype(BF)
        rc_oth[...] = rt_acc[...].astype(BF)


def mixture(rows_own, rows_oth, grad_own, grad_oth, place_rows, place_own, place_oth, gates,
            weights, in_bias, out_bias, capp, base, count, devices, before=(), after=()):
    micro, half, width = rows_own.shape
    experts, _, ff = in_bias.shape
    steps = ff // FF_BLOCK
    blocks = experts * steps
    first = base * steps
    lanes = 128
    slots = micro * capp
    w_block = (width, FF_BLOCK)
    group = (micro, half, width)
    dots = (micro, half, lanes)
    shape = grad_shape(devices, width, count * ff)
    sums = [jax.ShapeDtypeStruct(group, BF)] * 4 + [jax.ShapeDtypeStruct(dots, F32)] * 2
    sum_specs = [whole(group)] * 4 + [whole(dots)] * 2
    return call(
        functools.partial(moe_kernel, micro, capp, base, bool(before)),
        (count, steps),
        [
            whole(group), whole(group), whole(group), whole(group),
            whole(place_rows.shape), whole(place_own.shape), whole(place_oth.shape),
            whole(gates.shape),
            pl.BlockSpec(w_block, lambda e, c: (0, first + e * steps + c)),
            pl.BlockSpec(w_block, lambda e, c: (0, blocks + first + e * steps + c)),
            pl.BlockSpec((1, 1, FF_BLOCK), lambda e, c: (base + e, 0, c)),
            pl.BlockSpec((1, 1, width), lambda e, c: (base + e, 0, 0)),
        ] + (sum_specs if before else []),
        sum_specs + [
            grad_block(shape, FF_BLOCK, lambda e, c: e * steps + c),
            pl.BlockSpec((1, 1, FF_BLOCK), lambda e, c: (e, 0, c)),
            pl.BlockSpec((1, 1, width), lambda e, c: (e, 0, 0)),
        ],
        sums + [
            jax.ShapeDtypeStruct(shape, BF),
            jax.ShapeDtypeStruct((count, 1, ff), F32),
            jax.ShapeDtypeStruct((count, 1, width), F32),
        ],
        [
            pltpu.VMEM((slots, width), BF), pltpu.VMEM((slots, width), BF),
            pltpu.VMEM((slots, width), BF), pltpu.VMEM((slots, 128), F32),
            pltpu.VMEM((slots, width), F32), pltpu.VMEM((slots, width), F32),
            pltpu.VMEM(group, F32), pltpu.VMEM(group, F32),
            pltpu.VMEM(group, F32), pltpu.VMEM(group, F32),
        ],
        12.0 * slots * count * width * ff + 16.0 * count * micro * capp * half * width,
        15.0e6 * count, "experts", after,
    )(rows_own, rows_oth, grad_own, grad_oth, place_rows, place_own, place_oth, gates,
      weights, weights, in_bias, out_bias, *before)


def gate_bwd_kernel(
    a_ref, og_ref, yt_ref, ro_ref, rr_ref, do_ref, dr_ref, gp_ref, rt_ref, g_ref, b_ref,
    y_ref, da_ref, drt_ref, dg_ref, db_ref,
):
    step = pl.program_id(0)
    after = a_ref[...]
    incoming = og_ref[...].astype(F32)
    y_ref[...] = yt_ref[...]
    gates = gp_ref[...]
    gate_grad = do_ref[...] + dr_ref[...]
    logit_grad = gates * (gate_grad - jnp.sum(gates * gate_grad, axis=-1, keepdims=True))
    unit, scale = norm_parts(after)
    normed = unit * g_ref[...] + b_ref[...]
    router_grad = lax.dot_general(
        logit_grad, normed, (((0,), (0,)), ((), ())), precision=EXACT, preferred_element_type=F32
    )
    normed_grad = ro_ref[...].astype(F32) + rr_ref[...].astype(F32)
    normed_grad += lax.dot_general(
        logit_grad, rt_ref[...], (((1,), (1,)), ((), ())), precision=EXACT,
        preferred_element_type=F32,
    )
    hidden_grad, gain_grad, shift_grad = norm_pull(unit, scale, g_ref[...], normed_grad)
    da_ref[...] = incoming + hidden_grad

    @pl.when(step == 0)
    def _():
        drt_ref[...] = router_grad
        dg_ref[...] = gain_grad
        db_ref[...] = shift_grad

    @pl.when(step > 0)
    def _():
        drt_ref[...] += router_grad
        dg_ref[...] += gain_grad
        db_ref[...] += shift_grad


def gate_back(after, incoming, y_oth, r_own, r_got, d_own, d_got, gates, router, gain, shift):
    rows, width = after.shape
    lanes = gates.shape[1]
    block = rows // 2
    row = rows_of(block, width)
    row_low = rows_of(block, lanes)
    return call(
        gate_bwd_kernel, (2,),
        [
            row, row, row, row, row, row_low, row_low, row_low,
            whole((width, lanes)), whole((1, width)), whole((1, width)),
        ],
        [row, row, whole((lanes, width)), whole((1, width)), whole((1, width))],
        [
            jax.ShapeDtypeStruct((rows, width), BF),
            jax.ShapeDtypeStruct((rows, width), F32),
            jax.ShapeDtypeStruct((lanes, width), F32),
            jax.ShapeDtypeStruct((1, width), F32),
            jax.ShapeDtypeStruct((1, width), F32),
        ],
        [], 4.0 * rows * width * lanes, 14.0e6, "gate_bwd",
    )(after, incoming, y_oth, r_own, r_got, d_own, d_got, gates, router, gain, shift)


def swap(value):
    return lax.ppermute(value, "tensor", [(0, 1), (1, 0)])


def in_order(mine, other, axis):
    first = lax.axis_index("tensor") == 0
    return jnp.stack([jnp.where(first, mine, other), jnp.where(first, other, mine)], axis=axis)


def gather_rows(share):
    return lax.all_gather(share, "dp", axis=0, tiled=True)


def chip_ring(chips):
    if chips == 8:
        return [0, 2, 4, 6, 7, 5, 3, 1]
    return list(range(chips))


def ring_add_kernel(kind, at_ref, *refs):
    def chunk(grads, given):
        return grads[0, 0].astype(F32) + given[0].astype(F32)

    if kind == 0:
        grads, given, ahead, behind = refs
        total = chunk(grads, given).astype(BF)
        ahead[...] = total[0]
        behind[...] = total[1]
    elif kind == 3:
        grads, given, got_a, got_b, out = refs
        out[...] = chunk(grads, given) + (got_a[...].astype(F32) + got_b[...].astype(F32))
    else:
        grads_a, given_a, grads_b, given_b, got_a, got_b, ahead, behind = refs
        one, two = chunk(grads_a, given_a), chunk(grads_b, given_b)
        if kind == 1:
            ahead[0] = (one[0] + got_a[...].astype(F32)).astype(BF)
            ahead[1] = one[1].astype(BF)
            behind[0] = two[0].astype(BF)
            behind[1] = (two[1] + got_b[...].astype(F32)).astype(BF)
        else:
            ahead[...] = (one + got_a[...].astype(F32)).astype(BF)
            behind[...] = (two + got_b[...].astype(F32)).astype(BF)


class RingSum:
    def __init__(self, grad):
        count = lax.axis_size("dp")
        self.chips = count // 2
        self.ring = chip_ring(self.chips)
        position = [self.ring.index(chip) for chip in range(self.chips)]
        me = lax.axis_index("dp")
        self.core = me % 2
        self.here = jnp.array(position, jnp.int32)[me // 2]
        self.pieces = grad.reshape((self.chips, 2) + grad.shape[1:])
        self.away = self.chips // 2
        sent = lax.dynamic_index_in_dim(self.pieces, 1 - self.core, 1, keepdims=False)
        self.messages = (sent,)
        self.given = lax.ppermute(sent, "dp", [(at, at ^ 1) for at in range(count)])
        self.got = ()
        self.result = None

    def send(self, value, step):
        pairs = [
            (self.ring[at] * 2 + side, self.ring[(at + step) % self.chips] * 2 + side)
            for at in range(self.chips)
            for side in range(2)
        ]
        return lax.ppermute(value, "dp", pairs)

    def step(self, after=()):
        table = jnp.array(self.ring, jnp.int32)
        away = self.away
        chips = [table[(self.here + away) % self.chips], table[(self.here - away) % self.chips]]
        places = jnp.stack([self.core, *chips]).astype(jnp.int32)
        one, rows, columns = self.pieces.shape[2:]
        shape = (one, rows, columns)

        def chunk_specs(which):
            return [
                pl.BlockSpec((1, 1) + shape, lambda _, at: (at[1 + which], at[0], 0, 0, 0)),
                pl.BlockSpec((1,) + shape, lambda _, at: (at[1 + which], 0, 0, 0)),
            ]

        far = self.chips // 2
        kind = 3 if away == 0 else 0 if away == far else 1 if away == far - 1 else 2
        two_ways = kind in (1, 2)
        in_specs = chunk_specs(0) + (chunk_specs(1) if two_ways else [])
        args = [self.pieces, self.given] * (2 if two_ways else 1) + list(self.got)
        in_specs += [whole(got.shape) for got in self.got]
        out = shape if kind else shape[1:]
        kinds = [jax.ShapeDtypeStruct(out, F32 if kind == 3 else BF)] * (1 if kind == 3 else 2)
        sums = call(
            functools.partial(ring_add_kernel, kind), (1,), in_specs,
            [whole(out)] * len(kinds), kinds, [], 0, 1.0e6, "ring_add", after, prefetch=1,
        )(places, *args)
        self.away -= 1
        if kind == 3:
            self.result = sums[0]
            self.messages = ()
            return
        self.messages = tuple(sums)
        self.got = (self.send(sums[0], 1), self.send(sums[1], -1))


class PlainSum:
    def __init__(self, grad):
        axis = 1 if grad.ndim == 3 else 0
        done = lax.psum_scatter(grad, "dp", scatter_dimension=axis, tiled=True)
        self.result = done.reshape((2,) + done.shape[-2:]).astype(F32)
        self.messages = ()

    def step(self, after=()):
        return


def sum_small(vector):
    vector = vector + swap(vector)
    count = lax.axis_size("dp")
    step = 1
    while step < count:
        vector = vector + lax.ppermute(vector, "dp", [(at, at ^ step) for at in range(count)])
        step *= 2
    return vector


def join_halves(parts):
    mine = lax.axis_index("tensor")
    rows = parts[0].shape[0]
    pairs = [part.reshape(rows, 2, -1) for part in parts]
    sent = jnp.concatenate(
        [lax.dynamic_index_in_dim(pair, 1 - mine, 1, keepdims=False) for pair in pairs], axis=1
    )
    kept = jnp.concatenate(
        [lax.dynamic_index_in_dim(pair, mine, 1, keepdims=False) for pair in pairs], axis=1
    )
    return kept + swap(sent)


def own_half(value, axis):
    size = value.shape[axis] // 2
    return lax.dynamic_slice_in_dim(value, lax.axis_index("tensor") * size, size, axis)


def local(
    block_input, norm_gain, row_bias, qkv_weight, qkv_bias, out_weight, mlp_in, mlp_in_bias,
    mlp_out, mlp_out_bias, router, expert_in, expert_in_bias, expert_out, expert_out_bias,
    routes, slot_index, out_grad,
):
    micro, images, length, width = block_input.shape
    experts = router.shape[1]
    share_rows = mlp_in.shape[0]
    own_images = images // 2
    pad = round_up(length, ROW_PAD)
    half = own_images * pad
    rows = micro * half
    capp = round_up(CAP, ROW_PAD)
    side = lax.axis_index("tensor")

    def attn_share(layer):
        return jnp.concatenate(
            [qkv_weight[layer].reshape(share_rows, -1), out_weight[layer]], axis=1
        )

    first_mine = jnp.concatenate(
        [attn_share(0), attn_share(1), mlp_in, mlp_out], axis=1
    )
    first_other = swap(first_mine)
    attn_columns = 8 * (width // 2)

    def whole_columns(value, other, parts):
        pair = in_order(
            value.reshape(share_rows, parts, -1), other.reshape(share_rows, parts, -1), 2
        )
        return pair.reshape(share_rows, -1)

    first_w = gather_rows(
        jnp.concatenate(
            [
                whole_columns(first_mine[:, :attn_columns], first_other[:, :attn_columns], 8),
                whole_columns(first_mine[:, attn_columns:], first_other[:, attn_columns:], 2),
            ],
            axis=1,
        )
    )
    dense_at = 2 * attn_columns
    expert_w = gather_rows(
        jnp.concatenate(
            [expert_in.reshape(share_rows, -1), expert_out.reshape(share_rows, -1)], axis=1
        )
    )

    biases = jnp.concatenate([qkv_bias.reshape(-1), mlp_in_bias])
    biases_other = swap(biases)
    bias_pair = in_order(biases, biases_other, 0)
    split = qkv_bias.size
    qkv_bias_full = jnp.moveaxis(
        bias_pair[:, :split].reshape((2,) + qkv_bias.shape), 0, 2
    ).reshape(qkv_bias.shape[:2] + (width,))
    mlp_bias_full = bias_pair[:, split:].reshape(1, -1)

    def qkv_bias_row(layer):
        zero = jnp.zeros((width,), F32)
        return jnp.concatenate(
            [qkv_bias_full[layer, 0], zero, qkv_bias_full[layer, 1]]
        ).reshape(1, -1)

    def padded(value, start):
        part = lax.dynamic_slice_in_dim(value, start, own_images, 1)
        return jnp.pad(part, ((0, 0), (0, 0), (0, pad - length), (0, 0)))

    mine_at = side * own_images
    other_at = (1 - side) * own_images
    hidden = padded(block_input, mine_at).astype(F32).reshape(rows, width)
    grad_own = padded(out_grad, mine_at).reshape(micro, half, width)
    grad_oth = padded(out_grad, other_at).reshape(micro, half, width)

    kept = slot_index < CAP
    place = jnp.where(kept, routes * capp + slot_index, -1)
    pick = jnp.where(kept, routes, -1)

    def lay(value, start):
        part = lax.dynamic_slice_in_dim(value, start, own_images, 1)
        part = jnp.pad(
            part, ((0, 0), (0, 0), (0, pad - length), (0, 0)), constant_values=-1
        )
        return part.reshape(micro, half, 2)

    place_own, place_oth = lay(place, mine_at), lay(place, other_at)
    place_rows = jnp.concatenate(
        [jnp.swapaxes(place_own, 1, 2), jnp.swapaxes(place_oth, 1, 2)], axis=1
    )
    select = lay(pick, mine_at).reshape(rows, 2)
    router_wide = jnp.pad(router, ((0, 0), (0, 128 - experts)))

    def row(vector):
        return vector.reshape(1, -1)

    qkv_one, lse_one, mix_one, after_one = attention_forward(
        hidden, row(norm_gain[0, 0]), row(row_bias[0, 0]), first_w, 0, qkv_bias_row(0),
        row(row_bias[0, 2]), length, pad,
    )
    after_ffn = dense_forward(
        after_one, row(norm_gain[0, 1]), row(row_bias[0, 1]), first_w, dense_at, mlp_bias_full,
        row(mlp_out_bias),
    )
    qkv_two, lse_two, mix_two, after_two, rows_own, gates, chosen = attention_forward(
        after_ffn, row(norm_gain[1, 0]), row(row_bias[1, 0]), first_w, 1, qkv_bias_row(1),
        row(row_bias[1, 2]), length, pad,
        (row(norm_gain[1, 1]), row(row_bias[1, 1]), router_wide, select, experts),
    )
    rows_oth = swap(rows_own)
    gate_own = jnp.swapaxes(chosen[:, :2].reshape(micro, half, 2), 1, 2)
    gate_oth = swap(gate_own)
    gate_pair = jnp.concatenate([gate_own, gate_oth], axis=1)
    devices = lax.axis_size("dp")
    sum_over = PlainSum if len(grad_shape(devices, width, width)) == 3 else RingSum
    sums, expert_sums, ein_biases, eout_biases = (), [], [], []
    per_call = experts // 2
    for base in range(0, experts, per_call):
        found = mixture(
            rows_own.reshape(micro, half, width), rows_oth.reshape(micro, half, width),
            grad_own, grad_oth, place_rows, place_own, place_oth, gate_pair, expert_w,
            expert_in_bias.reshape(experts, 1, -1), expert_out_bias.reshape(experts, 1, -1),
            capp, base, per_call, devices, sums,
        )
        sums = tuple(found[:6])
        expert_sums.append(PlainSum(found[6]))
        ein_biases.append(found[7])
        eout_biases.append(found[8])
    y_own, y_oth, r_own, r_oth, d_own, d_oth = sums
    ein_bias = jnp.concatenate(ein_biases)
    eout_bias = jnp.concatenate(eout_biases)
    r_got, d_got = swap(r_oth), swap(d_oth)

    def flat(value):
        return value.reshape(rows, value.shape[-1])

    y_sent, grad_two, router_grad, gain_moe, shift_moe = gate_back(
        after_two, flat(grad_own), flat(y_oth), flat(r_own), flat(r_got),
        flat(d_own), flat(d_got), gates, router_wide,
        row(norm_gain[1, 1]), row(row_bias[1, 1]),
    )
    y_got = swap(y_sent)
    out_own = after_two + (flat(y_own).astype(F32) + y_got.astype(F32))

    stored_two = (qkv_two, lse_two, mix_two)
    cores = [
        attention_core_back(grad_two, first_w, 1, stored_two, length, pad, which)
        for which in range(2)
    ]
    grad_ffn, w_two, qb_two, ob_two, gain_two, shift_two = attention_grad(
        grad_two, after_ffn, row(norm_gain[1, 0]), row(row_bias[1, 0]), first_w, 1, cores,
        mix_two, devices,
    )
    sum_two = sum_over(w_two)
    dense_args = (
        grad_ffn, after_one, row(norm_gain[0, 1]), row(row_bias[0, 1]), first_w, dense_at,
        mlp_bias_full, devices,
    )
    part, dense_low, in_bias_low = dense_back(*dense_args, None, sum_two.messages)
    sum_low = sum_over(dense_low)
    sum_two.step((in_bias_low,))
    (
        grad_one, dense_high, in_bias_high, out_bias_grad, gain_ffn, shift_ffn,
    ) = dense_back(*dense_args, part, sum_two.messages + sum_low.messages)
    sum_high = sum_over(dense_high)
    done = (in_bias_high,)
    sum_two.step(done)
    sum_low.step(done)
    stored_one = (qkv_one, lse_one, mix_one)
    cores = []
    for which in range(2):
        flying = sum_two.messages + sum_low.messages + sum_high.messages
        cores.append(
            attention_core_back(
                grad_one, first_w, 0, stored_one, length, pad, which, flying
            )
        )
        done = (cores[-1][1],)
        sum_two.step(done)
        sum_low.step(done)
        sum_high.step(done)
    flying = sum_two.messages + sum_low.messages + sum_high.messages
    grad_zero, w_one, qb_one, ob_one, gain_one, shift_one = attention_grad(
        grad_one, hidden, row(norm_gain[0, 0]), row(row_bias[0, 0]), first_w, 0, cores,
        mix_one, devices, flying,
    )
    sum_one = sum_over(w_one)
    done = (qb_one,)
    for _ in range(devices // 2):
        for chain in (sum_two, sum_low, sum_high, sum_one):
            if chain.result is None:
                chain.step(done)
        done = ()
    in_bias_grad = jnp.concatenate([in_bias_low, in_bias_high], axis=1)

    def images_of(value):
        value = value.astype(BF).reshape(micro, own_images, pad, width)[:, :, :length]
        return in_order(value, swap(value), 1).reshape(block_input.shape)

    block_output = images_of(out_own)
    input_grad = images_of(grad_zero).astype(F32)

    expert_grads = jnp.concatenate(
        [chain.result.reshape(2, share_rows, per_call, -1) for chain in expert_sums], axis=2
    )

    def attn_done(done):
        return join_halves(
            [done[0, :, :width], done[0, :, width:], done[1, :, :width], done[1, :, width:]]
        )

    attn_grads = [attn_done(sum_one.result), attn_done(sum_two.result)]
    dense_done = join_halves(
        [
            jnp.concatenate([sum_low.result[part], sum_high.result[part]], axis=1)
            for part in range(2)
        ]
    )
    split_at = 3 * width // 2

    place_in = (side == jnp.arange(2)).astype(F32)
    ein_bias_wide = place_in[:, None, None] * ein_bias.reshape(1, experts, -1)
    late = [gain_one, shift_one, ob_one, qb_one]
    early = [
        gain_ffn, gain_two, gain_moe, shift_ffn, shift_two, shift_moe, ob_two, qb_two,
        in_bias_grad, out_bias_grad, router_grad[:experts], ein_bias_wide, 0.5 * eout_bias,
    ]

    def sum_list(values):
        total = sum_small(jnp.concatenate([value.reshape(-1) for value in values]))
        parts, at = [], 0
        for value in values:
            parts.append(total[at : at + value.size].reshape(value.shape))
            at += value.size
        return parts

    gain_one, shift_one, ob_one, qb_one = sum_list(late)
    (
        gain_ffn, gain_two, gain_moe, shift_ffn, shift_two, shift_moe, ob_two, qb_two,
        in_bias_sum, out_bias_sum, router_sum, ein_sum, eout_sum,
    ) = sum_list(early)
    gain_sum = jnp.concatenate([gain_one, gain_ffn, gain_two, gain_moe])
    shift_sum = jnp.concatenate([shift_one, shift_ffn, ob_one, shift_two, shift_moe, ob_two])
    qb_sum = jnp.concatenate([qb_one, qb_two])
    qb_sum = own_half(qb_sum.reshape(2, 3, width), 2)
    return (
        block_output,
        input_grad,
        gain_sum.reshape(norm_gain.shape),
        shift_sum.reshape(row_bias.shape),
        jnp.stack([part[:, :split_at] for part in attn_grads]).reshape(qkv_weight.shape),
        jnp.stack([qb_sum[:, 0], qb_sum[:, 2]], axis=1),
        jnp.stack([part[:, split_at:] for part in attn_grads]),
        dense_done[:, : mlp_in.shape[1]],
        own_half(in_bias_sum.reshape(-1), 0),
        dense_done[:, mlp_in.shape[1] :],
        out_bias_sum.reshape(-1),
        router_sum.T,
        expert_grads[0],
        lax.dynamic_index_in_dim(ein_sum, side, 0, keepdims=False),
        expert_grads[1],
        eout_sum.reshape(experts, width),
    )


def solution(mesh):
    return jax.shard_map(
        local,
        mesh=mesh,
        in_specs=(
            P(None, "dp", None, None), P(), P(), P(None, "dp", None, "tensor"),
            P(None, None, "tensor"), P(None, "dp", "tensor"), P("dp", "tensor"), P("tensor"),
            P("dp", "tensor"), P(), P(), P("dp", None, "tensor"), P(None, "tensor"),
            P("dp", None, "tensor"), P(), P(None, "dp", None, None), P(None, "dp", None, None),
            P(None, "dp", None, None),
        ),
        out_specs=(
            P(None, "dp", None, None), P(None, "dp", None, None), P(), P(),
            P(None, "dp", None, "tensor"), P(None, None, "tensor"), P(None, "dp", "tensor"),
            P("dp", "tensor"), P("tensor"), P("dp", "tensor"), P(), P(),
            P("dp", None, "tensor"), P(None, "tensor"), P("dp", None, "tensor"), P(),
        ),
        check_vma=False,
    )
```

```python
import functools

import jax
import jax.numpy as jnp
from jax import lax
from jax.experimental import pallas as pl
from jax.experimental.pallas import tpu as pltpu
from jax.sharding import PartitionSpec as P

HD = 64
CAP = 295
NORM_EPS = 1e-06
EXACT = lax.Precision.HIGHEST
BF = jnp.bfloat16
F32 = jnp.float32
VMEM_LIMIT = 58 * 1024 * 1024
FF_BLOCK = 512
ROW_PAD = 16
GELU_SLOPE = 0.7978845608028654
GELU_CUBE = 0.044715


def round_up(value, unit):
    return -(-value // unit) * unit


def mm(left, right):
    return jnp.dot(left, right, preferred_element_type=F32)


def mm_bt(left, right):
    return lax.dot_general(left, right, (((1,), (1,)), ((), ())), preferred_element_type=F32)


def mm_at(left, right):
    return lax.dot_general(left, right, (((0,), (0,)), ((), ())), preferred_element_type=F32)


def norm_parts(hidden):
    center = jnp.mean(hidden, axis=-1, keepdims=True)
    centred = hidden - center
    spread = jnp.mean(centred * centred, axis=-1, keepdims=True)
    scale = lax.rsqrt(spread + NORM_EPS)
    return centred * scale, scale


def norm_pull(unit, scale, gain, incoming):
    wide = incoming * gain
    mean_wide = jnp.mean(wide, axis=-1, keepdims=True)
    mean_dot = jnp.mean(wide * unit, axis=-1, keepdims=True)
    hidden_grad = scale * (wide - mean_wide - unit * mean_dot)
    gain_grad = jnp.sum(incoming * unit, axis=0, keepdims=True)
    shift_grad = jnp.sum(incoming, axis=0, keepdims=True)
    return hidden_grad, gain_grad, shift_grad


def gelu_pair(preact):
    square = preact * preact
    inner = GELU_SLOPE * preact * (1.0 + GELU_CUBE * square)
    bend = jnp.tanh(inner)
    half = 0.5 * (1.0 + bend)
    active = preact * half
    slope = half + 0.5 * preact * (1.0 - bend * bend) * (
        GELU_SLOPE * (1.0 + 3.0 * GELU_CUBE * square)
    )
    return active, slope


def gelu_value(preact):
    square = preact * preact
    inner = GELU_SLOPE * preact * (1.0 + GELU_CUBE * square)
    return 0.5 * preact * (1.0 + jnp.tanh(inner))


def call(kernel, grid, in_specs, out_specs, out_shape, scratch, flops, traffic, name,
         after=(), prefetch=0):
    taken = prefetch + len(in_specs)
    skipped = len(after)

    def body(*refs):
        kernel(*refs[:taken], *refs[taken + skipped :])

    made = pl.pallas_call(
        body,
        grid_spec=pltpu.PrefetchScalarGridSpec(
            num_scalar_prefetch=prefetch,
            grid=grid,
            in_specs=list(in_specs) + [pl.BlockSpec(memory_space=pl.ANY)] * skipped,
            out_specs=out_specs,
            scratch_shapes=scratch,
        ),
        out_shape=out_shape,
        name=name,
        compiler_params=pltpu.CompilerParams(
            vmem_limit_bytes=VMEM_LIMIT,
            dimension_semantics=("arbitrary",) * len(grid),
        ),
        cost_estimate=pl.CostEstimate(
            flops=int(flops), bytes_accessed=int(traffic), transcendentals=0
        ),
    )
    return lambda *args: made(*args, *after)


def whole_tiles(devices, width):
    return (width // devices) % ROW_PAD == 0


def grad_shapes(devices, width, columns, split):
    if not whole_tiles(devices, width):
        return [(2, width, columns)]
    if split:
        return [(devices // 2, 2, width // devices, columns)] * 2
    return [(devices, 2, width // devices, columns)]


def grad_block(shape, columns, index):
    block = shape[:-1] + (columns,)
    zeros = (0,) * (len(shape) - 1)
    return pl.BlockSpec(block, lambda *at: zeros + (index(*at),))


def put_grad(refs, core_ref, part, cols, value):
    ref = refs[0]
    if len(refs) == 2:
        pieces = value.reshape(ref.shape[0], 2, ref.shape[2], value.shape[1])
        core = core_ref[0]

        @pl.when(core == 0)
        def _():
            refs[0][:, part, :, cols] = pieces[:, 0]
            refs[1][:, part, :, cols] = pieces[:, 1]

        @pl.when(core != 0)
        def _():
            refs[0][:, part, :, cols] = pieces[:, 1]
            refs[1][:, part, :, cols] = pieces[:, 0]
    elif len(ref.shape) == 3:
        ref[part, :, cols] = value
    else:
        ref[:, part, :, cols] = value.reshape(ref.shape[0], ref.shape[2], value.shape[1])


def flat_rows(value):
    return value.reshape(-1, value.shape[-1])


def weight_spec(weights, sides, columns, index):
    devices, _, rows, _ = weights.shape
    return pl.BlockSpec(
        (devices, sides, rows, columns), index, pipeline_mode=pl.Buffered(1)
    )


def whole(shape):
    zeros = (0,) * len(shape)
    return pl.BlockSpec(shape, lambda *_: zeros, pipeline_mode=pl.Buffered(1))


def rows_of(block, width):
    return pl.BlockSpec((block, width), lambda step, *_: (step, 0))


def half_of(value, block, which):
    at = which if value.shape[0] > block else 0
    rest = (0,) * (value.ndim - 1)
    return pl.BlockSpec((block,) + value.shape[1:], lambda *_: (at,) + rest)


def attn_fwd_kernel(
    length, pad, heads, router_on,
    h_ref, g_ref, b_ref, w_ref, qb_ref, ob_ref, *rest,
):
    if router_on:
        g2_ref, b2_ref, rt_ref, sel_ref = rest[:4]
        qkv_ref, lse_ref, o_ref, a_ref, rb_ref, gp_ref, wt_ref = rest[4:]
    else:
        qkv_ref, lse_ref, o_ref, a_ref = rest
    width = h_ref.shape[1]
    images = h_ref.shape[0] // pad
    hidden = h_ref[...]
    unit, _ = norm_parts(hidden)
    normed = (unit * g_ref[...] + b_ref[...]).astype(BF)
    third = width // 2
    for t in range(2):
        cols = slice(t * 3 * third, (t + 1) * 3 * third)
        matrix = flat_rows(w_ref[:, t, :, : 3 * third])
        qkv_ref[:, cols] = (mm(normed, matrix) + qb_ref[:, cols]).astype(BF)
    pairs = heads // 2
    lane = lax.broadcasted_iota(jnp.int32, (pad, 2 * HD), 1)
    key_row = lax.broadcasted_iota(jnp.int32, (pad, pad), 0)

    def pair_step(step, carry):
        image = step // pairs
        pair = step % pairs
        rows = pl.ds(pl.multiple_of(image * pad, ROW_PAD), pad)

        def col(part):
            side = pair // (pairs // 2)
            at = (side * 3 + part) * (width // 2) + (pair % (pairs // 2)) * 2 * HD
            return pl.ds(pl.multiple_of(at, 2 * HD), 2 * HD)

        place = pl.ds(pl.multiple_of(pair * 2 * HD, 2 * HD), 2 * HD)

        query = qkv_ref[rows, col(0)] * HD ** (-0.5)
        key = qkv_ref[rows, col(1)]
        value = qkv_ref[rows, col(2)]
        mixed = []
        for half in range(2):
            mine = (lane >= HD) if half else (lane < HD)
            scores = mm_bt(key, jnp.where(mine, query, 0).astype(BF))
            scores = jnp.where(key_row < length, scores, -1e30)
            top = jnp.max(scores, axis=0, keepdims=True)
            weights = jnp.exp(scores - top)
            total = jnp.sum(weights, axis=0, keepdims=True)
            probs = (weights * (1.0 / total)).astype(BF)
            mixed.append(mm_at(probs, value))
            lse_ref[image, pl.ds(pair * 2 + half, 1), :] = top + jnp.log(total)
        o_ref[rows, place] = jnp.where(lane < HD, mixed[0], mixed[1]).astype(BF)
        return carry

    lax.fori_loop(0, images * pairs, pair_step, 0)
    out_matrix = jnp.concatenate(
        [flat_rows(w_ref[:, t, :, 3 * third :]) for t in range(2)], axis=1
    )
    after = hidden + mm_bt(o_ref[...], out_matrix) + ob_ref[...]
    a_ref[...] = after
    if router_on:
        unit2, _ = norm_parts(after)
        normed2 = unit2 * g2_ref[...] + b2_ref[...]
        rb_ref[...] = normed2.astype(BF)
        logits = jnp.dot(normed2, rt_ref[...], precision=EXACT, preferred_element_type=F32)
        lanes = lax.broadcasted_iota(jnp.int32, logits.shape, 1)
        live = lanes < router_on
        logits = jnp.where(live, logits, -1e30)
        gates = jnp.exp(logits - jnp.max(logits, axis=-1, keepdims=True))
        gates = gates / jnp.sum(gates, axis=-1, keepdims=True)
        gates = jnp.where(live, gates, 0.0)
        gp_ref[...] = gates
        first = jnp.sum(jnp.where(lanes == sel_ref[:, 0:1], gates, 0.0), axis=-1, keepdims=True)
        second = jnp.sum(jnp.where(lanes == sel_ref[:, 1:2], gates, 0.0), axis=-1, keepdims=True)
        wt_ref[...] = jnp.where(lanes == 0, first, jnp.where(lanes == 1, second, 0.0))


def attention_forward(
    hidden, gain, shift, weights, layer, qkv_bias, out_bias, length, pad, start, count,
    router=None,
):
    micro = 2
    rows, width = hidden.shape
    heads = width // HD
    block = rows // micro
    lse_rows = round_up(heads, 8)
    images = block // pad
    made = count * block
    in_specs = [
        pl.BlockSpec((block, width), lambda step: (start + step, 0)),
        whole((1, width)), whole((1, width)),
        weight_spec(weights, 2, 2 * width, lambda *_: (0, 0, 0, layer)),
        whole((1, 3 * width)), whole((1, width)),
    ]
    args = [hidden, gain, shift, weights, qkv_bias, out_bias]
    out_specs = [
        rows_of(block, 3 * width),
        pl.BlockSpec((images, lse_rows, pad), lambda step: (step, 0, 0)),
        rows_of(block, width),
        rows_of(block, width),
    ]
    out_shape = [
        jax.ShapeDtypeStruct((made, 3 * width), BF),
        jax.ShapeDtypeStruct((count * images, lse_rows, pad), F32),
        jax.ShapeDtypeStruct((made, width), BF),
        jax.ShapeDtypeStruct((made, width), F32),
    ]
    router_on = 0
    if router is not None:
        gain2, shift2, router_wide, select, router_on = router
        lanes = router_wide.shape[1]
        in_specs += [
            whole((1, width)), whole((1, width)), whole((width, lanes)),
            pl.BlockSpec((block, 2), lambda step: (start + step, 0)),
        ]
        args += [gain2, shift2, router_wide, select]
        out_specs += [rows_of(block, width), rows_of(block, lanes), rows_of(block, lanes)]
        out_shape += [
            jax.ShapeDtypeStruct((made, width), BF),
            jax.ShapeDtypeStruct((made, lanes), F32),
            jax.ShapeDtypeStruct((made, lanes), F32),
        ]
    return call(
        functools.partial(attn_fwd_kernel, length, pad, heads, router_on),
        (count,), in_specs, out_specs, out_shape, [],
        8.0 * made * width * width + 16.0 * made * pad * width, 12.0e6, "attn_fwd",
    )(*args)


def attn_core_kernel(
    length, pad, heads, da_ref, wo_ref, qkv_ref, lse_ref, dqkv_ref, low_ref, grad_sc,
):
    width = da_ref.shape[1]
    images = da_ref.shape[0] // pad
    pairs = heads // 2
    low = da_ref[...].astype(BF)
    low_ref[...] = low
    out_matrix = jnp.concatenate([flat_rows(wo_ref[:, t]) for t in range(2)], axis=1)
    grad_sc[...] = mm(low, out_matrix).astype(BF)
    lane = lax.broadcasted_iota(jnp.int32, (pad, 2 * HD), 1)
    key_row = lax.broadcasted_iota(jnp.int32, (pad, pad), 0)

    def pair_step(step, carry):
        image = step // pairs
        pair = step % pairs
        rows = pl.ds(pl.multiple_of(image * pad, ROW_PAD), pad)

        def col(part):
            side = pair // (pairs // 2)
            at = (side * 3 + part) * (width // 2) + (pair % (pairs // 2)) * 2 * HD
            return pl.ds(pl.multiple_of(at, 2 * HD), 2 * HD)

        place = pl.ds(pl.multiple_of(pair * 2 * HD, 2 * HD), 2 * HD)

        query = (qkv_ref[rows, col(0)] * HD ** (-0.5)).astype(BF)
        key = qkv_ref[rows, col(1)]
        value = qkv_ref[rows, col(2)]
        mixed = grad_sc[rows, place]
        parts = []
        for half in range(2):
            mine = (lane >= HD) if half else (lane < HD)
            scores = mm_bt(key, jnp.where(mine, query, 0).astype(BF))
            total = lse_ref[image, pl.ds(pair * 2 + half, 1), :]
            probs = jnp.where(key_row < length, jnp.exp(scores - total), 0.0)
            probs_grad = mm_bt(value, jnp.where(mine, mixed, 0).astype(BF))
            product = probs * probs_grad
            delta = jnp.sum(product, axis=0, keepdims=True)
            score_grad = (product - probs * delta).astype(BF)
            parts.append((
                mm_at(score_grad, key) * HD ** (-0.5),
                mm(score_grad, query),
                mm(probs.astype(BF), mixed),
            ))
        for part in range(3):
            dqkv_ref[rows, col(part)] = jnp.where(
                lane < HD, parts[0][part], parts[1][part]
            ).astype(BF)
        return carry

    lax.fori_loop(0, images * pairs, pair_step, 0)


def attention_core_back(incoming, weights, layer, stored, length, pad, which, after=()):
    qkv, lse, block = stored
    width = incoming.shape[1]
    heads = width // HD
    images = block // pad
    return call(
        functools.partial(attn_core_kernel, length, pad, heads),
        (1,),
        [
            half_of(incoming, block, which),
            weight_spec(weights, 2, width // 2, lambda *_: (0, 0, 0, 4 * layer + 3)),
            half_of(qkv, block, which),
            half_of(lse, images, which),
        ],
        [whole((block, 3 * width)), whole((block, width))],
        [
            jax.ShapeDtypeStruct((block, 3 * width), BF),
            jax.ShapeDtypeStruct((block, width), BF),
        ],
        [pltpu.VMEM((block, width), BF)],
        2.0 * block * width * width + 20.0 * block * pad * width * 4, 8.0e6, "attn_core",
        after,
    )(incoming, weights, qkv, lse)


def attn_grad_kernel(
    core_ref, da0_ref, da1_ref, h_ref, g_ref, b_ref, w_ref, dq0_ref, dq1_ref,
    low0_ref, low1_ref, o0_ref, o1_ref, *outs,
):
    dw_refs = outs[: len(outs) - 5]
    dh_ref, dqb_ref, dob_ref, dg_ref, db_ref = outs[len(outs) - 5 :]
    width = h_ref.shape[1]
    block = dq0_ref.shape[0]
    gain = g_ref[...]
    unit, scale = norm_parts(h_ref[...])
    normed = (unit * gain + b_ref[...]).astype(BF)
    half = (slice(0, block), slice(block, 2 * block))
    third = width // 2
    normed_grad = [None, None]
    for t in range(2):
        cols = slice(t * 3 * third, (t + 1) * 3 * third)
        matrix = flat_rows(w_ref[:, t, :, : 3 * third])
        piece = sums = mix = None
        sides = ((dq0_ref, low0_ref, o0_ref), (dq1_ref, low1_ref, o1_ref))
        for side, (dq_ref, low_ref, o_ref) in enumerate(sides):
            grads = dq_ref[:, cols]
            term = mm_bt(grads, matrix)
            normed_grad[side] = term if t == 0 else normed_grad[side] + term
            outer = mm_at(normed[half[side]], grads)
            total = jnp.sum(grads.astype(F32), axis=0, keepdims=True)
            out = mm_at(low_ref[...], o_ref[:, t * third : (t + 1) * third])
            piece = outer if side == 0 else piece + outer
            sums = total if side == 0 else sums + total
            mix = out if side == 0 else mix + out
        put_grad(dw_refs, core_ref, t, slice(0, 3 * third), piece.astype(BF))
        put_grad(dw_refs, core_ref, t, slice(3 * third, 4 * third), mix.astype(BF))
        dqb_ref[:, cols] = sums
    dob_ref[...] = jnp.sum(low0_ref[...].astype(F32), axis=0, keepdims=True) + jnp.sum(
        low1_ref[...].astype(F32), axis=0, keepdims=True
    )
    for side, da_ref in enumerate((da0_ref, da1_ref)):
        hidden_grad, gain_grad, shift_grad = norm_pull(
            unit[half[side]], scale[half[side]], gain, normed_grad[side]
        )
        dh_ref[half[side], :] = (da_ref[...] + hidden_grad).astype(dh_ref.dtype)
        if side == 0:
            dg_ref[...] = gain_grad
            db_ref[...] = shift_grad
        else:
            dg_ref[...] += gain_grad
            db_ref[...] += shift_grad


def attention_grad(
    core, incoming, hidden, gain, shift, weights, layer, cores, mixed, devices, split, kind,
    after=(),
):
    rows, width = hidden.shape
    shapes = grad_shapes(devices, width, 2 * width, split)
    block = rows // 2
    short = jax.ShapeDtypeStruct((1, width), F32)
    made = call(
        attn_grad_kernel, (1,),
        [
            half_of(incoming[0], block, 0), half_of(incoming[1], block, 1),
            whole((rows, width)), whole((1, width)), whole((1, width)),
            weight_spec(weights, 2, 2 * width, lambda *_: (0, 0, 0, layer)),
            whole((block, 3 * width)), whole((block, 3 * width)),
            whole((block, width)), whole((block, width)),
            half_of(mixed[0], block, 0), half_of(mixed[1], block, 1),
        ],
        [whole(shape) for shape in shapes] + [
            whole((rows, width)), whole((1, 3 * width)),
            whole((1, width)), whole((1, width)), whole((1, width)),
        ],
        [jax.ShapeDtypeStruct(shape, BF) for shape in shapes] + [
            jax.ShapeDtypeStruct((rows, width), kind),
            jax.ShapeDtypeStruct((1, 3 * width), F32),
            short, short, short,
        ],
        [],
        14.0 * rows * width * width, 25.0e6, "attn_grad", after, prefetch=1,
    )(core, *incoming, hidden, gain, shift, weights, cores[0][0], cores[1][0], cores[0][1],
      cores[1][1], *mixed)
    return made[: len(shapes)], made[len(shapes) :]


def dense_fwd_kernel(a_ref, g_ref, b_ref, win_ref, wout_ref, bin_ref, bout_ref, x_ref, m_sc, acc):
    step = pl.program_id(0)

    @pl.when(step == 0)
    def _():
        unit, _ = norm_parts(a_ref[...])
        m_sc[...] = (unit * g_ref[...] + b_ref[...]).astype(BF)
        acc[...] = a_ref[...] + bout_ref[...]

    preact = mm(m_sc[...], flat_rows(win_ref[...])) + bin_ref[...]
    active = gelu_value(preact).astype(BF)
    acc[...] += mm_bt(active, flat_rows(wout_ref[...]))

    @pl.when(step == pl.num_programs(0) - 1)
    def _():
        x_ref[...] = acc[...]


def dense_specs(weights, at, ff):
    devices, _, rows, _ = weights.shape
    steps = ff // 2 // FF_BLOCK
    block = (devices, 1, rows, FF_BLOCK)
    start = at // FF_BLOCK
    return [
        pl.BlockSpec(block, lambda c, *_: (0, c // steps, 0, start + c % steps)),
        pl.BlockSpec(block, lambda c, *_: (0, c // steps, 0, start + steps + c % steps)),
        pl.BlockSpec((1, FF_BLOCK), lambda c, *_: (0, c)),
    ]


def dense_forward(hidden, gain, shift, weights, at, in_bias, out_bias):
    rows, width = hidden.shape
    ff = in_bias.shape[1]
    return call(
        dense_fwd_kernel, (ff // FF_BLOCK,),
        [whole((rows, width)), whole((1, width)), whole((1, width))]
        + dense_specs(weights, at, ff) + [whole((1, width))],
        whole((rows, width)),
        jax.ShapeDtypeStruct((rows, width), F32),
        [pltpu.VMEM((rows, width), BF), pltpu.VMEM((rows, width), F32)],
        4.0 * rows * width * ff, 15.0e6, "dense_fwd",
    )(hidden, gain, shift, weights, weights, in_bias, out_bias)


def dense_bwd_kernel(
    core_ref, dx_ref, a_ref, g_ref, b_ref, win_ref, wout_ref, bin_ref, *rest,
):
    dw_refs = rest[: len(rest) - 8]
    da_ref, dbin_ref, dbout_ref, dg_ref, db_ref, m_sc, low_sc, acc = rest[len(rest) - 8 :]
    step = pl.program_id(0)

    @pl.when(step == 0)
    def _():
        unit, _ = norm_parts(a_ref[...])
        m_sc[...] = (unit * g_ref[...] + b_ref[...]).astype(BF)
        low = dx_ref[...].astype(BF)
        low_sc[...] = low
        dbout_ref[...] = jnp.sum(low.astype(F32), axis=0, keepdims=True)
        acc[...] = jnp.zeros_like(acc)

    normed = m_sc[...]
    low = low_sc[...]
    in_matrix = flat_rows(win_ref[...])
    preact = mm(normed, in_matrix) + bin_ref[...]
    active, slope = gelu_pair(preact)
    preact_grad = (slope * mm(low, flat_rows(wout_ref[...]))).astype(BF)
    dbin_ref[...] = jnp.sum(preact_grad.astype(F32), axis=0, keepdims=True)
    every = slice(None)
    put_grad(dw_refs, core_ref, 1, every, mm_at(low, active.astype(BF)).astype(BF))
    put_grad(dw_refs, core_ref, 0, every, mm_at(normed, preact_grad).astype(BF))
    acc[...] += mm_bt(preact_grad, in_matrix)

    @pl.when(step == pl.num_programs(0) - 1)
    def _():
        unit, scale = norm_parts(a_ref[...])
        hidden_grad, gain_grad, shift_grad = norm_pull(unit, scale, g_ref[...], acc[...])
        da_ref[...] = dx_ref[...] + hidden_grad
        dg_ref[...] = gain_grad
        db_ref[...] = shift_grad


def dense_back(core, incoming, hidden, gain, shift, weights, at, in_bias, devices, split,
               after=()):
    rows, width = hidden.shape
    ff = in_bias.shape[1]
    shapes = grad_shapes(devices, width, ff, split)
    short = jax.ShapeDtypeStruct((1, width), F32)
    made = call(
        dense_bwd_kernel, (ff // FF_BLOCK,),
        [whole((rows, width)), whole((rows, width)), whole((1, width)), whole((1, width))]
        + dense_specs(weights, at, ff),
        [grad_block(shape, FF_BLOCK, lambda c, *_: c) for shape in shapes] + [
            whole((rows, width)), pl.BlockSpec((1, FF_BLOCK), lambda c, *_: (0, c)),
            whole((1, width)), whole((1, width)), whole((1, width)),
        ],
        [jax.ShapeDtypeStruct(shape, BF) for shape in shapes] + [
            jax.ShapeDtypeStruct((rows, width), F32), jax.ShapeDtypeStruct((1, ff), F32),
            short, short, short,
        ],
        [
            pltpu.VMEM((rows, width), BF), pltpu.VMEM((rows, width), BF),
            pltpu.VMEM((rows, width), F32),
        ],
        10.0 * rows * width * ff, 35.0e6, "dense_bwd", after, prefetch=1,
    )(core, incoming, hidden, gain, shift, weights, weights, in_bias)
    return made[: len(shapes)], made[len(shapes) :]


def moe_kernel(
    capp,
    rb_own0, rb_own1, rb_oth0, rb_oth1, og_own, og_oth, dr_ref, dc_own, dc_oth, w_ref,
    win_ref, wout_ref, bin_ref, bout_ref,
    yc_own, yc_oth, rc_own, rc_oth0, rc_oth1, dg_own, dg_oth, dw_ref, dbin_ref, dbout_ref,
    b_sc, og_sc, dy_sc, w_sc, y_acc, r_acc, yo_acc, yt_acc, ro_acc, rt_acc,
):
    micro = 2
    expert = pl.program_id(0)
    chunk = pl.program_id(1)
    last_expert = expert == pl.num_programs(0) - 1
    last_chunk = chunk == pl.num_programs(1) - 1
    half = rb_own0.shape[0]
    rb_all = ((rb_own0, rb_oth0), (rb_own1, rb_oth1))

    @pl.when(chunk == 0)
    def _():
        for m in range(micro):
            slots = slice(m * capp, (m + 1) * capp)
            ids = lax.broadcasted_iota(jnp.int32, (capp, half), 0) + expert * capp
            tokens = None
            for side, og in enumerate((og_own, og_oth)):
                hit0 = dr_ref[m, 2 * side : 2 * side + 1, :] == ids
                hit1 = dr_ref[m, 2 * side + 1 : 2 * side + 2, :] == ids
                pick = jnp.where(hit0 | hit1, 1.0, 0.0).astype(BF)
                gate = jnp.sum(
                    jnp.where(hit0, w_ref[m, 2 * side : 2 * side + 1, :], 0.0)
                    + jnp.where(hit1, w_ref[m, 2 * side + 1 : 2 * side + 2, :], 0.0),
                    axis=-1, keepdims=True,
                )
                found = (mm(pick, rb_all[m][side][...]), mm(pick, og[m]), gate)
                tokens = found if tokens is None else tuple(
                    one + two for one, two in zip(tokens, found)
                )
            b_sc[slots, :] = tokens[0].astype(BF)
            og_sc[slots, :] = tokens[1].astype(BF)
            dy_sc[slots, :] = (tokens[1] * tokens[2]).astype(BF)
            w_sc[slots, :] = jnp.broadcast_to(tokens[2], (capp, w_sc.shape[1]))
        y_acc[...] = jnp.zeros_like(y_acc)
        r_acc[...] = jnp.zeros_like(r_acc)

    tokens = b_sc[...]
    low = dy_sc[...]
    preact = mm(tokens, win_ref[...]) + bin_ref[0]
    active, slope = gelu_pair(preact)
    active = active.astype(BF)
    preact_grad = (slope * mm(low, wout_ref[...])).astype(BF)
    dbin_ref[0] = jnp.sum(preact_grad.astype(F32), axis=0, keepdims=True)
    y_acc[...] += mm_bt(active, wout_ref[...])
    r_acc[...] += mm_bt(preact_grad, win_ref[...])
    every = slice(None)
    put_grad((dw_ref,), None, 1, every, mm_at(low, active).astype(BF))
    put_grad((dw_ref,), None, 0, every, mm_at(tokens, preact_grad).astype(BF))

    @pl.when(last_chunk)
    def _():
        dbout_ref[0] = jnp.sum(dy_sc[...].astype(F32), axis=0, keepdims=True)
        for m in range(micro):
            slots = slice(m * capp, (m + 1) * capp)
            result = y_acc[slots, :] + 0.5 * bout_ref[0]
            dots = jnp.sum(og_sc[slots, :].astype(F32) * result, axis=-1, keepdims=True)
            lanes = lax.broadcasted_iota(jnp.int32, (capp, 128), 1)
            dots = jnp.where(lanes == expert, dots, 0.0)
            weighted = (w_sc[slots, 0:1] * result).astype(BF)
            rows_grad = r_acc[slots, :].astype(BF)
            ids = lax.broadcasted_iota(jnp.int32, (half, capp), 1) + expert * capp
            for dc, yc, rc, dg in (
                (dc_own, yo_acc, ro_acc, dg_own), (dc_oth, yt_acc, rt_acc, dg_oth)
            ):
                hit = (dc[m, :, 0:1] == ids) | (dc[m, :, 1:2] == ids)
                pick = jnp.where(hit, 1.0, 0.0)
                low_pick = pick.astype(BF)
                y_new = mm(low_pick, weighted)
                r_new = mm(low_pick, rows_grad)
                d_new = lax.dot_general(
                    dots, pick, (((0,), (1,)), ((), ())), precision=EXACT,
                    preferred_element_type=F32,
                )[: dg.shape[1]]

                @pl.when(expert == 0)
                def _():
                    yc[m] = y_new
                    rc[m] = r_new
                    dg[m] = d_new

                @pl.when(expert > 0)
                def _():
                    yc[m] += y_new
                    rc[m] += r_new
                    dg[m] += d_new

    @pl.when(last_chunk & last_expert)
    def _():
        yc_own[...] = yo_acc[...].astype(BF)
        yc_oth[...] = yt_acc[...].astype(BF)
        rc_own[...] = ro_acc[...].astype(BF)
        rc_oth0[...] = rt_acc[0].astype(BF)
        rc_oth1[...] = rt_acc[1].astype(BF)


def mixture(rows_own, rows_oth, grad_own, grad_oth, place_rows, place_own, place_oth, gates,
            weights, in_bias, out_bias, capp, devices):
    micro, half, width = grad_own.shape
    experts, _, ff = in_bias.shape
    steps = ff // FF_BLOCK
    blocks = experts * steps
    slots = micro * capp
    w_block = (width, FF_BLOCK)
    group = (micro, half, width)
    dots = (micro, 8, half)
    flat = (half, width)
    (shape,) = grad_shapes(devices, width, experts * ff, False)
    return call(
        functools.partial(moe_kernel, capp),
        (experts, steps),
        [
            whole(flat), whole(flat), whole(flat), whole(flat), whole(group), whole(group),
            whole(place_rows.shape), whole(place_own.shape), whole(place_oth.shape),
            whole(gates.shape),
            pl.BlockSpec(w_block, lambda e, c: (0, e * steps + c)),
            pl.BlockSpec(w_block, lambda e, c: (0, blocks + e * steps + c)),
            pl.BlockSpec((1, 1, FF_BLOCK), lambda e, c: (e, 0, c)),
            pl.BlockSpec((1, 1, width), lambda e, c: (e, 0, 0)),
        ],
        [
            whole(group), whole(group), whole(group), whole(flat), whole(flat),
            whole(dots), whole(dots),
            grad_block(shape, FF_BLOCK, lambda e, c: e * steps + c),
            pl.BlockSpec((1, 1, FF_BLOCK), lambda e, c: (e, 0, c)),
            pl.BlockSpec((1, 1, width), lambda e, c: (e, 0, 0)),
        ],
        [
            jax.ShapeDtypeStruct(group, BF), jax.ShapeDtypeStruct(group, BF),
            jax.ShapeDtypeStruct(group, BF), jax.ShapeDtypeStruct(flat, BF),
            jax.ShapeDtypeStruct(flat, BF),
            jax.ShapeDtypeStruct(dots, F32), jax.ShapeDtypeStruct(dots, F32),
            jax.ShapeDtypeStruct(shape, BF),
            jax.ShapeDtypeStruct((experts, 1, ff), F32),
            jax.ShapeDtypeStruct((experts, 1, width), F32),
        ],
        [
            pltpu.VMEM((slots, width), BF), pltpu.VMEM((slots, width), BF),
            pltpu.VMEM((slots, width), BF), pltpu.VMEM((slots, 128), F32),
            pltpu.VMEM((slots, width), F32), pltpu.VMEM((slots, width), F32),
            pltpu.VMEM(group, F32), pltpu.VMEM(group, F32),
            pltpu.VMEM(group, F32), pltpu.VMEM(group, F32),
        ],
        12.0 * slots * experts * width * ff + 16.0 * experts * micro * capp * half * width,
        60.0e6, "experts",
    )(*rows_own, *rows_oth, grad_own, grad_oth, place_rows, place_own, place_oth, gates,
      weights, weights, in_bias, out_bias)


def gate_bwd_kernel(
    a_ref, og_ref, held_ref, ro_ref, rr_ref, do_ref, dr_ref, gp_ref, rt_ref, g_ref, b_ref,
    sent_ref, da_ref, drt_ref, dg_ref, db_ref,
):
    after = a_ref[...]
    incoming = og_ref[0].astype(F32)
    sent_ref[...] = held_ref[...]
    gates = gp_ref[...]
    found = do_ref[0] + dr_ref[0]
    spread = jnp.where(
        lax.broadcasted_iota(jnp.int32, (found.shape[0], gates.shape[1]), 0)
        == lax.broadcasted_iota(jnp.int32, (found.shape[0], gates.shape[1]), 1),
        1.0, 0.0,
    )
    gate_grad = lax.dot_general(
        found, spread, (((0,), (0,)), ((), ())), precision=EXACT, preferred_element_type=F32
    )
    logit_grad = gates * (gate_grad - jnp.sum(gates * gate_grad, axis=-1, keepdims=True))
    unit, scale = norm_parts(after)
    normed = unit * g_ref[...] + b_ref[...]
    drt_ref[...] = lax.dot_general(
        logit_grad, normed, (((0,), (0,)), ((), ())), precision=EXACT, preferred_element_type=F32
    )
    normed_grad = ro_ref[0].astype(F32) + rr_ref[...].astype(F32)
    normed_grad += lax.dot_general(
        logit_grad, rt_ref[...], (((1,), (1,)), ((), ())), precision=EXACT,
        preferred_element_type=F32,
    )
    hidden_grad, gain_grad, shift_grad = norm_pull(unit, scale, g_ref[...], normed_grad)
    da_ref[...] = incoming + hidden_grad
    dg_ref[...] = gain_grad
    db_ref[...] = shift_grad


def gate_back(after, incoming, held, r_own, r_got, d_own, d_got, gates, router, gain, shift,
              which, behind=()):
    block, width = after.shape
    lanes = gates.shape[1]
    one = pl.BlockSpec((1, block, width), lambda *_: (which, 0, 0))
    dots = pl.BlockSpec((1, 8, block), lambda *_: (which, 0, 0))
    flat = whole((block, width))
    low = whole((block, lanes))
    return call(
        gate_bwd_kernel, (1,),
        [
            flat, one, whole(held.shape), one, flat, dots, dots, low,
            whole((width, lanes)), whole((1, width)), whole((1, width)),
        ],
        [whole(held.shape), flat, whole((lanes, width)), whole((1, width)), whole((1, width))],
        [
            jax.ShapeDtypeStruct(held.shape, BF),
            jax.ShapeDtypeStruct((block, width), F32),
            jax.ShapeDtypeStruct((lanes, width), F32),
            jax.ShapeDtypeStruct((1, width), F32),
            jax.ShapeDtypeStruct((1, width), F32),
        ],
        [], 4.0 * block * width * lanes, 7.0e6, "gate_bwd", behind,
    )(after, incoming, held, r_own, r_got, d_own, d_got, gates, router, gain, shift)


def swap(value):
    return lax.ppermute(value, "tensor", [(0, 1), (1, 0)])


def in_order(mine, other, axis):
    first = lax.axis_index("tensor") == 0
    return jnp.stack([jnp.where(first, mine, other), jnp.where(first, other, mine)], axis=axis)


def gather_rows(share):
    return lax.all_gather(share, "dp", axis=0, tiled=True)


def chip_ring(chips):
    if chips == 8:
        return [0, 2, 4, 6, 7, 5, 3, 1]
    return list(range(chips))


def ring_add_kernel(kind, at_ref, *refs):
    def chunk(grads, given):
        return grads[0].astype(F32) + given[0].astype(F32)

    if kind == 0:
        grads, given, ahead, behind = refs
        total = chunk(grads, given).astype(BF)
        ahead[...] = total[0]
        behind[...] = total[1]
    elif kind == 3:
        grads, given, got_a, got_b, out = refs
        out[...] = chunk(grads, given) + (got_a[...].astype(F32) + got_b[...].astype(F32))
    else:
        grads_a, given_a, grads_b, given_b, got_a, got_b, ahead, behind = refs
        one, two = chunk(grads_a, given_a), chunk(grads_b, given_b)
        if kind == 1:
            ahead[0] = (one[0] + got_a[...].astype(F32)).astype(BF)
            ahead[1] = one[1].astype(BF)
            behind[0] = two[0].astype(BF)
            behind[1] = (two[1] + got_b[...].astype(F32)).astype(BF)
        else:
            ahead[...] = (one + got_a[...].astype(F32)).astype(BF)
            behind[...] = (two + got_b[...].astype(F32)).astype(BF)


class RingSum:
    def __init__(self, kept, sent):
        count = lax.axis_size("dp")
        self.chips = count // 2
        self.ring = chip_ring(self.chips)
        position = [self.ring.index(chip) for chip in range(self.chips)]
        self.here = jnp.array(position, jnp.int32)[lax.axis_index("dp") // 2]
        self.kept = kept
        self.away = self.chips // 2
        self.messages = (sent,)
        self.given = lax.ppermute(sent, "dp", [(at, at ^ 1) for at in range(count)])
        self.got = ()
        self.result = None

    def send(self, value, step):
        pairs = [
            (self.ring[at] * 2 + side, self.ring[(at + step) % self.chips] * 2 + side)
            for at in range(self.chips)
            for side in range(2)
        ]
        return lax.ppermute(value, "dp", pairs)

    def step(self, after=()):
        if self.result is not None:
            return
        table = jnp.array(self.ring, jnp.int32)
        away = self.away
        chips = [table[(self.here + away) % self.chips], table[(self.here - away) % self.chips]]
        places = jnp.stack(chips).astype(jnp.int32)
        shape = self.kept.shape[1:]

        def chunk_specs(which):
            return [
                pl.BlockSpec((1,) + shape, lambda _, at: (at[which], 0, 0, 0)),
                pl.BlockSpec((1,) + shape, lambda _, at: (at[which], 0, 0, 0)),
            ]

        far = self.chips // 2
        kind = 3 if away == 0 else 0 if away == far else 1 if away == far - 1 else 2
        two_ways = kind in (1, 2)
        in_specs = chunk_specs(0) + (chunk_specs(1) if two_ways else [])
        args = [self.kept, self.given] * (2 if two_ways else 1) + list(self.got)
        in_specs += [whole(got.shape) for got in self.got]
        out = shape if kind else shape[1:]
        kinds = [jax.ShapeDtypeStruct(out, F32 if kind == 3 else BF)] * (1 if kind == 3 else 2)
        sums = call(
            functools.partial(ring_add_kernel, kind), (1,), in_specs,
            [whole(out)] * len(kinds), kinds, [], 0, 1.0e6, "ring_add", after, prefetch=1,
        )(places, *args)
        self.away -= 1
        if kind == 3:
            self.result = sums[0]
            self.messages = ()
            return
        self.messages = tuple(sums)
        self.got = (self.send(sums[0], 1), self.send(sums[1], -1))


class PlainSum:
    def __init__(self, grad):
        axis = 1 if grad.ndim == 3 else 0
        done = lax.psum_scatter(grad, "dp", scatter_dimension=axis, tiled=True)
        self.messages = (done,)
        self.result = done.reshape((2,) + done.shape[-2:]).astype(F32)

    def step(self, after=()):
        return


def add_kernel(one_ref, two_ref, out_ref):
    out_ref[...] = one_ref[...] + two_ref[...]


class PairSum:
    def __init__(self, value):
        self.count = lax.axis_size("dp")
        self.value = value
        self.stage = 1
        self.send()

    def send(self):
        self.messages = (self.value,)
        if self.stage < self.count:
            pairs = [(at, at ^ self.stage) for at in range(self.count)]
            self.got = lax.ppermute(self.value, "dp", pairs)
        elif self.stage == self.count:
            self.got = swap(self.value)
        else:
            self.got = None
            self.messages = ()
        self.stage *= 2

    def step(self, after=()):
        if self.got is None:
            return
        shape = self.value.shape
        (self.value,) = call(
            add_kernel, (1,), [whole(shape)] * 2, [whole(shape)],
            [jax.ShapeDtypeStruct(shape, F32)], [], 0, 3.0e5, "small_add", after,
        )(self.value, self.got)
        self.send()


def pack_kernel(plan, side_ref, *refs):
    out_ref = refs[-1]
    width = out_ref.shape[1]
    out_ref[...] = jnp.zeros_like(out_ref)
    at = 0
    for inputs, rows, factor, sided in plan:
        total = None
        for which in inputs:
            ref = refs[which]
            value = ref[...].reshape(-1, ref.shape[-1])[:rows]
            total = value if total is None else total + value
        total = total * factor if factor != 1.0 else total
        parts = total.shape[1] // width
        for row in range(rows):
            for part in range(parts):
                piece = total[row : row + 1, part * width : (part + 1) * width]
                place = at + row * parts + part
                if sided:
                    place = place + side_ref[0] * (rows * parts)
                out_ref[pl.ds(place, 1), :] = piece
        at += rows * parts * (2 if sided else 1)


def pack_rows(groups, width):
    arrays, plan, total = [], [], 0
    for values, rows, factor, sided in groups:
        plan.append((tuple(range(len(arrays), len(arrays) + len(values))), rows, factor, sided))
        arrays += values
        total += rows * (values[0].shape[-1] // width) * (2 if sided else 1)
    shape = (round_up(total, 8), width)
    side = lax.axis_index("tensor").reshape(1)
    (out,) = call(
        functools.partial(pack_kernel, tuple(plan)), (1,),
        [whole(value.shape) for value in arrays], [whole(shape)],
        [jax.ShapeDtypeStruct(shape, F32)], [], 0, 3.0e5, "pack", (), prefetch=1,
    )(side, *arrays)
    return out


def out_kernel(a0_ref, a1_ref, y_ref, got_ref, out_ref):
    for m, a_ref in enumerate((a0_ref, a1_ref)):
        total = a_ref[...] + (y_ref[m].astype(F32) + got_ref[m].astype(F32))
        out_ref[m] = total.astype(BF)


def layer_output(hidden, y_own, y_got, after):
    shape = y_own.shape
    (out,) = call(
        out_kernel, (1,),
        [whole(hidden[0].shape)] * 2 + [whole(shape)] * 2, [whole(shape)],
        [jax.ShapeDtypeStruct(shape, BF)], [], 0, 8.0e6, "layer_output", after,
    )(*hidden, y_own, y_got)
    return out


def place_kernel(side_ref, own_ref, got_ref, out_ref):
    images, length = own_ref.shape[1], out_ref.shape[2]
    side = side_ref[0]
    for image in range(images):
        kept = own_ref[:, image, :length, :].astype(out_ref.dtype)
        out_ref[:, side * images + image] = kept
        other = got_ref[:, image, :length, :].astype(out_ref.dtype)
        out_ref[:, (1 - side) * images + image] = other


def place_images(own, got, shape, kind, after):
    micro, images, length, width = shape
    padded = (micro, images // 2, own.size // (micro * (images // 2) * width), width)
    side = lax.axis_index("tensor").reshape(1)
    (out,) = call(
        place_kernel, (micro,),
        [pl.BlockSpec((1,) + padded[1:], lambda m, *_: (m, 0, 0, 0))] * 2,
        [pl.BlockSpec((1,) + shape[1:], lambda m, *_: (m, 0, 0, 0))],
        [jax.ShapeDtypeStruct(shape, kind)], [], 0, 8.0e6, "place", after, prefetch=1,
    )(side, own.reshape(padded), got.reshape(padded))
    return out


def join_sides(mine_first):
    mine = lax.axis_index("tensor")
    kept = lax.dynamic_index_in_dim(mine_first, mine, 0, keepdims=False)
    sent = lax.dynamic_index_in_dim(mine_first, 1 - mine, 0, keepdims=False)
    return kept + swap(sent)


def own_half(value, axis):
    size = value.shape[axis] // 2
    return lax.dynamic_slice_in_dim(value, lax.axis_index("tensor") * size, size, axis)


def local(
    block_input, norm_gain, row_bias, qkv_weight, qkv_bias, out_weight, mlp_in, mlp_in_bias,
    mlp_out, mlp_out_bias, router, expert_in, expert_in_bias, expert_out, expert_out_bias,
    routes, slot_index, out_grad,
):
    micro, images, length, width = block_input.shape
    experts = router.shape[1]
    share_rows = mlp_in.shape[0]
    own_images = images // 2
    pad = round_up(length, ROW_PAD)
    half = own_images * pad
    rows = micro * half
    capp = round_up(CAP, ROW_PAD)
    side = lax.axis_index("tensor")

    def attn_share(layer):
        return jnp.concatenate(
            [qkv_weight[layer].reshape(share_rows, -1), out_weight[layer]], axis=1
        )

    devices = lax.axis_size("dp")
    first_mine = jnp.concatenate([attn_share(0), attn_share(1), mlp_in, mlp_out], axis=1)
    first_w = lax.all_gather(
        in_order(first_mine, swap(first_mine), 0), "dp", axis=0, tiled=False
    )
    if not whole_tiles(devices, width):
        first_w = jnp.moveaxis(first_w, 0, 1).reshape(1, 2, width, -1)
    dense_at = 4 * width
    expert_w = gather_rows(
        jnp.concatenate(
            [expert_in.reshape(share_rows, -1), expert_out.reshape(share_rows, -1)], axis=1
        )
    )

    biases = jnp.concatenate([qkv_bias.reshape(-1), mlp_in_bias])
    bias_pair = in_order(biases, swap(biases), 0)
    qkv_bias_pair = bias_pair[:, : qkv_bias.size].reshape((2,) + qkv_bias.shape)
    mlp_bias_full = bias_pair[:, qkv_bias.size :].reshape(1, -1)

    def qkv_bias_row(layer):
        pair = qkv_bias_pair[:, layer]
        zero = jnp.zeros_like(pair[:, 0])
        return jnp.concatenate([pair[:, 0], zero, pair[:, 1]], axis=1).reshape(1, -1)

    def padded(value, start):
        part = lax.dynamic_slice_in_dim(value, start, own_images, 1)
        return jnp.pad(part, ((0, 0), (0, 0), (0, pad - length), (0, 0)))

    mine_at = side * own_images
    other_at = (1 - side) * own_images
    hidden = padded(block_input, mine_at).astype(F32).reshape(rows, width)
    grad_own = padded(out_grad, mine_at).reshape(micro, half, width)
    grad_oth = padded(out_grad, other_at).reshape(micro, half, width)

    kept = slot_index < CAP
    place = jnp.where(kept, routes * capp + slot_index, -1)
    pick = jnp.where(kept, routes, -1)

    def lay(value, start):
        part = lax.dynamic_slice_in_dim(value, start, own_images, 1)
        part = jnp.pad(
            part, ((0, 0), (0, 0), (0, pad - length), (0, 0)), constant_values=-1
        )
        return part.reshape(micro, half, 2)

    place_own, place_oth = lay(place, mine_at), lay(place, other_at)
    place_rows = jnp.concatenate(
        [jnp.swapaxes(place_own, 1, 2), jnp.swapaxes(place_oth, 1, 2)], axis=1
    )
    select = lay(pick, mine_at).reshape(rows, 2)
    router_wide = jnp.pad(router, ((0, 0), (0, 128 - experts)))

    def row(vector):
        return vector.reshape(1, -1)

    qkv_one, lse_one, mix_one, after_one = attention_forward(
        hidden, row(norm_gain[0, 0]), row(row_bias[0, 0]), first_w, 0, qkv_bias_row(0),
        row(row_bias[0, 2]), length, pad, 0, micro,
    )
    after_ffn = dense_forward(
        after_one, row(norm_gain[0, 1]), row(row_bias[0, 1]), first_w, dense_at, mlp_bias_full,
        row(mlp_out_bias),
    )
    second = [
        attention_forward(
            after_ffn, row(norm_gain[1, 0]), row(row_bias[1, 0]), first_w, 1, qkv_bias_row(1),
            row(row_bias[1, 2]), length, pad, m, 1,
            (row(norm_gain[1, 1]), row(row_bias[1, 1]), router_wide, select, experts),
        )
        for m in range(micro)
    ]
    qkv_two, lse_two, mix_two, after_two, rows_own, gates, chosen = zip(*second)
    rows_oth = [swap(part) for part in rows_own]
    gate_own = jnp.stack([part[:, :2].T for part in chosen])
    gate_pair = jnp.concatenate([gate_own, swap(gate_own)], axis=1)
    ring = whole_tiles(devices, width)
    core = (lax.axis_index("dp") % 2).reshape(1)
    (
        y_own, y_oth, r_own, r_oth0, r_oth1, d_own, d_oth, expert_grad, ein_bias, eout_bias,
    ) = mixture(
        rows_own, rows_oth, grad_own, grad_oth, place_rows, place_own, place_oth, gate_pair,
        expert_w, expert_in_bias.reshape(experts, 1, -1),
        expert_out_bias.reshape(experts, 1, -1), capp, devices,
    )
    d_got = swap(d_oth)
    r_got = swap(r_oth0)
    expert_sum = PlainSum(expert_grad)
    grad_two, gate_parts, cores = [], [], []
    for m, held in enumerate((r_oth1, y_oth)):
        sent, grad_part, *small = gate_back(
            after_two[m], grad_own, held, r_own, r_got, d_own, d_got, gates[m],
            router_wide, row(norm_gain[1, 1]), row(row_bias[1, 1]), m,
            (cores[0][1],) if m else (),
        )
        r_got = swap(sent)
        grad_two.append(grad_part)
        gate_parts.append(small)
        cores.append(
            attention_core_back(
                grad_part, first_w, 1, (qkv_two[m], lse_two[m], half), length, pad, m, (sent,)
            )
        )
    y_got = r_got
    router_parts, gain_parts, shift_parts = (list(pair) for pair in zip(*gate_parts))
    two_grad, (grad_ffn, qb_two, ob_two, gain_two, shift_two) = attention_grad(
        core, grad_two, after_ffn, row(norm_gain[1, 0]), row(row_bias[1, 0]), first_w, 1, cores,
        mix_two, devices, ring, F32,
    )
    sum_two = RingSum(*two_grad) if ring else PlainSum(*two_grad)
    early_sum = PairSum(
        pack_rows(
            [
                ([gain_two], 1, 1.0, False), (gain_parts, 1, 1.0, False),
                ([shift_two], 1, 1.0, False), (shift_parts, 1, 1.0, False),
                ([ob_two], 1, 1.0, False), ([qb_two], 1, 1.0, False),
                (router_parts, experts, 1.0, False), ([eout_bias], experts, 0.5, False),
                ([ein_bias], experts, 1.0, True),
            ],
            width,
        )
    )
    dense_grad, (grad_one, in_bias_grad, out_bias_grad, gain_ffn, shift_ffn) = dense_back(
        core, grad_ffn, after_one, row(norm_gain[0, 1]), row(row_bias[0, 1]), first_w, dense_at,
        mlp_bias_full, devices, ring, sum_two.messages + early_sum.messages + (sent,),
    )
    done = (gain_ffn,)
    sum_two.step(done)
    early_sum.step(done)
    dense_sum = RingSum(*dense_grad) if ring else PlainSum(*dense_grad)
    out_own = layer_output(after_two, y_own, y_got, done)
    out_got = swap(out_own)
    chains = (sum_two, dense_sum, early_sum)

    def flying():
        return sum_two.messages + dense_sum.messages + early_sum.messages

    cores = []
    for which in range(2):
        cores.append(
            attention_core_back(
                grad_one, first_w, 0, (qkv_one, lse_one, half), length, pad, which,
                flying() + (out_own,),
            )
        )
        for chain in chains:
            chain.step((cores[-1][1],))
    block_output = place_images(out_own, out_got, block_input.shape, BF, (cores[-1][1],))
    one_grad, (grad_zero, qb_one, ob_one, gain_one, shift_one) = attention_grad(
        core, (grad_one, grad_one), hidden, row(norm_gain[0, 0]), row(row_bias[0, 0]), first_w,
        0, cores, (mix_one, mix_one), devices, ring, BF, flying(),
    )
    one_sum = RingSum(*one_grad) if ring else PlainSum(*one_grad)
    grad_got = swap(grad_zero)
    late_sum = PairSum(
        pack_rows(
            [
                ([gain_one], 1, 1.0, False), ([gain_ffn], 1, 1.0, False),
                ([shift_one], 1, 1.0, False), ([shift_ffn], 1, 1.0, False),
                ([ob_one], 1, 1.0, False), ([qb_one], 1, 1.0, False),
                ([in_bias_grad], 1, 1.0, False), ([out_bias_grad], 1, 1.0, False),
            ],
            width,
        )
    )
    last = (qb_one,)
    queue = [sum_two, one_sum]
    for _ in range(devices):
        queue += [dense_sum, sum_two, early_sum, late_sum, one_sum]
    for chain in queue:
        chain.step(last)
        if chain.messages:
            last = chain.messages
    input_grad = place_images(grad_zero, grad_got, block_input.shape, F32, last)

    expert_grads = expert_sum.result.reshape(2, share_rows, experts, -1)
    attn_grads = [join_sides(one_sum.result), join_sides(sum_two.result)]
    dense_done = join_sides(
        jnp.moveaxis(dense_sum.result.reshape(2, share_rows, 2, -1), 2, 0)
    )
    split_at = 3 * width // 2

    late, early = late_sum.value, early_sum.value
    gain_sum = jnp.concatenate([late[0:2], early[0:2]])
    shift_sum = jnp.concatenate([late[2:5], early[2:5]])
    qb_sum = jnp.stack([late[5:8], early[5:8]]).reshape(2, 2, 3, width // 2)
    qb_sum = lax.dynamic_index_in_dim(qb_sum, side, 1, keepdims=False)
    ff_rows = in_bias_grad.shape[1] // width
    in_bias_sum = late[8 : 8 + ff_rows]
    out_bias_sum = late[8 + ff_rows]
    at = 8 + experts
    router_sum = early[8:at]
    eout_sum = early[at : at + experts]
    at += experts
    ein_rows = expert_in_bias.size // width
    ein_sum = lax.dynamic_slice_in_dim(early, at + side * ein_rows, ein_rows, 0)
    return (
        block_output,
        input_grad,
        gain_sum.reshape(norm_gain.shape),
        shift_sum.reshape(row_bias.shape),
        jnp.stack([part[:, :split_at] for part in attn_grads]).reshape(qkv_weight.shape),
        jnp.stack([qb_sum[:, 0], qb_sum[:, 2]], axis=1),
        jnp.stack([part[:, split_at:] for part in attn_grads]),
        dense_done[0],
        own_half(in_bias_sum.reshape(-1), 0),
        dense_done[1],
        out_bias_sum.reshape(-1),
        router_sum.T,
        expert_grads[0],
        ein_sum.reshape(expert_in_bias.shape),
        expert_grads[1],
        eout_sum.reshape(experts, width),
    )


def solution(mesh):
    return jax.shard_map(
        local,
        mesh=mesh,
        in_specs=(
            P(None, "dp", None, None), P(), P(), P(None, "dp", None, "tensor"),
            P(None, None, "tensor"), P(None, "dp", "tensor"), P("dp", "tensor"), P("tensor"),
            P("dp", "tensor"), P(), P(), P("dp", None, "tensor"), P(None, "tensor"),
            P("dp", None, "tensor"), P(), P(None, "dp", None, None), P(None, "dp", None, None),
            P(None, "dp", None, None),
        ),
        out_specs=(
            P(None, "dp", None, None), P(None, "dp", None, None), P(), P(),
            P(None, "dp", None, "tensor"), P(None, None, "tensor"), P(None, "dp", "tensor"),
            P("dp", "tensor"), P("tensor"), P("dp", "tensor"), P(), P(),
            P("dp", None, "tensor"), P(None, "tensor"), P("dp", None, "tensor"), P(),
        ),
        check_vma=False,
    )
```

```python
import functools

import jax
import jax.numpy as jnp
from jax import lax
from jax.experimental import pallas as pl
from jax.experimental.pallas import tpu as pltpu
from jax.sharding import PartitionSpec as P

HD = 64
CAP = 295
NORM_EPS = 1e-06
EXACT = lax.Precision.HIGHEST
BF = jnp.bfloat16
F32 = jnp.float32
VMEM_LIMIT = 58 * 1024 * 1024
FF_BLOCK = 512
EXPERT_BLOCK = 768
ROW_PAD = 16
GELU_SLOPE = 0.7978845608028654
GELU_CUBE = 0.044715


def round_up(value, unit):
    return -(-value // unit) * unit


def mm(left, right):
    return jnp.dot(left, right, preferred_element_type=F32)


def mm_bt(left, right):
    return lax.dot_general(left, right, (((1,), (1,)), ((), ())), preferred_element_type=F32)


def mm_at(left, right):
    return lax.dot_general(left, right, (((0,), (0,)), ((), ())), preferred_element_type=F32)


def norm_parts(hidden):
    center = jnp.mean(hidden, axis=-1, keepdims=True)
    centred = hidden - center
    spread = jnp.mean(centred * centred, axis=-1, keepdims=True)
    scale = lax.rsqrt(spread + NORM_EPS)
    return centred * scale, scale


def norm_pull(unit, scale, gain, incoming):
    wide = incoming * gain
    mean_wide = jnp.mean(wide, axis=-1, keepdims=True)
    mean_dot = jnp.mean(wide * unit, axis=-1, keepdims=True)
    hidden_grad = scale * (wide - mean_wide - unit * mean_dot)
    gain_grad = jnp.sum(incoming * unit, axis=0, keepdims=True)
    shift_grad = jnp.sum(incoming, axis=0, keepdims=True)
    return hidden_grad, gain_grad, shift_grad


def gelu_pair(preact):
    square = preact * preact
    inner = GELU_SLOPE * preact * (1.0 + GELU_CUBE * square)
    bend = jnp.tanh(inner)
    half = 0.5 * (1.0 + bend)
    active = preact * half
    slope = half + 0.5 * preact * (1.0 - bend * bend) * (
        GELU_SLOPE * (1.0 + 3.0 * GELU_CUBE * square)
    )
    return active, slope


def gelu_value(preact):
    square = preact * preact
    inner = GELU_SLOPE * preact * (1.0 + GELU_CUBE * square)
    return 0.5 * preact * (1.0 + jnp.tanh(inner))


def call(kernel, grid, in_specs, out_specs, out_shape, scratch, flops, traffic, name,
         after=(), prefetch=0, aliases=None):
    taken = prefetch + len(in_specs)
    skipped = len(after)

    def body(*refs):
        kernel(*refs[:taken], *refs[taken + skipped :])

    made = pl.pallas_call(
        body,
        grid_spec=pltpu.PrefetchScalarGridSpec(
            num_scalar_prefetch=prefetch,
            grid=grid,
            in_specs=list(in_specs) + [pl.BlockSpec(memory_space=pl.ANY)] * skipped,
            out_specs=out_specs,
            scratch_shapes=scratch,
        ),
        out_shape=out_shape,
        input_output_aliases=aliases or {},
        name=name,
        compiler_params=pltpu.CompilerParams(
            vmem_limit_bytes=VMEM_LIMIT,
            dimension_semantics=("arbitrary",) * len(grid),
        ),
        cost_estimate=pl.CostEstimate(
            flops=int(flops), bytes_accessed=int(traffic), transcendentals=0
        ),
    )
    return lambda *args: made(*args, *after)


def whole_tiles(devices, width):
    return (width // devices) % ROW_PAD == 0


def grad_shapes(devices, width, columns, split):
    if not whole_tiles(devices, width):
        return [(2, width, columns)]
    if split:
        return [(devices // 2, 2, width // devices, columns)] * 2
    return [(devices, 2, width // devices, columns)]


def grad_block(shape, columns, index):
    block = shape[:-1] + (columns,)
    zeros = (0,) * (len(shape) - 1)
    return pl.BlockSpec(block, lambda *at: zeros + (index(*at),))


def put_grad(refs, core_ref, part, cols, value):
    ref = refs[0]
    if len(refs) == 2:
        pieces = value.reshape(ref.shape[0], 2, ref.shape[2], value.shape[1])
        core = core_ref[0]

        @pl.when(core == 0)
        def _():
            refs[0][:, part, :, cols] = pieces[:, 0]
            refs[1][:, part, :, cols] = pieces[:, 1]

        @pl.when(core != 0)
        def _():
            refs[0][:, part, :, cols] = pieces[:, 1]
            refs[1][:, part, :, cols] = pieces[:, 0]
    elif len(ref.shape) == 3:
        ref[part, :, cols] = value
    else:
        ref[:, part, :, cols] = value.reshape(ref.shape[0], ref.shape[2], value.shape[1])


def flat_rows(value):
    return value.reshape(-1, value.shape[-1])


def weight_spec(weights, sides, columns, index):
    devices, _, rows, _ = weights.shape
    return pl.BlockSpec(
        (devices, sides, rows, columns), index, pipeline_mode=pl.Buffered(1)
    )


def whole(shape):
    zeros = (0,) * len(shape)
    return pl.BlockSpec(shape, lambda *_: zeros, pipeline_mode=pl.Buffered(1))


def rows_of(block, width):
    return pl.BlockSpec((block, width), lambda step, *_: (step, 0))


def half_of(value, block, which):
    at = which if value.shape[0] > block else 0
    rest = (0,) * (value.ndim - 1)
    return pl.BlockSpec((block,) + value.shape[1:], lambda *_: (at,) + rest)


def attn_fwd_kernel(
    length, pad, heads, router_on,
    h_ref, g_ref, b_ref, w_ref, qb_ref, ob_ref, *rest,
):
    if router_on:
        g2_ref, b2_ref, rt_ref, sel_ref = rest[:4]
        qkv_ref, lse_ref, o_ref, a_ref, rb_ref, gp_ref, wt_ref = rest[4:]
    else:
        qkv_ref, lse_ref, o_ref, a_ref = rest
    width = h_ref.shape[1]
    images = h_ref.shape[0] // pad
    hidden = h_ref[...]
    unit, _ = norm_parts(hidden)
    normed = (unit * g_ref[...] + b_ref[...]).astype(BF)
    third = width // 2
    for t in range(2):
        cols = slice(t * 3 * third, (t + 1) * 3 * third)
        matrix = flat_rows(w_ref[:, t, :, : 3 * third])
        qkv_ref[:, cols] = (mm(normed, matrix) + qb_ref[:, cols]).astype(BF)
    pairs = heads // 2
    lane = lax.broadcasted_iota(jnp.int32, (pad, 2 * HD), 1)
    key_row = lax.broadcasted_iota(jnp.int32, (pad, pad), 0)

    def pair_step(step, carry):
        image = step // pairs
        pair = step % pairs
        rows = pl.ds(pl.multiple_of(image * pad, ROW_PAD), pad)

        def col(part):
            side = pair // (pairs // 2)
            at = (side * 3 + part) * (width // 2) + (pair % (pairs // 2)) * 2 * HD
            return pl.ds(pl.multiple_of(at, 2 * HD), 2 * HD)

        place = pl.ds(pl.multiple_of(pair * 2 * HD, 2 * HD), 2 * HD)

        query = qkv_ref[rows, col(0)] * HD ** (-0.5)
        key = qkv_ref[rows, col(1)]
        value = qkv_ref[rows, col(2)]
        mixed = []
        for half in range(2):
            mine = (lane >= HD) if half else (lane < HD)
            scores = mm_bt(key, jnp.where(mine, query, 0).astype(BF))
            scores = jnp.where(key_row < length, scores, -1e30)
            top = jnp.max(scores, axis=0, keepdims=True)
            weights = jnp.exp(scores - top)
            total = jnp.sum(weights, axis=0, keepdims=True)
            probs = (weights * (1.0 / total)).astype(BF)
            mixed.append(mm_at(probs, value))
            lse_ref[image, pl.ds(pair * 2 + half, 1), :] = top + jnp.log(total)
        o_ref[rows, place] = jnp.where(lane < HD, mixed[0], mixed[1]).astype(BF)
        return carry

    lax.fori_loop(0, images * pairs, pair_step, 0, unroll=6)
    out_matrix = jnp.concatenate(
        [flat_rows(w_ref[:, t, :, 3 * third :]) for t in range(2)], axis=1
    )
    after = hidden + mm_bt(o_ref[...], out_matrix) + ob_ref[...]
    a_ref[...] = after
    if router_on:
        unit2, _ = norm_parts(after)
        normed2 = unit2 * g2_ref[...] + b2_ref[...]
        rb_ref[...] = normed2.astype(BF)
        logits = jnp.dot(normed2, rt_ref[...], precision=EXACT, preferred_element_type=F32)
        lanes = lax.broadcasted_iota(jnp.int32, logits.shape, 1)
        live = lanes < router_on
        logits = jnp.where(live, logits, -1e30)
        gates = jnp.exp(logits - jnp.max(logits, axis=-1, keepdims=True))
        gates = gates / jnp.sum(gates, axis=-1, keepdims=True)
        gates = jnp.where(live, gates, 0.0)
        gp_ref[...] = gates
        first = jnp.sum(jnp.where(lanes == sel_ref[:, 0:1], gates, 0.0), axis=-1, keepdims=True)
        second = jnp.sum(jnp.where(lanes == sel_ref[:, 1:2], gates, 0.0), axis=-1, keepdims=True)
        wt_ref[...] = jnp.where(lanes == 0, first, jnp.where(lanes == 1, second, 0.0))


def attention_forward(
    hidden, gain, shift, weights, layer, qkv_bias, out_bias, length, pad, start, count,
    router=None,
):
    micro = 2
    rows, width = hidden.shape
    heads = width // HD
    block = rows // micro
    lse_rows = round_up(heads, 8)
    images = block // pad
    made = count * block
    in_specs = [
        pl.BlockSpec((block, width), lambda step: (start + step, 0)),
        whole((1, width)), whole((1, width)),
        weight_spec(weights, 2, 2 * width, lambda *_: (0, 0, 0, layer)),
        whole((1, 3 * width)), whole((1, width)),
    ]
    args = [hidden, gain, shift, weights, qkv_bias, out_bias]
    out_specs = [
        rows_of(block, 3 * width),
        pl.BlockSpec((images, lse_rows, pad), lambda step: (step, 0, 0)),
        rows_of(block, width),
        rows_of(block, width),
    ]
    out_shape = [
        jax.ShapeDtypeStruct((made, 3 * width), BF),
        jax.ShapeDtypeStruct((count * images, lse_rows, pad), F32),
        jax.ShapeDtypeStruct((made, width), BF),
        jax.ShapeDtypeStruct((made, width), F32),
    ]
    router_on = 0
    if router is not None:
        gain2, shift2, router_wide, select, router_on = router
        lanes = router_wide.shape[1]
        in_specs += [
            whole((1, width)), whole((1, width)), whole((width, lanes)),
            pl.BlockSpec((block, 2), lambda step: (start + step, 0)),
        ]
        args += [gain2, shift2, router_wide, select]
        out_specs += [rows_of(block, width), rows_of(block, lanes), rows_of(block, lanes)]
        out_shape += [
            jax.ShapeDtypeStruct((made, width), BF),
            jax.ShapeDtypeStruct((made, lanes), F32),
            jax.ShapeDtypeStruct((made, lanes), F32),
        ]
    return call(
        functools.partial(attn_fwd_kernel, length, pad, heads, router_on),
        (count,), in_specs, out_specs, out_shape, [],
        8.0 * made * width * width + 16.0 * made * pad * width, 12.0e6, "attn_fwd",
    )(*args)


def attn_core_kernel(
    length, pad, heads, da_ref, wo_ref, qkv_ref, lse_ref, dqkv_ref, low_ref, grad_sc,
):
    width = da_ref.shape[1]
    images = da_ref.shape[0] // pad
    pairs = heads // 2
    low = da_ref[...].astype(BF)
    low_ref[...] = low
    out_matrix = jnp.concatenate([flat_rows(wo_ref[:, t]) for t in range(2)], axis=1)
    grad_sc[...] = mm(low, out_matrix).astype(BF)
    lane = lax.broadcasted_iota(jnp.int32, (pad, 2 * HD), 1)
    key_row = lax.broadcasted_iota(jnp.int32, (pad, pad), 0)

    def pair_step(step, carry):
        image = step // pairs
        pair = step % pairs
        rows = pl.ds(pl.multiple_of(image * pad, ROW_PAD), pad)

        def col(part):
            side = pair // (pairs // 2)
            at = (side * 3 + part) * (width // 2) + (pair % (pairs // 2)) * 2 * HD
            return pl.ds(pl.multiple_of(at, 2 * HD), 2 * HD)

        place = pl.ds(pl.multiple_of(pair * 2 * HD, 2 * HD), 2 * HD)

        query = (qkv_ref[rows, col(0)] * HD ** (-0.5)).astype(BF)
        key = qkv_ref[rows, col(1)]
        value = qkv_ref[rows, col(2)]
        mixed = grad_sc[rows, place]
        key_turned = key.T
        parts = []
        for half in range(2):
            mine = (lane >= HD) if half else (lane < HD)
            scores = mm_bt(key, jnp.where(mine, query, 0).astype(BF))
            total = lse_ref[image, pl.ds(pair * 2 + half, 1), :]
            probs = jnp.where(key_row < length, jnp.exp(scores - total), 0.0)
            probs_grad = mm_bt(value, jnp.where(mine, mixed, 0).astype(BF))
            product = probs * probs_grad
            delta = jnp.sum(product, axis=0, keepdims=True)
            score_grad = (product - probs * delta).astype(BF)
            parts.append((
                mm(key_turned, score_grad) * HD ** (-0.5),
                mm(score_grad, query),
                mm(probs.astype(BF), mixed),
            ))
        turned = lax.broadcasted_iota(jnp.int32, (2 * HD, pad), 0)
        query_grad = jnp.where(turned < HD, parts[0][0], parts[1][0])
        dqkv_ref[rows, col(0)] = query_grad.T.astype(BF)
        for part in range(1, 3):
            dqkv_ref[rows, col(part)] = jnp.where(
                lane < HD, parts[0][part], parts[1][part]
            ).astype(BF)
        return carry

    lax.fori_loop(0, images * pairs, pair_step, 0, unroll=6)


def attention_core_back(incoming, weights, layer, stored, length, pad, which, after=()):
    qkv, lse, block = stored
    width = incoming.shape[1]
    heads = width // HD
    images = block // pad
    return call(
        functools.partial(attn_core_kernel, length, pad, heads),
        (1,),
        [
            half_of(incoming, block, which),
            weight_spec(weights, 2, width // 2, lambda *_: (0, 0, 0, 4 * layer + 3)),
            half_of(qkv, block, which),
            half_of(lse, images, which),
        ],
        [whole((block, 3 * width)), whole((block, width))],
        [
            jax.ShapeDtypeStruct((block, 3 * width), BF),
            jax.ShapeDtypeStruct((block, width), BF),
        ],
        [pltpu.VMEM((block, width), BF)],
        2.0 * block * width * width + 20.0 * block * pad * width * 4, 8.0e6, "attn_core",
        after,
    )(incoming, weights, qkv, lse)


def attn_grad_kernel(
    core_ref, da0_ref, da1_ref, h_ref, g_ref, b_ref, w_ref, dq0_ref, dq1_ref,
    low0_ref, low1_ref, o0_ref, o1_ref, *rest,
):
    dw_refs = rest[: len(rest) - 7]
    dh_ref, dqb_ref, dob_ref, dg_ref, db_ref, n_sc, acc = rest[len(rest) - 7 :]
    step = pl.program_id(0)
    block = dq0_ref.shape[0]
    wide = dq0_ref.shape[1]
    gain = g_ref[...]
    half = (slice(0, block), slice(block, 2 * block))

    @pl.when(step == 0)
    def _():
        unit, _ = norm_parts(h_ref[...])
        n_sc[...] = (unit * gain + b_ref[...]).astype(BF)
        acc[...] = jnp.zeros_like(acc)
        dob_ref[...] = jnp.sum(low0_ref[...].astype(F32), axis=0, keepdims=True) + jnp.sum(
            low1_ref[...].astype(F32), axis=0, keepdims=True
        )

    matrix = flat_rows(w_ref[:, 0, :, :wide])
    piece = sums = mix = None
    sides = ((dq0_ref, low0_ref, o0_ref), (dq1_ref, low1_ref, o1_ref))
    for side, (dq_ref, low_ref, o_ref) in enumerate(sides):
        grads = dq_ref[...]
        acc[half[side], :] += mm_bt(grads, matrix)
        outer = mm_at(n_sc[half[side], :], grads)
        total = jnp.sum(grads.astype(F32), axis=0, keepdims=True)
        out = mm_at(low_ref[...], o_ref[...])
        piece = outer if side == 0 else piece + outer
        sums = total if side == 0 else sums + total
        mix = out if side == 0 else mix + out
    put_grad(dw_refs, core_ref, 0, slice(0, wide), piece.astype(BF))
    put_grad(dw_refs, core_ref, 0, slice(wide, w_ref.shape[3]), mix.astype(BF))
    dqb_ref[...] = sums

    @pl.when(step == pl.num_programs(0) - 1)
    def _():
        unit, scale = norm_parts(h_ref[...])
        for side, da_ref in enumerate((da0_ref, da1_ref)):
            hidden_grad, gain_grad, shift_grad = norm_pull(
                unit[half[side]], scale[half[side]], gain, acc[half[side], :]
            )
            dh_ref[half[side], :] = (da_ref[...] + hidden_grad).astype(dh_ref.dtype)
            if side == 0:
                dg_ref[...] = gain_grad
                db_ref[...] = shift_grad
            else:
                dg_ref[...] += gain_grad
                db_ref[...] += shift_grad


def attention_grad(
    core, incoming, hidden, gain, shift, weights, layer, cores, mixed, devices, split, kind,
    after=(),
):
    rows, width = hidden.shape
    shapes = grad_shapes(devices, width, 2 * width, split)
    block = rows // 2
    short = jax.ShapeDtypeStruct((1, width), F32)
    third = width // 2

    def side_block(shape):
        if len(shape) == 3:
            return pl.BlockSpec((1,) + shape[1:], lambda t, *_: (t, 0, 0))
        return pl.BlockSpec(
            (shape[0], 1) + shape[2:], lambda t, *_: (0, t, 0, 0)
        )

    def columns_of(value, which, columns):
        at = which if value.shape[0] > block else 0
        return pl.BlockSpec((block, columns), lambda t, *_: (at, t))

    made = call(
        attn_grad_kernel, (2,),
        [
            half_of(incoming[0], block, 0), half_of(incoming[1], block, 1),
            whole((rows, width)), whole((1, width)), whole((1, width)),
            pl.BlockSpec(
                (weights.shape[0], 1, weights.shape[2], 2 * width),
                lambda t, *_: (0, t, 0, layer),
            ),
            columns_of(cores[0][0], 0, 3 * third), columns_of(cores[1][0], 0, 3 * third),
            whole((block, width)), whole((block, width)),
            columns_of(mixed[0], 0, third), columns_of(mixed[1], 1, third),
        ],
        [side_block(shape) for shape in shapes] + [
            whole((rows, width)), pl.BlockSpec((1, 3 * third), lambda t, *_: (0, t)),
            whole((1, width)), whole((1, width)), whole((1, width)),
        ],
        [jax.ShapeDtypeStruct(shape, BF) for shape in shapes] + [
            jax.ShapeDtypeStruct((rows, width), kind),
            jax.ShapeDtypeStruct((1, 3 * width), F32),
            short, short, short,
        ],
        [pltpu.VMEM((rows, width), BF), pltpu.VMEM((rows, width), F32)],
        14.0 * rows * width * width, 25.0e6, "attn_grad", after, prefetch=1,
    )(core, *incoming, hidden, gain, shift, weights, cores[0][0], cores[1][0], cores[0][1],
      cores[1][1], *mixed)
    return made[: len(shapes)], made[len(shapes) :]


def dense_fwd_kernel(a_ref, g_ref, b_ref, win_ref, wout_ref, bin_ref, bout_ref, x_ref, m_sc, acc):
    step = pl.program_id(0)

    @pl.when(step == 0)
    def _():
        unit, _ = norm_parts(a_ref[...])
        m_sc[...] = (unit * g_ref[...] + b_ref[...]).astype(BF)
        acc[...] = a_ref[...] + bout_ref[...]

    preact = mm(m_sc[...], flat_rows(win_ref[...])) + bin_ref[...]
    active = gelu_value(preact).astype(BF)
    acc[...] += mm_bt(active, flat_rows(wout_ref[...]))

    @pl.when(step == pl.num_programs(0) - 1)
    def _():
        x_ref[...] = acc[...]


def dense_specs(weights, at, ff):
    devices, _, rows, _ = weights.shape
    steps = ff // 2 // FF_BLOCK
    block = (devices, 1, rows, FF_BLOCK)
    start = at // FF_BLOCK
    return [
        pl.BlockSpec(block, lambda c, *_: (0, c // steps, 0, start + c % steps)),
        pl.BlockSpec(block, lambda c, *_: (0, c // steps, 0, start + steps + c % steps)),
        pl.BlockSpec((1, FF_BLOCK), lambda c, *_: (0, c)),
    ]


def dense_forward(hidden, gain, shift, weights, at, in_bias, out_bias):
    rows, width = hidden.shape
    ff = in_bias.shape[1]
    return call(
        dense_fwd_kernel, (ff // FF_BLOCK,),
        [whole((rows, width)), whole((1, width)), whole((1, width))]
        + dense_specs(weights, at, ff) + [whole((1, width))],
        whole((rows, width)),
        jax.ShapeDtypeStruct((rows, width), F32),
        [pltpu.VMEM((rows, width), BF), pltpu.VMEM((rows, width), F32)],
        4.0 * rows * width * ff, 15.0e6, "dense_fwd",
    )(hidden, gain, shift, weights, weights, in_bias, out_bias)


def dense_bwd_kernel(
    core_ref, dx_ref, a_ref, g_ref, b_ref, win_ref, wout_ref, bin_ref, *rest,
):
    dw_refs = rest[: len(rest) - 8]
    da_ref, dbin_ref, dbout_ref, dg_ref, db_ref, m_sc, low_sc, acc = rest[len(rest) - 8 :]
    step = pl.program_id(0)

    @pl.when(step == 0)
    def _():
        unit, _ = norm_parts(a_ref[...])
        m_sc[...] = (unit * g_ref[...] + b_ref[...]).astype(BF)
        low = dx_ref[...].astype(BF)
        low_sc[...] = low
        dbout_ref[...] = jnp.sum(low.astype(F32), axis=0, keepdims=True)
        acc[...] = jnp.zeros_like(acc)

    normed = m_sc[...]
    low = low_sc[...]
    in_matrix = flat_rows(win_ref[...])
    preact = mm(normed, in_matrix) + bin_ref[...]
    active, slope = gelu_pair(preact)
    preact_grad = (slope * mm(low, flat_rows(wout_ref[...]))).astype(BF)
    dbin_ref[...] = jnp.sum(preact_grad.astype(F32), axis=0, keepdims=True)
    every = slice(None)
    put_grad(dw_refs, core_ref, 1, every, mm_at(low, active.astype(BF)).astype(BF))
    put_grad(dw_refs, core_ref, 0, every, mm_at(normed, preact_grad).astype(BF))
    acc[...] += mm_bt(preact_grad, in_matrix)

    @pl.when(step == pl.num_programs(0) - 1)
    def _():
        unit, scale = norm_parts(a_ref[...])
        hidden_grad, gain_grad, shift_grad = norm_pull(unit, scale, g_ref[...], acc[...])
        da_ref[...] = dx_ref[...] + hidden_grad
        dg_ref[...] = gain_grad
        db_ref[...] = shift_grad


def dense_back(core, incoming, hidden, gain, shift, weights, at, in_bias, devices, split,
               after=()):
    rows, width = hidden.shape
    ff = in_bias.shape[1]
    shapes = grad_shapes(devices, width, ff, split)
    short = jax.ShapeDtypeStruct((1, width), F32)
    made = call(
        dense_bwd_kernel, (ff // FF_BLOCK,),
        [whole((rows, width)), whole((rows, width)), whole((1, width)), whole((1, width))]
        + dense_specs(weights, at, ff),
        [grad_block(shape, FF_BLOCK, lambda c, *_: c) for shape in shapes] + [
            whole((rows, width)), pl.BlockSpec((1, FF_BLOCK), lambda c, *_: (0, c)),
            whole((1, width)), whole((1, width)), whole((1, width)),
        ],
        [jax.ShapeDtypeStruct(shape, BF) for shape in shapes] + [
            jax.ShapeDtypeStruct((rows, width), F32), jax.ShapeDtypeStruct((1, ff), F32),
            short, short, short,
        ],
        [
            pltpu.VMEM((rows, width), BF), pltpu.VMEM((rows, width), BF),
            pltpu.VMEM((rows, width), F32),
        ],
        10.0 * rows * width * ff, 35.0e6, "dense_bwd", after, prefetch=1,
    )(core, incoming, hidden, gain, shift, weights, weights, in_bias)
    return made[: len(shapes)], made[len(shapes) :]


def pick_rows(place_ref, m, expert, capp):
    half = place_ref.shape[2]
    ids = lax.broadcasted_iota(jnp.int32, (capp, half), 0) + expert * capp
    return place_ref[m, 0:1, :] == ids, place_ref[m, 1:2, :] == ids


def as_pick(hit):
    return jnp.where(hit, 1.0, 0.0).astype(BF)


def spread_kernel(capp, own_ref, oth_ref, po_ref, pt_ref, out_ref):
    expert = pl.program_id(0)
    for m in range(own_ref.shape[0]):
        total = None
        for ref, place_ref in ((own_ref, po_ref), (oth_ref, pt_ref)):
            hit0, hit1 = pick_rows(place_ref, m, expert, capp)
            part = mm(as_pick(hit0 | hit1), ref[m])
            total = part if total is None else total + part
        out_ref[0, m * capp : (m + 1) * capp, :] = total.astype(BF)


def spread_rows(own, oth, place_own, place_oth, experts, capp):
    micro, half, width = own.shape
    slots = micro * capp
    (out,) = call(
        functools.partial(spread_kernel, capp), (experts,),
        [whole(own.shape), whole(oth.shape), whole(place_own.shape), whole(place_oth.shape)],
        [pl.BlockSpec((1, slots, width), lambda e: (e, 0, 0))],
        [jax.ShapeDtypeStruct((experts, slots, width), BF)],
        [], 4.0 * experts * slots * half * width, 9.0e6, "spread",
    )(own, oth, place_own, place_oth)
    return out


def moe_kernel(
    capp,
    rb_own0, rb_own1, rb_oth0, rb_oth1, og_ref, po_ref, pt_ref, w_ref,
    win_ref, wout_ref, bin_ref, bout_ref,
    y_ref, r_ref, d_ref, dw_ref, dbin_ref, dbout_ref,
    b_sc, dy_sc, w_sc, y_acc, r_acc,
):
    micro = 2
    expert = pl.program_id(0)
    chunk = pl.program_id(1)
    last_chunk = chunk == pl.num_programs(1) - 1
    rb_all = ((rb_own0, rb_oth0), (rb_own1, rb_oth1))

    @pl.when(chunk == 0)
    def _():
        for m in range(micro):
            slots = slice(m * capp, (m + 1) * capp)
            rows = gate = None
            for side, place_ref in enumerate((po_ref, pt_ref)):
                hit0, hit1 = pick_rows(place_ref, m, expert, capp)
                part = mm(as_pick(hit0 | hit1), rb_all[m][side][...])
                weight = jnp.sum(
                    jnp.where(hit0, w_ref[m, 2 * side : 2 * side + 1, :], 0.0)
                    + jnp.where(hit1, w_ref[m, 2 * side + 1 : 2 * side + 2, :], 0.0),
                    axis=-1, keepdims=True,
                )
                rows = part if side == 0 else rows + part
                gate = weight if side == 0 else gate + weight
            b_sc[slots, :] = rows.astype(BF)
            dy_sc[slots, :] = (og_ref[0, slots, :].astype(F32) * gate).astype(BF)
            w_sc[slots, :] = jnp.broadcast_to(gate, (capp, w_sc.shape[1]))

    tokens = b_sc[...]
    low = dy_sc[...]
    preact = mm(tokens, win_ref[...]) + bin_ref[0]
    active, slope = gelu_pair(preact)
    active = active.astype(BF)
    preact_grad = (slope * mm(low, wout_ref[...])).astype(BF)
    dbin_ref[0] = jnp.sum(preact_grad.astype(F32), axis=0, keepdims=True)
    result = mm_bt(active, wout_ref[...])
    rows_grad = mm_bt(preact_grad, win_ref[...])
    every = slice(None)
    put_grad((dw_ref,), None, 1, every, mm_at(low, active).astype(BF))
    put_grad((dw_ref,), None, 0, every, mm_at(tokens, preact_grad).astype(BF))

    @pl.when(chunk == 0)
    def _():
        y_acc[...] = result
        r_acc[...] = rows_grad

    @pl.when((chunk > 0) & jnp.logical_not(last_chunk))
    def _():
        y_acc[...] += result
        r_acc[...] += rows_grad

    @pl.when(last_chunk)
    def _():
        dbout_ref[0] = jnp.sum(dy_sc[...].astype(F32), axis=0, keepdims=True)
        total = y_acc[...] + result + 0.5 * bout_ref[0]
        dots = jnp.sum(og_ref[0].astype(F32) * total, axis=-1, keepdims=True)
        high = dots.astype(BF)
        rest = dots - high.astype(F32)
        mid = rest.astype(BF)
        tiny = (rest - mid.astype(F32)).astype(BF)
        lanes = lax.broadcasted_iota(jnp.int32, d_ref.shape[1:], 1)
        zero = jnp.zeros(d_ref.shape[1:], BF)
        d_ref[0] = jnp.where(
            lanes == expert, high,
            jnp.where(lanes == 8 + expert, mid, jnp.where(lanes == 16 + expert, tiny, zero)),
        )
        y_ref[0] = (w_sc[:, 0:1] * total).astype(BF)
        r_ref[0] = (r_acc[...] + rows_grad).astype(BF)


def mixture(rows_own, rows_oth, grad_rows, place_own, place_oth, gates, weights, in_bias,
            out_bias, capp, devices):
    half, width = rows_own[0].shape
    experts, slots, _ = grad_rows.shape
    ff = in_bias.shape[2]
    block = EXPERT_BLOCK
    steps = ff // block
    blocks = experts * steps
    w_block = (width, block)
    flat = (half, width)
    (shape,) = grad_shapes(devices, width, experts * ff, False)
    by_expert = pl.BlockSpec((1, slots, width), lambda e, c: (e, 0, 0))
    return call(
        functools.partial(moe_kernel, capp),
        (experts, steps),
        [
            whole(flat), whole(flat), whole(flat), whole(flat), by_expert,
            whole(place_own.shape), whole(place_oth.shape), whole(gates.shape),
            pl.BlockSpec(w_block, lambda e, c: (0, e * steps + c)),
            pl.BlockSpec(w_block, lambda e, c: (0, blocks + e * steps + c)),
            pl.BlockSpec((1, 1, block), lambda e, c: (e, 0, c)),
            pl.BlockSpec((1, 1, width), lambda e, c: (e, 0, 0)),
        ],
        [
            by_expert, by_expert, pl.BlockSpec((1, slots, 128), lambda e, c: (e, 0, 0)),
            grad_block(shape, block, lambda e, c: e * steps + c),
            pl.BlockSpec((1, 1, block), lambda e, c: (e, 0, c)),
            pl.BlockSpec((1, 1, width), lambda e, c: (e, 0, 0)),
        ],
        [
            jax.ShapeDtypeStruct((experts, slots, width), BF),
            jax.ShapeDtypeStruct((experts, slots, width), BF),
            jax.ShapeDtypeStruct((experts, slots, 128), BF),
            jax.ShapeDtypeStruct(shape, BF),
            jax.ShapeDtypeStruct((experts, 1, ff), F32),
            jax.ShapeDtypeStruct((experts, 1, width), F32),
        ],
        [
            pltpu.VMEM((slots, width), BF), pltpu.VMEM((slots, width), BF),
            pltpu.VMEM((slots, 128), F32),
            pltpu.VMEM((slots, width), F32), pltpu.VMEM((slots, width), F32),
        ],
        12.0 * slots * experts * width * ff + 4.0 * experts * slots * half * width,
        60.0e6, "experts",
    )(*rows_own, *rows_oth, grad_rows, place_own, place_oth, gates, weights, weights,
      in_bias, out_bias)


def collect_kernel(capp, jobs, *refs):
    picks = {}
    for m, place, source, out, kind in jobs:
        rows_ref, out_ref = refs[source], refs[out]
        experts = rows_ref.shape[0]
        half = refs[place].shape[1]
        if (m, place) not in picks:
            hits = []
            for expert in range(experts):
                ids = lax.broadcasted_iota(jnp.int32, (half, capp), 1) + expert * capp
                hit = (refs[place][m, :, 0:1] == ids) | (refs[place][m, :, 1:2] == ids)
                hits.append(as_pick(hit))
            picks[m, place] = hits
        total = None
        for expert, pick in enumerate(picks[m, place]):
            rows = rows_ref[expert, m * capp : (m + 1) * capp, :]
            if kind == "dots":
                part = lax.dot_general(
                    rows, pick, (((0,), (1,)), ((), ())), preferred_element_type=F32
                )
            else:
                part = mm(pick, rows)
            total = part if total is None else total + part
        if kind == "dots":
            total = total[0:8] + total[8:16] + total[16:24]
        if len(out_ref.shape) == 3:
            out_ref[m] = total.astype(out_ref.dtype)
        else:
            out_ref[...] = total.astype(out_ref.dtype)


def collect(capp, arrays, outs, jobs, name, after=()):
    experts, slots, width = arrays[-1].shape
    return call(
        functools.partial(collect_kernel, capp, tuple(jobs)), (1,),
        [whole(value.shape) for value in arrays], [whole(shape) for shape, _ in outs],
        [jax.ShapeDtypeStruct(shape, kind) for shape, kind in outs], [],
        2.0 * len(jobs) * arrays[0].shape[1] * experts * capp * width, 8.0e6, name, after,
    )(*arrays)


def gate_bwd_kernel(
    a_ref, og_ref, held_ref, ro_ref, rr_ref, do_ref, dr_ref, gp_ref, rt_ref, g_ref, b_ref,
    sent_ref, da_ref, drt_ref, dg_ref, db_ref,
):
    after = a_ref[...]
    incoming = og_ref[0].astype(F32)
    sent_ref[...] = held_ref[...]
    gates = gp_ref[...]
    found = do_ref[0] + dr_ref[0]
    spread = jnp.where(
        lax.broadcasted_iota(jnp.int32, (found.shape[0], gates.shape[1]), 0)
        == lax.broadcasted_iota(jnp.int32, (found.shape[0], gates.shape[1]), 1),
        1.0, 0.0,
    )
    gate_grad = lax.dot_general(
        found, spread, (((0,), (0,)), ((), ())), precision=EXACT, preferred_element_type=F32
    )
    logit_grad = gates * (gate_grad - jnp.sum(gates * gate_grad, axis=-1, keepdims=True))
    unit, scale = norm_parts(after)
    normed = unit * g_ref[...] + b_ref[...]
    drt_ref[...] = lax.dot_general(
        logit_grad, normed, (((0,), (0,)), ((), ())), precision=EXACT, preferred_element_type=F32
    )
    normed_grad = ro_ref[0].astype(F32) + rr_ref[...].astype(F32)
    normed_grad += lax.dot_general(
        logit_grad, rt_ref[...], (((1,), (1,)), ((), ())), precision=EXACT,
        preferred_element_type=F32,
    )
    hidden_grad, gain_grad, shift_grad = norm_pull(unit, scale, g_ref[...], normed_grad)
    da_ref[...] = incoming + hidden_grad
    dg_ref[...] = gain_grad
    db_ref[...] = shift_grad


def gate_back(after, incoming, held, r_own, r_got, d_own, d_got, gates, router, gain, shift,
              which, behind=()):
    block, width = after.shape
    lanes = gates.shape[1]
    one = pl.BlockSpec((1, block, width), lambda *_: (which, 0, 0))
    dots = pl.BlockSpec((1, 8, block), lambda *_: (which, 0, 0))
    flat = whole((block, width))
    low = whole((block, lanes))
    return call(
        gate_bwd_kernel, (1,),
        [
            flat, one, whole(held.shape), one, flat, dots, dots, low,
            whole((width, lanes)), whole((1, width)), whole((1, width)),
        ],
        [whole(held.shape), flat, whole((lanes, width)), whole((1, width)), whole((1, width))],
        [
            jax.ShapeDtypeStruct(held.shape, BF),
            jax.ShapeDtypeStruct((block, width), F32),
            jax.ShapeDtypeStruct((lanes, width), F32),
            jax.ShapeDtypeStruct((1, width), F32),
            jax.ShapeDtypeStruct((1, width), F32),
        ],
        [], 4.0 * block * width * lanes, 7.0e6, "gate_bwd", behind,
    )(after, incoming, held, r_own, r_got, d_own, d_got, gates, router, gain, shift)


def swap(value):
    return lax.ppermute(value, "tensor", [(0, 1), (1, 0)])


def in_order(mine, other, axis):
    first = lax.axis_index("tensor") == 0
    return jnp.stack([jnp.where(first, mine, other), jnp.where(first, other, mine)], axis=axis)


def gather_rows(share):
    return lax.all_gather(share, "dp", axis=0, tiled=True)


def ring_chip(place, chips):
    half = chips // 2
    even = 2 * place
    odd = 2 * (chips - 1 - place) + 1
    if isinstance(place, int):
        return even if place < half else odd
    return jnp.where(place < half, even, odd)


def ring_add(kind, refs):
    def chunk(grads, given):
        return grads[0].astype(F32) + given[0].astype(F32)

    if kind == 0:
        grads, given, ahead, behind = refs
        total = chunk(grads, given).astype(BF)
        ahead[...] = total[0]
        behind[...] = total[1]
    elif kind == 3:
        grads, given, got_a, got_b, out = refs
        out[...] = chunk(grads, given) + (got_a[...].astype(F32) + got_b[...].astype(F32))
    elif kind == 4:
        one, two, out = refs
        out[...] = one[...] + two[...]
    else:
        grads_a, given_a, grads_b, given_b, got_a, got_b, ahead, behind = refs
        one, two = chunk(grads_a, given_a), chunk(grads_b, given_b)
        if kind == 1:
            ahead[0] = (one[0] + got_a[...].astype(F32)).astype(BF)
            ahead[1] = one[1].astype(BF)
            behind[0] = two[0].astype(BF)
            behind[1] = (two[1] + got_b[...].astype(F32)).astype(BF)
        else:
            ahead[...] = (one + got_a[...].astype(F32)).astype(BF)
            behind[...] = (two + got_b[...].astype(F32)).astype(BF)


def step_kernel(plans, _, *refs):
    taken = sum(ins for _, ins, _ in plans)
    at, out_at = 0, taken
    for kind, ins, outs in plans:
        ring_add(kind, refs[at : at + ins] + refs[out_at : out_at + outs])
        at += ins
        out_at += outs


def step_all(chains, after=()):
    live = [chain for chain in chains if not chain.finished()]
    if not live:
        return tuple(after)
    stages = [chain.stage(index) for index, chain in enumerate(live)]
    places = jnp.stack([place for stage in stages for place in stage[1]]).astype(jnp.int32)
    sums = call(
        functools.partial(
            step_kernel, tuple((stage[0], len(stage[2]), len(stage[4])) for stage in stages)
        ),
        (1,), [spec for stage in stages for spec in stage[2]],
        [whole(out.shape) for stage in stages for out in stage[4]],
        [out for stage in stages for out in stage[4]], [], 0, 2.0e6, "ring_add", after,
        prefetch=1,
    )(places, *[value for stage in stages for value in stage[3]])
    at = 0
    for chain, stage in zip(live, stages):
        chain.take(sums[at : at + len(stage[4])])
        at += len(stage[4])
    return tuple(sums[:1])


class RingSum:
    def __init__(self, kept, sent):
        count = lax.axis_size("dp")
        self.chips = count // 2
        self.ring = [ring_chip(place, self.chips) for place in range(self.chips)]
        chip = lax.axis_index("dp") // 2
        self.here = jnp.where(chip % 2 == 0, chip // 2, self.chips - 1 - chip // 2)
        self.kept = kept
        self.away = self.chips // 2
        self.messages = (sent,)
        self.given = lax.ppermute(sent, "dp", [(at, at ^ 1) for at in range(count)])
        self.got = ()
        self.result = None

    def send(self, value, step):
        pairs = [
            (self.ring[at] * 2 + side, self.ring[(at + step) % self.chips] * 2 + side)
            for at in range(self.chips)
            for side in range(2)
        ]
        return lax.ppermute(value, "dp", pairs)

    def finished(self):
        return self.result is not None

    def stage(self, index):
        away = self.away
        chips = [
            ring_chip((self.here + far) % self.chips, self.chips)
            for far in (away, self.chips - away)
        ]
        shape = self.kept.shape[1:]

        def chunk_specs(which):
            slot = 2 * index + which
            return [pl.BlockSpec((1,) + shape, lambda _, at: (at[slot], 0, 0, 0))] * 2

        far = self.chips // 2
        kind = 3 if away == 0 else 0 if away == far else 1 if away == far - 1 else 2
        two_ways = kind in (1, 2)
        in_specs = chunk_specs(0) + (chunk_specs(1) if two_ways else [])
        in_specs += [whole(got.shape) for got in self.got]
        args = [self.kept, self.given] * (2 if two_ways else 1) + list(self.got)
        out = shape if kind else shape[1:]
        outs = [jax.ShapeDtypeStruct(out, F32 if kind == 3 else BF)] * (1 if kind == 3 else 2)
        return kind, chips, in_specs, args, outs

    def take(self, sums):
        if self.away == 0:
            self.result = sums[0]
            self.messages = ()
            return
        self.away -= 1
        self.messages = tuple(sums)
        self.got = (self.send(sums[0], 1), self.send(sums[1], -1))


class PlainSum:
    def __init__(self, grad):
        axis = 1 if grad.ndim == 3 else 0
        done = lax.psum_scatter(grad, "dp", scatter_dimension=axis, tiled=True)
        self.messages = (done,)
        self.result = done.reshape((2,) + done.shape[-2:]).astype(F32)

    def finished(self):
        return True


def hold_kernel(value_ref, out_ref):
    return


def hold(value, after):
    anywhere = pl.BlockSpec(memory_space=pl.ANY)
    return call(
        hold_kernel, (1,), [anywhere], anywhere, jax.ShapeDtypeStruct(value.shape, value.dtype),
        [], 0, 1.0e3, "hold", after, aliases={0: 0},
    )(value)


def expert_out_kernel(sum_ref, in_ref, out_ref):
    experts, ff = in_ref.shape[1], in_ref.shape[2]
    for part, ref in enumerate((in_ref, out_ref)):
        for expert in range(experts):
            ref[:, expert, :] = sum_ref[part, :, expert * ff : (expert + 1) * ff].astype(F32)


def expert_outputs(total, shape, after):
    return call(
        expert_out_kernel, (1,), [whole(total.shape)], [whole(shape)] * 2,
        [jax.ShapeDtypeStruct(shape, F32)] * 2, [], 0, 4.0e6, "expert_out", after,
    )(total)


class PairSum:
    def __init__(self, value):
        self.count = lax.axis_size("dp")
        self.value = value
        self.reach = 1
        self.send()

    def send(self):
        self.messages = (self.value,)
        if self.reach < self.count:
            pairs = [(at, at ^ self.reach) for at in range(self.count)]
            self.got = lax.ppermute(self.value, "dp", pairs)
        elif self.reach == self.count:
            self.got = swap(self.value)
        else:
            self.got = None
            self.messages = ()
        self.reach *= 2

    def finished(self):
        return self.got is None

    def stage(self, index):
        zero = jnp.zeros((), jnp.int32)
        shape = self.value.shape
        return (
            4, [zero, zero], [whole(shape)] * 2, [self.value, self.got],
            [jax.ShapeDtypeStruct(shape, F32)],
        )

    def take(self, sums):
        (self.value,) = sums
        self.send()


def pack_kernel(plan, side_ref, *refs):
    out_ref = refs[-1]
    width = out_ref.shape[1]
    out_ref[...] = jnp.zeros_like(out_ref)
    at = 0
    for inputs, rows, factor, sided in plan:
        total = None
        for which in inputs:
            ref = refs[which]
            value = ref[...].reshape(-1, ref.shape[-1])[:rows]
            total = value if total is None else total + value
        total = total * factor if factor != 1.0 else total
        parts = total.shape[1] // width
        for row in range(rows):
            for part in range(parts):
                piece = total[row : row + 1, part * width : (part + 1) * width]
                place = at + row * parts + part
                if sided:
                    place = place + side_ref[0] * (rows * parts)
                out_ref[pl.ds(place, 1), :] = piece
        at += rows * parts * (2 if sided else 1)


def pack_rows(groups, width):
    arrays, plan, total = [], [], 0
    for values, rows, factor, sided in groups:
        plan.append((tuple(range(len(arrays), len(arrays) + len(values))), rows, factor, sided))
        arrays += values
        total += rows * (values[0].shape[-1] // width) * (2 if sided else 1)
    shape = (round_up(total, 8), width)
    side = lax.axis_index("tensor").reshape(1)
    (out,) = call(
        functools.partial(pack_kernel, tuple(plan)), (1,),
        [whole(value.shape) for value in arrays], [whole(shape)],
        [jax.ShapeDtypeStruct(shape, F32)], [], 0, 3.0e5, "pack", (), prefetch=1,
    )(side, *arrays)
    return out


def out_kernel(a0_ref, a1_ref, y_ref, got_ref, out_ref):
    for m, a_ref in enumerate((a0_ref, a1_ref)):
        total = a_ref[...] + (y_ref[m].astype(F32) + got_ref[m].astype(F32))
        out_ref[m] = total.astype(BF)


def layer_output(hidden, y_own, y_got, after):
    shape = y_own.shape
    (out,) = call(
        out_kernel, (1,),
        [whole(hidden[0].shape)] * 2 + [whole(shape)] * 2, [whole(shape)],
        [jax.ShapeDtypeStruct(shape, BF)], [], 0, 8.0e6, "layer_output", after,
    )(*hidden, y_own, y_got)
    return out


def place_kernel(side_ref, own_ref, got_ref, out_ref):
    images, length = own_ref.shape[1], out_ref.shape[2]
    side = side_ref[0]
    for image in range(images):
        kept = own_ref[:, image, :length, :].astype(out_ref.dtype)
        out_ref[:, side * images + image] = kept
        other = got_ref[:, image, :length, :].astype(out_ref.dtype)
        out_ref[:, (1 - side) * images + image] = other


def place_rows_kernel(side_ref, own_ref, got_ref, out_ref):
    images, length = own_ref.shape[1], out_ref.shape[1]
    for side, (first, second) in enumerate(((own_ref, got_ref), (got_ref, own_ref))):
        @pl.when(side_ref[0] == side)
        def _():
            for image in range(images):
                out_ref[0, :, image, :] = first[0, image, :length, :].astype(out_ref.dtype)
                out_ref[0, :, images + image, :] = second[0, image, :length, :].astype(
                    out_ref.dtype
                )


def place_images(own, got, shape, kind, after):
    micro, images, length, width = shape
    padded = (micro, images // 2, own.size // (micro * (images // 2) * width), width)
    side = lax.axis_index("tensor").reshape(1)
    if kind == F32:
        turned = (micro, length, images, width)
        (out,) = call(
            place_rows_kernel, (micro,),
            [pl.BlockSpec((1,) + padded[1:], lambda m, *_: (m, 0, 0, 0))] * 2,
            [pl.BlockSpec((1,) + turned[1:], lambda m, *_: (m, 0, 0, 0))],
            [jax.ShapeDtypeStruct(turned, kind)], [], 0, 8.0e6, "place", after, prefetch=1,
        )(side, own.reshape(padded), got.reshape(padded))
        return jnp.swapaxes(out, 1, 2)
    (out,) = call(
        place_kernel, (micro,),
        [pl.BlockSpec((1,) + padded[1:], lambda m, *_: (m, 0, 0, 0))] * 2,
        [pl.BlockSpec((1,) + shape[1:], lambda m, *_: (m, 0, 0, 0))],
        [jax.ShapeDtypeStruct(shape, kind)], [], 0, 8.0e6, "place", after, prefetch=1,
    )(side, own.reshape(padded), got.reshape(padded))
    return out


def join_sides(mine_first):
    mine = lax.axis_index("tensor")
    kept = lax.dynamic_index_in_dim(mine_first, mine, 0, keepdims=False)
    sent = lax.dynamic_index_in_dim(mine_first, 1 - mine, 0, keepdims=False)
    return kept + swap(sent.astype(BF)).astype(F32)


def own_half(value, axis):
    size = value.shape[axis] // 2
    return lax.dynamic_slice_in_dim(value, lax.axis_index("tensor") * size, size, axis)


def local(
    block_input, norm_gain, row_bias, qkv_weight, qkv_bias, out_weight, mlp_in, mlp_in_bias,
    mlp_out, mlp_out_bias, router, expert_in, expert_in_bias, expert_out, expert_out_bias,
    routes, slot_index, out_grad,
):
    micro, images, length, width = block_input.shape
    experts = router.shape[1]
    share_rows = mlp_in.shape[0]
    own_images = images // 2
    pad = round_up(length, ROW_PAD)
    half = own_images * pad
    rows = micro * half
    capp = round_up(CAP, ROW_PAD)
    side = lax.axis_index("tensor")

    def attn_share(layer):
        return jnp.concatenate(
            [qkv_weight[layer].reshape(share_rows, -1), out_weight[layer]], axis=1
        )

    devices = lax.axis_size("dp")
    first_mine = jnp.concatenate([attn_share(0), attn_share(1), mlp_in, mlp_out], axis=1)
    first_w = lax.all_gather(
        in_order(first_mine, swap(first_mine), 0), "dp", axis=0, tiled=False
    )
    if not whole_tiles(devices, width):
        first_w = jnp.moveaxis(first_w, 0, 1).reshape(1, 2, width, -1)
    dense_at = 4 * width
    expert_w = gather_rows(
        jnp.concatenate(
            [expert_in.reshape(share_rows, -1), expert_out.reshape(share_rows, -1)], axis=1
        )
    )

    biases = jnp.concatenate([qkv_bias.reshape(-1), mlp_in_bias])
    bias_pair = in_order(biases, swap(biases), 0)
    qkv_bias_pair = bias_pair[:, : qkv_bias.size].reshape((2,) + qkv_bias.shape)
    mlp_bias_full = bias_pair[:, qkv_bias.size :].reshape(1, -1)

    def qkv_bias_row(layer):
        pair = qkv_bias_pair[:, layer]
        zero = jnp.zeros_like(pair[:, 0])
        return jnp.concatenate([pair[:, 0], zero, pair[:, 1]], axis=1).reshape(1, -1)

    def padded(value, start):
        part = lax.dynamic_slice_in_dim(value, start, own_images, 1)
        return jnp.pad(part, ((0, 0), (0, 0), (0, pad - length), (0, 0)))

    mine_at = side * own_images
    other_at = (1 - side) * own_images
    hidden = padded(block_input, mine_at).astype(F32).reshape(rows, width)
    grad_own = padded(out_grad, mine_at).reshape(micro, half, width)
    grad_oth = padded(out_grad, other_at).reshape(micro, half, width)

    kept = slot_index < CAP
    place = jnp.where(kept, routes * capp + slot_index, -1)
    pick = jnp.where(kept, routes, -1)

    def lay(value, start):
        part = lax.dynamic_slice_in_dim(value, start, own_images, 1)
        part = jnp.pad(
            part, ((0, 0), (0, 0), (0, pad - length), (0, 0)), constant_values=-1
        )
        return part.reshape(micro, half, 2)

    place_own, place_oth = lay(place, mine_at), lay(place, other_at)
    place_own_rows = jnp.swapaxes(place_own, 1, 2)
    place_oth_rows = jnp.swapaxes(place_oth, 1, 2)
    grad_rows = spread_rows(
        grad_own, grad_oth, place_own_rows, place_oth_rows, experts, capp
    )
    select = lay(pick, mine_at).reshape(rows, 2)
    router_wide = jnp.pad(router, ((0, 0), (0, 128 - experts)))

    def row(vector):
        return vector.reshape(1, -1)

    qkv_one, lse_one, mix_one, after_one = attention_forward(
        hidden, row(norm_gain[0, 0]), row(row_bias[0, 0]), first_w, 0, qkv_bias_row(0),
        row(row_bias[0, 2]), length, pad, 0, micro,
    )
    after_ffn = dense_forward(
        after_one, row(norm_gain[0, 1]), row(row_bias[0, 1]), first_w, dense_at, mlp_bias_full,
        row(mlp_out_bias),
    )
    second = [
        attention_forward(
            after_ffn, row(norm_gain[1, 0]), row(row_bias[1, 0]), first_w, 1, qkv_bias_row(1),
            row(row_bias[1, 2]), length, pad, m, 1,
            (row(norm_gain[1, 1]), row(row_bias[1, 1]), router_wide, select, experts),
        )
        for m in range(micro)
    ]
    qkv_two, lse_two, mix_two, after_two, rows_own, gates, chosen = zip(*second)
    rows_oth = [swap(part) for part in rows_own]
    gate_own = jnp.stack([part[:, :2].T for part in chosen])
    gate_pair = jnp.concatenate([gate_own, swap(gate_own)], axis=1)
    ring = whole_tiles(devices, width)
    core = (lax.axis_index("dp") % 2).reshape(1)
    y_slots, r_slots, d_slots, expert_grad, ein_bias, eout_bias = mixture(
        rows_own, rows_oth, grad_rows, place_own_rows, place_oth_rows, gate_pair, expert_w,
        expert_in_bias.reshape(experts, 1, -1), expert_out_bias.reshape(experts, 1, -1), capp,
        devices,
    )
    group, one, dots = (micro, half, width), (half, width), (micro, 8, half)
    r_oth0, r_oth1, d_oth = collect(
        capp, (place_oth, d_slots, r_slots), ((one, BF), (one, BF), (dots, F32)),
        (
            (0, 0, 2, 3, "rows"), (1, 0, 2, 4, "rows"), (0, 0, 1, 5, "dots"),
            (1, 0, 1, 5, "dots"),
        ),
        "collect_first",
    )
    y_own, y_oth, r_own, d_own = collect(
        capp, (place_own, place_oth, d_slots, r_slots, y_slots),
        ((group, BF), (group, BF), (group, BF), (dots, F32)),
        (
            (0, 0, 3, 7, "rows"), (1, 0, 3, 7, "rows"), (0, 0, 2, 8, "dots"),
            (1, 0, 2, 8, "dots"), (0, 0, 4, 5, "rows"), (1, 0, 4, 5, "rows"),
            (0, 1, 4, 6, "rows"), (1, 1, 4, 6, "rows"),
        ),
        "collect_rest", (r_oth0,),
    )
    d_got = swap(d_oth)
    r_got = swap(r_oth0)
    expert_sum = PlainSum(expert_grad)
    grad_two, gate_parts, cores = [], [], []
    for m, held in enumerate((r_oth1, y_oth)):
        sent, grad_part, *small = gate_back(
            after_two[m], grad_own, held, r_own, r_got, d_own, d_got, gates[m],
            router_wide, row(norm_gain[1, 1]), row(row_bias[1, 1]), m,
            (cores[0][1],) if m else (),
        )
        r_got = swap(sent)
        grad_two.append(grad_part)
        gate_parts.append(small)
        cores.append(
            attention_core_back(
                grad_part, first_w, 1, (qkv_two[m], lse_two[m], half), length, pad, m, (sent,)
            )
        )
    y_got = r_got
    router_parts, gain_parts, shift_parts = (list(pair) for pair in zip(*gate_parts))
    two_grad, (grad_ffn, qb_two, ob_two, gain_two, shift_two) = attention_grad(
        core, grad_two, after_ffn, row(norm_gain[1, 0]), row(row_bias[1, 0]), first_w, 1, cores,
        mix_two, devices, ring, F32,
    )
    sum_two = RingSum(*two_grad) if ring else PlainSum(*two_grad)
    out_own = layer_output(after_two, y_own, y_got, (gain_two,))
    out_got = swap(out_own)
    early = (
            [
                ([gain_two], 1, 1.0, False), (gain_parts, 1, 1.0, False),
                ([shift_two], 1, 1.0, False), (shift_parts, 1, 1.0, False),
                ([ob_two], 1, 1.0, False), ([qb_two], 1, 1.0, False),
                (router_parts, experts, 1.0, False), ([eout_bias], experts, 0.5, False),
                ([ein_bias], experts, 1.0, True),
            ]
    )
    dense_grad, (grad_one, in_bias_grad, out_bias_grad, gain_ffn, shift_ffn) = dense_back(
        core, grad_ffn, after_one, row(norm_gain[0, 1]), row(row_bias[0, 1]), first_w, dense_at,
        mlp_bias_full, devices, ring, sum_two.messages + (out_own,),
    )
    last = step_all([sum_two], (gain_ffn, out_got))
    if ring:
        dense_sum = RingSum(dense_grad[0], hold(dense_grad[1], last))
    else:
        dense_sum = PlainSum(*dense_grad)
    block_output = place_images(out_own, out_got, block_input.shape, BF, last)
    step_all([dense_sum], (block_output,))
    cores = []
    for which in range(2):
        cores.append(
            attention_core_back(
                grad_one, first_w, 0, (qkv_one, lse_one, half), length, pad, which,
                sum_two.messages + dense_sum.messages + (block_output,),
            )
        )
        step_all([sum_two, dense_sum], (cores[-1][1],))
    one_grad, (grad_zero, qb_one, ob_one, gain_one, shift_one) = attention_grad(
        core, (grad_one, grad_one), hidden, row(norm_gain[0, 0]), row(row_bias[0, 0]), first_w,
        0, cores, (mix_one, mix_one), devices, False, BF,
        sum_two.messages + dense_sum.messages,
    )
    last = step_all([sum_two, dense_sum], (qb_one,))
    one_sum = PlainSum(hold(one_grad[0], expert_sum.messages + last))
    late_sum = PairSum(
        pack_rows(
            [
                ([gain_one], 1, 1.0, False), ([gain_ffn], 1, 1.0, False),
                ([shift_one], 1, 1.0, False), ([shift_ffn], 1, 1.0, False),
                ([ob_one], 1, 1.0, False), ([qb_one], 1, 1.0, False),
                ([in_bias_grad], 1, 1.0, False), ([out_bias_grad], 1, 1.0, False),
            ] + early,
            width,
        )
    )
    expert_total = expert_sum.messages[0].reshape((2, share_rows, -1))
    expert_grads = expert_outputs(expert_total, expert_in.shape, last)
    last = (expert_grads[0],)
    grad_got = swap(grad_zero)
    for turn in range(devices):
        last = step_all([sum_two, dense_sum, late_sum], last)
        if turn == 2:
            input_grad = place_images(grad_zero, grad_got, block_input.shape, F32, last)
            last = (input_grad,)

    one_done = join_sides(one_sum.result)
    joined = join_sides(
        jnp.concatenate(
            [
                sum_two.result[:, None],
                jnp.moveaxis(dense_sum.result.reshape(2, share_rows, 2, -1), 2, 0),
            ],
            axis=1,
        )
    )
    attn_grads, dense_done = [one_done, joined[0]], joined[1:]
    split_at = 3 * width // 2

    late = late_sum.value
    ff_rows = in_bias_grad.shape[1] // width
    early = late[9 + ff_rows :]
    gain_sum = jnp.concatenate([late[0:2], early[0:2]])
    shift_sum = jnp.concatenate([late[2:5], early[2:5]])
    qb_sum = jnp.stack([late[5:8], early[5:8]]).reshape(2, 2, 3, width // 2)
    qb_sum = lax.dynamic_index_in_dim(qb_sum, side, 1, keepdims=False)
    in_bias_sum = late[8 : 8 + ff_rows]
    out_bias_sum = late[8 + ff_rows]
    at = 8 + experts
    router_sum = early[8:at]
    eout_sum = early[at : at + experts]
    at += experts
    ein_rows = expert_in_bias.size // width
    ein_sum = lax.dynamic_slice_in_dim(early, at + side * ein_rows, ein_rows, 0)
    return (
        block_output,
        input_grad,
        gain_sum.reshape(norm_gain.shape),
        shift_sum.reshape(row_bias.shape),
        jnp.stack([part[:, :split_at] for part in attn_grads]).reshape(qkv_weight.shape),
        jnp.stack([qb_sum[:, 0], qb_sum[:, 2]], axis=1),
        jnp.stack([part[:, split_at:] for part in attn_grads]),
        dense_done[0],
        own_half(in_bias_sum.reshape(-1), 0),
        dense_done[1],
        out_bias_sum.reshape(-1),
        router_sum.T,
        expert_grads[0],
        ein_sum.reshape(expert_in_bias.shape),
        expert_grads[1],
        eout_sum.reshape(experts, width),
    )


def solution(mesh):
    return jax.shard_map(
        local,
        mesh=mesh,
        in_specs=(
            P(None, "dp", None, None), P(), P(), P(None, "dp", None, "tensor"),
            P(None, None, "tensor"), P(None, "dp", "tensor"), P("dp", "tensor"), P("tensor"),
            P("dp", "tensor"), P(), P(), P("dp", None, "tensor"), P(None, "tensor"),
            P("dp", None, "tensor"), P(), P(None, "dp", None, None), P(None, "dp", None, None),
            P(None, "dp", None, None),
        ),
        out_specs=(
            P(None, "dp", None, None), P(None, "dp", None, None), P(), P(),
            P(None, "dp", None, "tensor"), P(None, None, "tensor"), P(None, "dp", "tensor"),
            P("dp", "tensor"), P("tensor"), P("dp", "tensor"), P(), P(),
            P("dp", None, "tensor"), P(None, "tensor"), P("dp", None, "tensor"), P(),
        ),
        check_vma=False,
    )
```

```python
import functools

import jax
import jax.numpy as jnp
from jax import lax
from jax.experimental import pallas as pl
from jax.experimental.pallas import tpu as pltpu
from jax.sharding import PartitionSpec as P

HD = 64
CAP = 295
NORM_EPS = 1e-06
EXACT = lax.Precision.HIGHEST
BF = jnp.bfloat16
F32 = jnp.float32
VMEM_LIMIT = 58 * 1024 * 1024
FF_BLOCK = 512
EXPERT_BLOCK = 1536
ROW_PAD = 16
GELU_SLOPE = 0.7978845608028654
GELU_CUBE = 0.044715


def round_up(value, unit):
    return -(-value // unit) * unit


def mm(left, right):
    return jnp.dot(left, right, preferred_element_type=F32)


def mm_bt(left, right):
    return lax.dot_general(left, right, (((1,), (1,)), ((), ())), preferred_element_type=F32)


def mm_at(left, right):
    return lax.dot_general(left, right, (((0,), (0,)), ((), ())), preferred_element_type=F32)


def norm_parts(hidden):
    center = jnp.mean(hidden, axis=-1, keepdims=True)
    centred = hidden - center
    spread = jnp.mean(centred * centred, axis=-1, keepdims=True)
    scale = lax.rsqrt(spread + NORM_EPS)
    return centred * scale, scale


def norm_pull(unit, scale, gain, incoming):
    wide = incoming * gain
    mean_wide = jnp.mean(wide, axis=-1, keepdims=True)
    mean_dot = jnp.mean(wide * unit, axis=-1, keepdims=True)
    hidden_grad = scale * (wide - mean_wide - unit * mean_dot)
    gain_grad = jnp.sum(incoming * unit, axis=0, keepdims=True)
    shift_grad = jnp.sum(incoming, axis=0, keepdims=True)
    return hidden_grad, gain_grad, shift_grad


def gelu_pair(preact):
    square = preact * preact
    inner = GELU_SLOPE * preact * (1.0 + GELU_CUBE * square)
    bend = jnp.tanh(inner)
    half = 0.5 * (1.0 + bend)
    active = preact * half
    slope = half + 0.5 * preact * (1.0 - bend * bend) * (
        GELU_SLOPE * (1.0 + 3.0 * GELU_CUBE * square)
    )
    return active, slope


def gelu_value(preact):
    square = preact * preact
    inner = GELU_SLOPE * preact * (1.0 + GELU_CUBE * square)
    return 0.5 * preact * (1.0 + jnp.tanh(inner))


def call(kernel, grid, in_specs, out_specs, out_shape, scratch, flops, traffic, name,
         after=(), prefetch=0, aliases=None):
    taken = prefetch + len(in_specs)
    skipped = len(after)

    def body(*refs):
        kernel(*refs[:taken], *refs[taken + skipped :])

    made = pl.pallas_call(
        body,
        grid_spec=pltpu.PrefetchScalarGridSpec(
            num_scalar_prefetch=prefetch,
            grid=grid,
            in_specs=list(in_specs) + [pl.BlockSpec(memory_space=pl.ANY)] * skipped,
            out_specs=out_specs,
            scratch_shapes=scratch,
        ),
        out_shape=out_shape,
        input_output_aliases=aliases or {},
        name=name,
        compiler_params=pltpu.CompilerParams(
            vmem_limit_bytes=VMEM_LIMIT,
            dimension_semantics=("arbitrary",) * len(grid),
        ),
        cost_estimate=pl.CostEstimate(
            flops=int(flops), bytes_accessed=int(traffic), transcendentals=0
        ),
    )
    return lambda *args: made(*args, *after)


def whole_tiles(devices, width):
    return (width // devices) % ROW_PAD == 0


def grad_shapes(devices, width, columns, split):
    if not whole_tiles(devices, width):
        return [(2, width, columns)]
    if split:
        return [(devices // 2, 2, width // devices, columns)] * 2
    return [(devices, 2, width // devices, columns)]


def grad_block(shape, columns, index):
    block = shape[:-1] + (columns,)
    zeros = (0,) * (len(shape) - 1)
    return pl.BlockSpec(block, lambda *at: zeros + (index(*at),))


def put_grad(refs, core_ref, part, cols, value):
    ref = refs[0]
    if len(refs) == 2:
        pieces = value.reshape(ref.shape[0], 2, ref.shape[2], value.shape[1])
        core = core_ref[0]

        @pl.when(core == 0)
        def _():
            refs[0][:, part, :, cols] = pieces[:, 0]
            refs[1][:, part, :, cols] = pieces[:, 1]

        @pl.when(core != 0)
        def _():
            refs[0][:, part, :, cols] = pieces[:, 1]
            refs[1][:, part, :, cols] = pieces[:, 0]
    elif len(ref.shape) == 3:
        ref[part, :, cols] = value
    else:
        ref[:, part, :, cols] = value.reshape(ref.shape[0], ref.shape[2], value.shape[1])


def flat_rows(value):
    return value.reshape(-1, value.shape[-1])


def weight_spec(weights, sides, columns, index):
    devices, _, rows, _ = weights.shape
    return pl.BlockSpec(
        (devices, sides, rows, columns), index, pipeline_mode=pl.Buffered(1)
    )


def whole(shape):
    zeros = (0,) * len(shape)
    return pl.BlockSpec(shape, lambda *_: zeros, pipeline_mode=pl.Buffered(1))


def rows_of(block, width):
    return pl.BlockSpec((block, width), lambda step, *_: (step, 0))


def half_of(value, block, which):
    at = which if value.shape[0] > block else 0
    rest = (0,) * (value.ndim - 1)
    return pl.BlockSpec((block,) + value.shape[1:], lambda *_: (at,) + rest)


def attn_fwd_kernel(
    length, pad, heads, router_on,
    h_ref, g_ref, b_ref, w_ref, qb_ref, ob_ref, *rest,
):
    if router_on:
        g2_ref, b2_ref, rt_ref, sel_ref = rest[:4]
        qkv_ref, lse_ref, o_ref, a_ref, rb_ref, gp_ref, wt_ref = rest[4:]
    else:
        qkv_ref, lse_ref, o_ref, a_ref = rest
    width = h_ref.shape[1]
    images = h_ref.shape[0] // pad
    hidden = h_ref[...]
    unit, _ = norm_parts(hidden)
    normed = (unit * g_ref[...] + b_ref[...]).astype(BF)
    third = width // 2
    for t in range(2):
        cols = slice(t * 3 * third, (t + 1) * 3 * third)
        matrix = flat_rows(w_ref[:, t, :, : 3 * third])
        qkv_ref[:, cols] = (mm(normed, matrix) + qb_ref[:, cols]).astype(BF)
    pairs = heads // 2
    lane = lax.broadcasted_iota(jnp.int32, (pad, 2 * HD), 1)
    key_row = lax.broadcasted_iota(jnp.int32, (pad, pad), 0)

    def pair_step(step, carry):
        image = step // pairs
        pair = step % pairs
        rows = pl.ds(pl.multiple_of(image * pad, ROW_PAD), pad)

        def col(part):
            side = pair // (pairs // 2)
            at = (side * 3 + part) * (width // 2) + (pair % (pairs // 2)) * 2 * HD
            return pl.ds(pl.multiple_of(at, 2 * HD), 2 * HD)

        place = pl.ds(pl.multiple_of(pair * 2 * HD, 2 * HD), 2 * HD)

        query = qkv_ref[rows, col(0)] * HD ** (-0.5)
        key = qkv_ref[rows, col(1)]
        value = qkv_ref[rows, col(2)]
        mixed = []
        for half in range(2):
            mine = (lane >= HD) if half else (lane < HD)
            scores = mm_bt(key, jnp.where(mine, query, 0).astype(BF))
            scores = jnp.where(key_row < length, scores, -1e30)
            top = jnp.max(scores, axis=0, keepdims=True)
            weights = jnp.exp(scores - top)
            total = jnp.sum(weights, axis=0, keepdims=True)
            probs = (weights * (1.0 / total)).astype(BF)
            mixed.append(mm_at(probs, value))
            lse_ref[image, pl.ds(pair * 2 + half, 1), :] = top + jnp.log(total)
        o_ref[rows, place] = jnp.where(lane < HD, mixed[0], mixed[1]).astype(BF)
        return carry

    lax.fori_loop(0, images * pairs, pair_step, 0, unroll=6)
    out_matrix = jnp.concatenate(
        [flat_rows(w_ref[:, t, :, 3 * third :]) for t in range(2)], axis=1
    )
    after = hidden + mm_bt(o_ref[...], out_matrix) + ob_ref[...]
    a_ref[...] = after
    if router_on:
        unit2, _ = norm_parts(after)
        normed2 = unit2 * g2_ref[...] + b2_ref[...]
        rb_ref[...] = normed2.astype(BF)
        logits = jnp.dot(normed2, rt_ref[...], precision=EXACT, preferred_element_type=F32)
        lanes = lax.broadcasted_iota(jnp.int32, logits.shape, 1)
        live = lanes < router_on
        logits = jnp.where(live, logits, -1e30)
        gates = jnp.exp(logits - jnp.max(logits, axis=-1, keepdims=True))
        gates = gates / jnp.sum(gates, axis=-1, keepdims=True)
        gates = jnp.where(live, gates, 0.0)
        gp_ref[...] = gates
        first = jnp.sum(jnp.where(lanes == sel_ref[:, 0:1], gates, 0.0), axis=-1, keepdims=True)
        second = jnp.sum(jnp.where(lanes == sel_ref[:, 1:2], gates, 0.0), axis=-1, keepdims=True)
        wt_ref[...] = jnp.where(lanes == 0, first, jnp.where(lanes == 1, second, 0.0))


def attention_forward(
    hidden, gain, shift, weights, layer, qkv_bias, out_bias, length, pad, start, count,
    router=None,
):
    micro = 2
    rows, width = hidden.shape
    heads = width // HD
    block = rows // micro
    lse_rows = round_up(heads, 8)
    images = block // pad
    made = count * block
    in_specs = [
        pl.BlockSpec((block, width), lambda step: (start + step, 0)),
        whole((1, width)), whole((1, width)),
        weight_spec(weights, 2, 2 * width, lambda *_: (0, 0, 0, layer)),
        whole((1, 3 * width)), whole((1, width)),
    ]
    args = [hidden, gain, shift, weights, qkv_bias, out_bias]
    out_specs = [
        rows_of(block, 3 * width),
        pl.BlockSpec((images, lse_rows, pad), lambda step: (step, 0, 0)),
        rows_of(block, width),
        rows_of(block, width),
    ]
    out_shape = [
        jax.ShapeDtypeStruct((made, 3 * width), BF),
        jax.ShapeDtypeStruct((count * images, lse_rows, pad), F32),
        jax.ShapeDtypeStruct((made, width), BF),
        jax.ShapeDtypeStruct((made, width), F32),
    ]
    router_on = 0
    if router is not None:
        gain2, shift2, router_wide, select, router_on = router
        lanes = router_wide.shape[1]
        in_specs += [
            whole((1, width)), whole((1, width)), whole((width, lanes)),
            pl.BlockSpec((block, 2), lambda step: (start + step, 0)),
        ]
        args += [gain2, shift2, router_wide, select]
        out_specs += [rows_of(block, width), rows_of(block, lanes), rows_of(block, lanes)]
        out_shape += [
            jax.ShapeDtypeStruct((made, width), BF),
            jax.ShapeDtypeStruct((made, lanes), F32),
            jax.ShapeDtypeStruct((made, lanes), F32),
        ]
    return call(
        functools.partial(attn_fwd_kernel, length, pad, heads, router_on),
        (count,), in_specs, out_specs, out_shape, [],
        8.0 * made * width * width + 16.0 * made * pad * width, 12.0e6, "attn_fwd",
    )(*args)


def attn_core_kernel(
    length, pad, heads, da_ref, wo_ref, qkv_ref, lse_ref, dqkv_ref, low_ref, grad_sc,
):
    width = da_ref.shape[1]
    images = da_ref.shape[0] // pad
    pairs = heads // 2
    low = da_ref[...].astype(BF)
    low_ref[...] = low
    out_matrix = jnp.concatenate([flat_rows(wo_ref[:, t]) for t in range(2)], axis=1)
    grad_sc[...] = mm(low, out_matrix).astype(BF)
    lane = lax.broadcasted_iota(jnp.int32, (pad, 2 * HD), 1)
    key_row = lax.broadcasted_iota(jnp.int32, (pad, pad), 0)

    def pair_step(step, carry):
        image = step // pairs
        pair = step % pairs
        rows = pl.ds(pl.multiple_of(image * pad, ROW_PAD), pad)

        def col(part):
            side = pair // (pairs // 2)
            at = (side * 3 + part) * (width // 2) + (pair % (pairs // 2)) * 2 * HD
            return pl.ds(pl.multiple_of(at, 2 * HD), 2 * HD)

        place = pl.ds(pl.multiple_of(pair * 2 * HD, 2 * HD), 2 * HD)

        query = (qkv_ref[rows, col(0)] * HD ** (-0.5)).astype(BF)
        key = qkv_ref[rows, col(1)]
        value = qkv_ref[rows, col(2)]
        mixed = grad_sc[rows, place]
        key_turned = key.T
        parts = []
        for half in range(2):
            mine = (lane >= HD) if half else (lane < HD)
            scores = mm_bt(key, jnp.where(mine, query, 0).astype(BF))
            total = lse_ref[image, pl.ds(pair * 2 + half, 1), :]
            probs = jnp.where(key_row < length, jnp.exp(scores - total), 0.0)
            probs_grad = mm_bt(value, jnp.where(mine, mixed, 0).astype(BF))
            product = probs * probs_grad
            delta = jnp.sum(product, axis=0, keepdims=True)
            score_grad = (product - probs * delta).astype(BF)
            parts.append((
                mm(key_turned, score_grad) * HD ** (-0.5),
                mm(score_grad, query),
                mm(probs.astype(BF), mixed),
            ))
        turned = lax.broadcasted_iota(jnp.int32, (2 * HD, pad), 0)
        query_grad = jnp.where(turned < HD, parts[0][0], parts[1][0])
        dqkv_ref[rows, col(0)] = query_grad.T.astype(BF)
        for part in range(1, 3):
            dqkv_ref[rows, col(part)] = jnp.where(
                lane < HD, parts[0][part], parts[1][part]
            ).astype(BF)
        return carry

    lax.fori_loop(0, images * pairs, pair_step, 0, unroll=6)


def attention_core_back(incoming, weights, layer, stored, length, pad, which, after=()):
    qkv, lse, block = stored
    width = incoming.shape[1]
    heads = width // HD
    images = block // pad
    return call(
        functools.partial(attn_core_kernel, length, pad, heads),
        (1,),
        [
            half_of(incoming, block, which),
            weight_spec(weights, 2, width // 2, lambda *_: (0, 0, 0, 4 * layer + 3)),
            half_of(qkv, block, which),
            half_of(lse, images, which),
        ],
        [whole((block, 3 * width)), whole((block, width))],
        [
            jax.ShapeDtypeStruct((block, 3 * width), BF),
            jax.ShapeDtypeStruct((block, width), BF),
        ],
        [pltpu.VMEM((block, width), BF)],
        2.0 * block * width * width + 20.0 * block * pad * width * 4, 8.0e6, "attn_core",
        after,
    )(incoming, weights, qkv, lse)


def attn_grad_kernel(
    core_ref, da0_ref, da1_ref, h_ref, g_ref, b_ref, w_ref, dq0_ref, dq1_ref,
    low0_ref, low1_ref, o0_ref, o1_ref, *rest,
):
    dw_refs = rest[: len(rest) - 7]
    dh_ref, dqb_ref, dob_ref, dg_ref, db_ref, n_sc, acc = rest[len(rest) - 7 :]
    step = pl.program_id(0)
    block = dq0_ref.shape[0]
    wide = dq0_ref.shape[1]
    gain = g_ref[...]
    half = (slice(0, block), slice(block, 2 * block))

    @pl.when(step == 0)
    def _():
        unit, _ = norm_parts(h_ref[...])
        n_sc[...] = (unit * gain + b_ref[...]).astype(BF)
        acc[...] = jnp.zeros_like(acc)
        dob_ref[...] = jnp.sum(low0_ref[...].astype(F32), axis=0, keepdims=True) + jnp.sum(
            low1_ref[...].astype(F32), axis=0, keepdims=True
        )

    matrix = flat_rows(w_ref[:, 0, :, :wide])
    piece = sums = mix = None
    sides = ((dq0_ref, low0_ref, o0_ref), (dq1_ref, low1_ref, o1_ref))
    for side, (dq_ref, low_ref, o_ref) in enumerate(sides):
        grads = dq_ref[...]
        acc[half[side], :] += mm_bt(grads, matrix)
        outer = mm_at(n_sc[half[side], :], grads)
        total = jnp.sum(grads.astype(F32), axis=0, keepdims=True)
        out = mm_at(low_ref[...], o_ref[...])
        piece = outer if side == 0 else piece + outer
        sums = total if side == 0 else sums + total
        mix = out if side == 0 else mix + out
    put_grad(dw_refs, core_ref, 0, slice(0, wide), piece.astype(BF))
    put_grad(dw_refs, core_ref, 0, slice(wide, w_ref.shape[3]), mix.astype(BF))
    dqb_ref[...] = sums

    @pl.when(step == pl.num_programs(0) - 1)
    def _():
        unit, scale = norm_parts(h_ref[...])
        for side, da_ref in enumerate((da0_ref, da1_ref)):
            hidden_grad, gain_grad, shift_grad = norm_pull(
                unit[half[side]], scale[half[side]], gain, acc[half[side], :]
            )
            dh_ref[half[side], :] = (da_ref[...] + hidden_grad).astype(dh_ref.dtype)
            if side == 0:
                dg_ref[...] = gain_grad
                db_ref[...] = shift_grad
            else:
                dg_ref[...] += gain_grad
                db_ref[...] += shift_grad


def attention_grad(
    core, incoming, hidden, gain, shift, weights, layer, cores, mixed, devices, split, kind,
    after=(),
):
    rows, width = hidden.shape
    shapes = grad_shapes(devices, width, 2 * width, split)
    block = rows // 2
    short = jax.ShapeDtypeStruct((1, width), F32)
    third = width // 2

    def side_block(shape):
        if len(shape) == 3:
            return pl.BlockSpec((1,) + shape[1:], lambda t, *_: (t, 0, 0))
        return pl.BlockSpec(
            (shape[0], 1) + shape[2:], lambda t, *_: (0, t, 0, 0)
        )

    def columns_of(value, which, columns):
        at = which if value.shape[0] > block else 0
        return pl.BlockSpec((block, columns), lambda t, *_: (at, t))

    made = call(
        attn_grad_kernel, (2,),
        [
            half_of(incoming[0], block, 0), half_of(incoming[1], block, 1),
            whole((rows, width)), whole((1, width)), whole((1, width)),
            pl.BlockSpec(
                (weights.shape[0], 1, weights.shape[2], 2 * width),
                lambda t, *_: (0, t, 0, layer),
            ),
            columns_of(cores[0][0], 0, 3 * third), columns_of(cores[1][0], 0, 3 * third),
            whole((block, width)), whole((block, width)),
            columns_of(mixed[0], 0, third), columns_of(mixed[1], 1, third),
        ],
        [side_block(shape) for shape in shapes] + [
            whole((rows, width)), pl.BlockSpec((1, 3 * third), lambda t, *_: (0, t)),
            whole((1, width)), whole((1, width)), whole((1, width)),
        ],
        [jax.ShapeDtypeStruct(shape, BF) for shape in shapes] + [
            jax.ShapeDtypeStruct((rows, width), kind),
            jax.ShapeDtypeStruct((1, 3 * width), F32),
            short, short, short,
        ],
        [pltpu.VMEM((rows, width), BF), pltpu.VMEM((rows, width), F32)],
        14.0 * rows * width * width, 25.0e6, "attn_grad", after, prefetch=1,
    )(core, *incoming, hidden, gain, shift, weights, cores[0][0], cores[1][0], cores[0][1],
      cores[1][1], *mixed)
    return made[: len(shapes)], made[len(shapes) :]


def dense_fwd_kernel(a_ref, g_ref, b_ref, win_ref, wout_ref, bin_ref, bout_ref, x_ref, m_sc, acc):
    step = pl.program_id(0)

    @pl.when(step == 0)
    def _():
        unit, _ = norm_parts(a_ref[...])
        m_sc[...] = (unit * g_ref[...] + b_ref[...]).astype(BF)
        acc[...] = a_ref[...] + bout_ref[...]

    preact = mm(m_sc[...], flat_rows(win_ref[...])) + bin_ref[...]
    active = gelu_value(preact).astype(BF)
    acc[...] += mm_bt(active, flat_rows(wout_ref[...]))

    @pl.when(step == pl.num_programs(0) - 1)
    def _():
        x_ref[...] = acc[...]


def dense_specs(weights, at, ff):
    devices, _, rows, _ = weights.shape
    steps = ff // 2 // FF_BLOCK
    block = (devices, 1, rows, FF_BLOCK)
    start = at // FF_BLOCK
    return [
        pl.BlockSpec(block, lambda c, *_: (0, c // steps, 0, start + c % steps)),
        pl.BlockSpec(block, lambda c, *_: (0, c // steps, 0, start + steps + c % steps)),
        pl.BlockSpec((1, FF_BLOCK), lambda c, *_: (0, c)),
    ]


def dense_forward(hidden, gain, shift, weights, at, in_bias, out_bias):
    rows, width = hidden.shape
    ff = in_bias.shape[1]
    return call(
        dense_fwd_kernel, (ff // FF_BLOCK,),
        [whole((rows, width)), whole((1, width)), whole((1, width))]
        + dense_specs(weights, at, ff) + [whole((1, width))],
        whole((rows, width)),
        jax.ShapeDtypeStruct((rows, width), F32),
        [pltpu.VMEM((rows, width), BF), pltpu.VMEM((rows, width), F32)],
        4.0 * rows * width * ff, 15.0e6, "dense_fwd",
    )(hidden, gain, shift, weights, weights, in_bias, out_bias)


def dense_bwd_kernel(
    core_ref, dx_ref, a_ref, g_ref, b_ref, win_ref, wout_ref, bin_ref, *rest,
):
    dw_refs = rest[: len(rest) - 8]
    da_ref, dbin_ref, dbout_ref, dg_ref, db_ref, m_sc, low_sc, acc = rest[len(rest) - 8 :]
    step = pl.program_id(0)

    @pl.when(step == 0)
    def _():
        unit, _ = norm_parts(a_ref[...])
        m_sc[...] = (unit * g_ref[...] + b_ref[...]).astype(BF)
        low = dx_ref[...].astype(BF)
        low_sc[...] = low
        dbout_ref[...] = jnp.sum(low.astype(F32), axis=0, keepdims=True)
        acc[...] = jnp.zeros_like(acc)

    normed = m_sc[...]
    low = low_sc[...]
    in_matrix = flat_rows(win_ref[...])
    preact = mm(normed, in_matrix) + bin_ref[...]
    active, slope = gelu_pair(preact)
    preact_grad = (slope * mm(low, flat_rows(wout_ref[...]))).astype(BF)
    dbin_ref[...] = jnp.sum(preact_grad.astype(F32), axis=0, keepdims=True)
    every = slice(None)
    put_grad(dw_refs, core_ref, 1, every, mm_at(low, active.astype(BF)).astype(BF))
    put_grad(dw_refs, core_ref, 0, every, mm_at(normed, preact_grad).astype(BF))
    acc[...] += mm_bt(preact_grad, in_matrix)

    @pl.when(step == pl.num_programs(0) - 1)
    def _():
        unit, scale = norm_parts(a_ref[...])
        hidden_grad, gain_grad, shift_grad = norm_pull(unit, scale, g_ref[...], acc[...])
        da_ref[...] = dx_ref[...] + hidden_grad
        dg_ref[...] = gain_grad
        db_ref[...] = shift_grad


def dense_back(core, incoming, hidden, gain, shift, weights, at, in_bias, devices, split,
               after=()):
    rows, width = hidden.shape
    ff = in_bias.shape[1]
    shapes = grad_shapes(devices, width, ff, split)
    short = jax.ShapeDtypeStruct((1, width), F32)
    made = call(
        dense_bwd_kernel, (ff // FF_BLOCK,),
        [whole((rows, width)), whole((rows, width)), whole((1, width)), whole((1, width))]
        + dense_specs(weights, at, ff),
        [grad_block(shape, FF_BLOCK, lambda c, *_: c) for shape in shapes] + [
            whole((rows, width)), pl.BlockSpec((1, FF_BLOCK), lambda c, *_: (0, c)),
            whole((1, width)), whole((1, width)), whole((1, width)),
        ],
        [jax.ShapeDtypeStruct(shape, BF) for shape in shapes] + [
            jax.ShapeDtypeStruct((rows, width), F32), jax.ShapeDtypeStruct((1, ff), F32),
            short, short, short,
        ],
        [
            pltpu.VMEM((rows, width), BF), pltpu.VMEM((rows, width), BF),
            pltpu.VMEM((rows, width), F32),
        ],
        10.0 * rows * width * ff, 35.0e6, "dense_bwd", after, prefetch=1,
    )(core, incoming, hidden, gain, shift, weights, weights, in_bias)
    return made[: len(shapes)], made[len(shapes) :]


def pick_rows(place_ref, m, expert, capp):
    half = place_ref.shape[2]
    ids = lax.broadcasted_iota(jnp.int32, (capp, half), 0) + expert * capp
    return place_ref[m, 0:1, :] == ids, place_ref[m, 1:2, :] == ids


def as_pick(hit):
    return jnp.where(hit, 1.0, 0.0).astype(BF)


def spread_kernel(capp, own_ref, oth_ref, po_ref, pt_ref, out_ref):
    expert = pl.program_id(0)
    for m in range(own_ref.shape[0]):
        total = None
        for ref, place_ref in ((own_ref, po_ref), (oth_ref, pt_ref)):
            hit0, hit1 = pick_rows(place_ref, m, expert, capp)
            part = mm(as_pick(hit0 | hit1), ref[m])
            total = part if total is None else total + part
        out_ref[0, m * capp : (m + 1) * capp, :] = total.astype(BF)


def spread_rows(own, oth, place_own, place_oth, experts, capp):
    micro, half, width = own.shape
    slots = micro * capp
    (out,) = call(
        functools.partial(spread_kernel, capp), (experts,),
        [whole(own.shape), whole(oth.shape), whole(place_own.shape), whole(place_oth.shape)],
        [pl.BlockSpec((1, slots, width), lambda e: (e, 0, 0))],
        [jax.ShapeDtypeStruct((experts, slots, width), BF)],
        [], 4.0 * experts * slots * half * width, 9.0e6, "spread",
    )(own, oth, place_own, place_oth)
    return out


def moe_kernel(
    capp,
    rb_own0, rb_own1, rb_oth0, rb_oth1, og_ref, po_ref, pt_ref, w_ref,
    win_ref, wout_ref, bin_ref, bout_ref,
    y_ref, r_ref, d_ref, dw_ref, dbin_ref, dbout_ref,
    b_sc, dy_sc, w_sc, y_acc, r_acc,
):
    micro = 2
    expert = pl.program_id(0)
    chunk = pl.program_id(1)
    last_chunk = chunk == pl.num_programs(1) - 1
    rb_all = ((rb_own0, rb_oth0), (rb_own1, rb_oth1))

    @pl.when(chunk == 0)
    def _():
        for m in range(micro):
            slots = slice(m * capp, (m + 1) * capp)
            rows = gate = None
            for side, place_ref in enumerate((po_ref, pt_ref)):
                hit0, hit1 = pick_rows(place_ref, m, expert, capp)
                part = mm(as_pick(hit0 | hit1), rb_all[m][side][...])
                weight = jnp.sum(
                    jnp.where(hit0, w_ref[m, 2 * side : 2 * side + 1, :], 0.0)
                    + jnp.where(hit1, w_ref[m, 2 * side + 1 : 2 * side + 2, :], 0.0),
                    axis=-1, keepdims=True,
                )
                rows = part if side == 0 else rows + part
                gate = weight if side == 0 else gate + weight
            b_sc[slots, :] = rows.astype(BF)
            dy_sc[slots, :] = (og_ref[0, slots, :].astype(F32) * gate).astype(BF)
            w_sc[slots, :] = jnp.broadcast_to(gate, (capp, w_sc.shape[1]))

    tokens = b_sc[...]
    low = dy_sc[...]
    preact = mm(tokens, win_ref[...]) + bin_ref[0]
    active, slope = gelu_pair(preact)
    active = active.astype(BF)
    preact_grad = (slope * mm(low, wout_ref[...])).astype(BF)
    dbin_ref[0] = jnp.sum(preact_grad.astype(F32), axis=0, keepdims=True)
    result = mm_bt(active, wout_ref[...])
    rows_grad = mm_bt(preact_grad, win_ref[...])
    every = slice(None)
    put_grad((dw_ref,), None, 1, every, mm_at(low, active).astype(BF))
    put_grad((dw_ref,), None, 0, every, mm_at(tokens, preact_grad).astype(BF))

    @pl.when(chunk == 0)
    def _():
        y_acc[...] = jnp.zeros_like(y_acc)
        r_acc[...] = jnp.zeros_like(r_acc)

    @pl.when(jnp.logical_not(last_chunk))
    def _():
        y_acc[...] += result
        r_acc[...] += rows_grad

    @pl.when(last_chunk)
    def _():
        dbout_ref[0] = jnp.sum(dy_sc[...].astype(F32), axis=0, keepdims=True)
        total = y_acc[...] + result + 0.5 * bout_ref[0]
        dots = jnp.sum(og_ref[0].astype(F32) * total, axis=-1, keepdims=True)
        high = dots.astype(BF)
        rest = dots - high.astype(F32)
        mid = rest.astype(BF)
        tiny = (rest - mid.astype(F32)).astype(BF)
        lanes = lax.broadcasted_iota(jnp.int32, d_ref.shape[1:], 1)
        zero = jnp.zeros(d_ref.shape[1:], BF)
        d_ref[0] = jnp.where(
            lanes == expert, high,
            jnp.where(lanes == 8 + expert, mid, jnp.where(lanes == 16 + expert, tiny, zero)),
        )
        y_ref[0] = (w_sc[:, 0:1] * total).astype(BF)
        r_ref[0] = (r_acc[...] + rows_grad).astype(BF)


def mixture(rows_own, rows_oth, grad_rows, place_own, place_oth, gates, weights, in_bias,
            out_bias, capp, devices):
    half, width = rows_own[0].shape
    experts, slots, _ = grad_rows.shape
    ff = in_bias.shape[2]
    block = EXPERT_BLOCK
    steps = ff // block
    blocks = experts * steps
    w_block = (width, block)
    flat = (half, width)
    (shape,) = grad_shapes(devices, width, experts * ff, False)
    by_expert = pl.BlockSpec((1, slots, width), lambda e, c: (e, 0, 0))
    return call(
        functools.partial(moe_kernel, capp),
        (experts, steps),
        [
            whole(flat), whole(flat), whole(flat), whole(flat), by_expert,
            whole(place_own.shape), whole(place_oth.shape), whole(gates.shape),
            pl.BlockSpec(w_block, lambda e, c: (0, e * steps + c)),
            pl.BlockSpec(w_block, lambda e, c: (0, blocks + e * steps + c)),
            pl.BlockSpec((1, 1, block), lambda e, c: (e, 0, c)),
            pl.BlockSpec((1, 1, width), lambda e, c: (e, 0, 0)),
        ],
        [
            by_expert, by_expert, pl.BlockSpec((1, slots, 128), lambda e, c: (e, 0, 0)),
            grad_block(shape, block, lambda e, c: e * steps + c),
            pl.BlockSpec((1, 1, block), lambda e, c: (e, 0, c)),
            pl.BlockSpec((1, 1, width), lambda e, c: (e, 0, 0)),
        ],
        [
            jax.ShapeDtypeStruct((experts, slots, width), BF),
            jax.ShapeDtypeStruct((experts, slots, width), BF),
            jax.ShapeDtypeStruct((experts, slots, 128), BF),
            jax.ShapeDtypeStruct(shape, BF),
            jax.ShapeDtypeStruct((experts, 1, ff), F32),
            jax.ShapeDtypeStruct((experts, 1, width), F32),
        ],
        [
            pltpu.VMEM((slots, width), BF), pltpu.VMEM((slots, width), BF),
            pltpu.VMEM((slots, 128), F32),
            pltpu.VMEM((slots, width), F32), pltpu.VMEM((slots, width), F32),
        ],
        12.0 * slots * experts * width * ff + 4.0 * experts * slots * half * width,
        60.0e6, "experts",
    )(*rows_own, *rows_oth, grad_rows, place_own, place_oth, gates, weights, weights,
      in_bias, out_bias)


def collect_kernel(capp, jobs, *refs):
    picks = {}
    for m, place, source, out, kind in jobs:
        rows_ref, out_ref = refs[source], refs[out]
        experts = rows_ref.shape[0]
        half = refs[place].shape[1]
        if (m, place) not in picks:
            hits = []
            for expert in range(experts):
                ids = lax.broadcasted_iota(jnp.int32, (half, capp), 1) + expert * capp
                hit = (refs[place][m, :, 0:1] == ids) | (refs[place][m, :, 1:2] == ids)
                hits.append(as_pick(hit))
            picks[m, place] = hits
        total = None
        for expert, pick in enumerate(picks[m, place]):
            rows = rows_ref[expert, m * capp : (m + 1) * capp, :]
            if kind == "dots":
                part = lax.dot_general(
                    rows, pick, (((0,), (1,)), ((), ())), preferred_element_type=F32
                )
            else:
                part = mm(pick, rows)
            total = part if total is None else total + part
        if kind == "dots":
            total = total[0:8] + total[8:16] + total[16:24]
        if len(out_ref.shape) == 3:
            out_ref[m] = total.astype(out_ref.dtype)
        else:
            out_ref[...] = total.astype(out_ref.dtype)


def collect(capp, arrays, outs, jobs, name, after=()):
    experts, slots, width = arrays[-1].shape
    return call(
        functools.partial(collect_kernel, capp, tuple(jobs)), (1,),
        [whole(value.shape) for value in arrays], [whole(shape) for shape, _ in outs],
        [jax.ShapeDtypeStruct(shape, kind) for shape, kind in outs], [],
        2.0 * len(jobs) * arrays[0].shape[1] * experts * capp * width, 8.0e6, name, after,
    )(*arrays)


def gate_bwd_kernel(
    a_ref, og_ref, held_ref, ro_ref, rr_ref, do_ref, dr_ref, gp_ref, rt_ref, g_ref, b_ref,
    sent_ref, da_ref, drt_ref, dg_ref, db_ref,
):
    after = a_ref[...]
    incoming = og_ref[0].astype(F32)
    sent_ref[...] = held_ref[...]
    gates = gp_ref[...]
    found = do_ref[0] + dr_ref[0]
    spread = jnp.where(
        lax.broadcasted_iota(jnp.int32, (found.shape[0], gates.shape[1]), 0)
        == lax.broadcasted_iota(jnp.int32, (found.shape[0], gates.shape[1]), 1),
        1.0, 0.0,
    )
    gate_grad = lax.dot_general(
        found, spread, (((0,), (0,)), ((), ())), precision=EXACT, preferred_element_type=F32
    )
    logit_grad = gates * (gate_grad - jnp.sum(gates * gate_grad, axis=-1, keepdims=True))
    unit, scale = norm_parts(after)
    normed = unit * g_ref[...] + b_ref[...]
    drt_ref[...] = lax.dot_general(
        logit_grad, normed, (((0,), (0,)), ((), ())), precision=EXACT, preferred_element_type=F32
    )
    normed_grad = ro_ref[0].astype(F32) + rr_ref[...].astype(F32)
    normed_grad += lax.dot_general(
        logit_grad, rt_ref[...], (((1,), (1,)), ((), ())), precision=EXACT,
        preferred_element_type=F32,
    )
    hidden_grad, gain_grad, shift_grad = norm_pull(unit, scale, g_ref[...], normed_grad)
    da_ref[...] = incoming + hidden_grad
    dg_ref[...] = gain_grad
    db_ref[...] = shift_grad


def gate_back(after, incoming, held, r_own, r_got, d_own, d_got, gates, router, gain, shift,
              which, behind=()):
    block, width = after.shape
    lanes = gates.shape[1]
    one = pl.BlockSpec((1, block, width), lambda *_: (which, 0, 0))
    dots = pl.BlockSpec((1, 8, block), lambda *_: (which, 0, 0))
    flat = whole((block, width))
    low = whole((block, lanes))
    return call(
        gate_bwd_kernel, (1,),
        [
            flat, one, whole(held.shape), one, flat, dots, dots, low,
            whole((width, lanes)), whole((1, width)), whole((1, width)),
        ],
        [whole(held.shape), flat, whole((lanes, width)), whole((1, width)), whole((1, width))],
        [
            jax.ShapeDtypeStruct(held.shape, BF),
            jax.ShapeDtypeStruct((block, width), F32),
            jax.ShapeDtypeStruct((lanes, width), F32),
            jax.ShapeDtypeStruct((1, width), F32),
            jax.ShapeDtypeStruct((1, width), F32),
        ],
        [], 4.0 * block * width * lanes, 7.0e6, "gate_bwd", behind,
    )(after, incoming, held, r_own, r_got, d_own, d_got, gates, router, gain, shift)


def swap(value):
    return lax.ppermute(value, "tensor", [(0, 1), (1, 0)])


def in_order(mine, other, axis):
    first = lax.axis_index("tensor") == 0
    return jnp.stack([jnp.where(first, mine, other), jnp.where(first, other, mine)], axis=axis)


def gather_rows(share):
    return lax.all_gather(share, "dp", axis=0, tiled=True)


def ring_chip(place, chips):
    half = chips // 2
    even = 2 * place
    odd = 2 * (chips - 1 - place) + 1
    if isinstance(place, int):
        return even if place < half else odd
    return jnp.where(place < half, even, odd)


def ring_add(kind, refs):
    def chunk(grads, given):
        return grads[0].astype(F32) + given[0].astype(F32)

    if kind == 0:
        grads, given, ahead, behind = refs
        total = chunk(grads, given).astype(BF)
        ahead[...] = total[0]
        behind[...] = total[1]
    elif kind == 3:
        grads, given, got_a, got_b, out = refs
        out[...] = chunk(grads, given) + (got_a[...].astype(F32) + got_b[...].astype(F32))
    elif kind == 4:
        one, two, out = refs
        out[...] = one[...] + two[...]
    else:
        grads_a, given_a, grads_b, given_b, got_a, got_b, ahead, behind = refs
        one, two = chunk(grads_a, given_a), chunk(grads_b, given_b)
        if kind == 1:
            ahead[0] = (one[0] + got_a[...].astype(F32)).astype(BF)
            ahead[1] = one[1].astype(BF)
            behind[0] = two[0].astype(BF)
            behind[1] = (two[1] + got_b[...].astype(F32)).astype(BF)
        else:
            ahead[...] = (one + got_a[...].astype(F32)).astype(BF)
            behind[...] = (two + got_b[...].astype(F32)).astype(BF)


def step_kernel(plans, _, *refs):
    taken = sum(ins for _, ins, _ in plans)
    at, out_at = 0, taken
    for kind, ins, outs in plans:
        ring_add(kind, refs[at : at + ins] + refs[out_at : out_at + outs])
        at += ins
        out_at += outs


def step_all(chains, after=()):
    live = [chain for chain in chains if not chain.finished()]
    if not live:
        return tuple(after)
    stages = [chain.stage(index) for index, chain in enumerate(live)]
    places = jnp.stack([place for stage in stages for place in stage[1]]).astype(jnp.int32)
    sums = call(
        functools.partial(
            step_kernel, tuple((stage[0], len(stage[2]), len(stage[4])) for stage in stages)
        ),
        (1,), [spec for stage in stages for spec in stage[2]],
        [whole(out.shape) for stage in stages for out in stage[4]],
        [out for stage in stages for out in stage[4]], [], 0, 2.0e6, "ring_add", after,
        prefetch=1,
    )(places, *[value for stage in stages for value in stage[3]])
    at = 0
    for chain, stage in zip(live, stages):
        chain.take(sums[at : at + len(stage[4])])
        at += len(stage[4])
    return tuple(sums[:1])


class RingSum:
    def __init__(self, kept, sent):
        count = lax.axis_size("dp")
        self.chips = count // 2
        self.ring = [ring_chip(place, self.chips) for place in range(self.chips)]
        chip = lax.axis_index("dp") // 2
        self.here = jnp.where(chip % 2 == 0, chip // 2, self.chips - 1 - chip // 2)
        self.kept = kept
        self.away = self.chips // 2
        self.messages = (sent,)
        self.given = lax.ppermute(sent, "dp", [(at, at ^ 1) for at in range(count)])
        self.got = ()
        self.result = None

    def send(self, value, step):
        pairs = [
            (self.ring[at] * 2 + side, self.ring[(at + step) % self.chips] * 2 + side)
            for at in range(self.chips)
            for side in range(2)
        ]
        return lax.ppermute(value, "dp", pairs)

    def finished(self):
        return self.result is not None

    def stage(self, index):
        away = self.away
        chips = [
            ring_chip((self.here + far) % self.chips, self.chips)
            for far in (away, self.chips - away)
        ]
        shape = self.kept.shape[1:]

        def chunk_specs(which):
            slot = 2 * index + which
            return [pl.BlockSpec((1,) + shape, lambda _, at: (at[slot], 0, 0, 0))] * 2

        far = self.chips // 2
        kind = 3 if away == 0 else 0 if away == far else 1 if away == far - 1 else 2
        two_ways = kind in (1, 2)
        in_specs = chunk_specs(0) + (chunk_specs(1) if two_ways else [])
        in_specs += [whole(got.shape) for got in self.got]
        args = [self.kept, self.given] * (2 if two_ways else 1) + list(self.got)
        out = shape if kind else shape[1:]
        outs = [jax.ShapeDtypeStruct(out, F32 if kind == 3 else BF)] * (1 if kind == 3 else 2)
        return kind, chips, in_specs, args, outs

    def take(self, sums):
        if self.away == 0:
            self.result = sums[0]
            self.messages = ()
            return
        self.away -= 1
        self.messages = tuple(sums)
        self.got = (self.send(sums[0], 1), self.send(sums[1], -1))


class PlainSum:
    def __init__(self, grad):
        axis = 1 if grad.ndim == 3 else 0
        done = lax.psum_scatter(grad, "dp", scatter_dimension=axis, tiled=True)
        self.messages = (done,)
        self.result = done.reshape((2,) + done.shape[-2:]).astype(F32)

    def finished(self):
        return True


def hold_kernel(value_ref, out_ref):
    return


def hold(value, after):
    anywhere = pl.BlockSpec(memory_space=pl.ANY)
    return call(
        hold_kernel, (1,), [anywhere], anywhere, jax.ShapeDtypeStruct(value.shape, value.dtype),
        [], 0, 1.0e3, "hold", after, aliases={0: 0},
    )(value)


def expert_out_kernel(sum_ref, in_ref, out_ref):
    experts, ff = in_ref.shape[1], in_ref.shape[2]
    for part, ref in enumerate((in_ref, out_ref)):
        for expert in range(experts):
            ref[:, expert, :] = sum_ref[part, :, expert * ff : (expert + 1) * ff].astype(F32)


def expert_outputs(total, shape, after):
    return call(
        expert_out_kernel, (1,), [whole(total.shape)], [whole(shape)] * 2,
        [jax.ShapeDtypeStruct(shape, F32)] * 2, [], 0, 4.0e6, "expert_out", after,
    )(total)


class PairSum:
    def __init__(self, value):
        self.count = lax.axis_size("dp")
        self.value = value
        self.reach = 1
        self.send()

    def send(self):
        self.messages = (self.value,)
        if self.reach < self.count:
            pairs = [(at, at ^ self.reach) for at in range(self.count)]
            self.got = lax.ppermute(self.value, "dp", pairs)
        elif self.reach == self.count:
            self.got = swap(self.value)
        else:
            self.got = None
            self.messages = ()
        self.reach *= 2

    def finished(self):
        return self.got is None

    def stage(self, index):
        zero = jnp.zeros((), jnp.int32)
        shape = self.value.shape
        return (
            4, [zero, zero], [whole(shape)] * 2, [self.value, self.got],
            [jax.ShapeDtypeStruct(shape, F32)],
        )

    def take(self, sums):
        (self.value,) = sums
        self.send()


def pack_kernel(plan, side_ref, *refs):
    out_ref = refs[-1]
    width = out_ref.shape[1]
    out_ref[...] = jnp.zeros_like(out_ref)
    at = 0
    for inputs, rows, factor, sided in plan:
        total = None
        for which in inputs:
            ref = refs[which]
            value = ref[...].reshape(-1, ref.shape[-1])[:rows]
            total = value if total is None else total + value
        total = total * factor if factor != 1.0 else total
        parts = total.shape[1] // width
        for row in range(rows):
            for part in range(parts):
                piece = total[row : row + 1, part * width : (part + 1) * width]
                place = at + row * parts + part
                if sided:
                    place = place + side_ref[0] * (rows * parts)
                out_ref[pl.ds(place, 1), :] = piece
        at += rows * parts * (2 if sided else 1)


def pack_rows(groups, width):
    arrays, plan, total = [], [], 0
    for values, rows, factor, sided in groups:
        plan.append((tuple(range(len(arrays), len(arrays) + len(values))), rows, factor, sided))
        arrays += values
        total += rows * (values[0].shape[-1] // width) * (2 if sided else 1)
    shape = (round_up(total, 8), width)
    side = lax.axis_index("tensor").reshape(1)
    (out,) = call(
        functools.partial(pack_kernel, tuple(plan)), (1,),
        [whole(value.shape) for value in arrays], [whole(shape)],
        [jax.ShapeDtypeStruct(shape, F32)], [], 0, 3.0e5, "pack", (), prefetch=1,
    )(side, *arrays)
    return out


def out_kernel(a0_ref, a1_ref, y_ref, got_ref, out_ref):
    for m, a_ref in enumerate((a0_ref, a1_ref)):
        total = a_ref[...] + (y_ref[m].astype(F32) + got_ref[m].astype(F32))
        out_ref[m] = total.astype(BF)


def layer_output(hidden, y_own, y_got, after):
    shape = y_own.shape
    (out,) = call(
        out_kernel, (1,),
        [whole(hidden[0].shape)] * 2 + [whole(shape)] * 2, [whole(shape)],
        [jax.ShapeDtypeStruct(shape, BF)], [], 0, 8.0e6, "layer_output", after,
    )(*hidden, y_own, y_got)
    return out


def place_kernel(side_ref, own_ref, got_ref, out_ref):
    images, length = own_ref.shape[1], out_ref.shape[2]
    side = side_ref[0]
    for image in range(images):
        kept = own_ref[:, image, :length, :].astype(out_ref.dtype)
        out_ref[:, side * images + image] = kept
        other = got_ref[:, image, :length, :].astype(out_ref.dtype)
        out_ref[:, (1 - side) * images + image] = other


def place_images(own, got, shape, kind, after):
    micro, images, length, width = shape
    padded = (micro, images // 2, own.size // (micro * (images // 2) * width), width)
    side = lax.axis_index("tensor").reshape(1)
    (out,) = call(
        place_kernel, (micro,),
        [pl.BlockSpec((1,) + padded[1:], lambda m, *_: (m, 0, 0, 0))] * 2,
        [pl.BlockSpec((1,) + shape[1:], lambda m, *_: (m, 0, 0, 0))],
        [jax.ShapeDtypeStruct(shape, kind)], [], 0, 8.0e6, "place", after, prefetch=1,
    )(side, own.reshape(padded), got.reshape(padded))
    return out


def join_sides(mine_first):
    mine = lax.axis_index("tensor")
    kept = lax.dynamic_index_in_dim(mine_first, mine, 0, keepdims=False)
    sent = lax.dynamic_index_in_dim(mine_first, 1 - mine, 0, keepdims=False)
    return kept + swap(sent.astype(BF)).astype(F32)


def own_half(value, axis):
    size = value.shape[axis] // 2
    return lax.dynamic_slice_in_dim(value, lax.axis_index("tensor") * size, size, axis)


def local(
    block_input, norm_gain, row_bias, qkv_weight, qkv_bias, out_weight, mlp_in, mlp_in_bias,
    mlp_out, mlp_out_bias, router, expert_in, expert_in_bias, expert_out, expert_out_bias,
    routes, slot_index, out_grad,
):
    micro, images, length, width = block_input.shape
    experts = router.shape[1]
    share_rows = mlp_in.shape[0]
    own_images = images // 2
    pad = round_up(length, ROW_PAD)
    half = own_images * pad
    rows = micro * half
    capp = round_up(CAP, ROW_PAD)
    side = lax.axis_index("tensor")

    def attn_share(layer):
        return jnp.concatenate(
            [qkv_weight[layer].reshape(share_rows, -1), out_weight[layer]], axis=1
        )

    devices = lax.axis_size("dp")
    first_mine = jnp.concatenate([attn_share(0), attn_share(1), mlp_in, mlp_out], axis=1)
    first_w = lax.all_gather(
        in_order(first_mine, swap(first_mine), 0), "dp", axis=0, tiled=False
    )
    if not whole_tiles(devices, width):
        first_w = jnp.moveaxis(first_w, 0, 1).reshape(1, 2, width, -1)
    dense_at = 4 * width
    expert_w = gather_rows(
        jnp.concatenate(
            [expert_in.reshape(share_rows, -1), expert_out.reshape(share_rows, -1)], axis=1
        )
    )

    biases = jnp.concatenate([qkv_bias.reshape(-1), mlp_in_bias])
    bias_pair = in_order(biases, swap(biases), 0)
    qkv_bias_pair = bias_pair[:, : qkv_bias.size].reshape((2,) + qkv_bias.shape)
    mlp_bias_full = bias_pair[:, qkv_bias.size :].reshape(1, -1)

    def qkv_bias_row(layer):
        pair = qkv_bias_pair[:, layer]
        zero = jnp.zeros_like(pair[:, 0])
        return jnp.concatenate([pair[:, 0], zero, pair[:, 1]], axis=1).reshape(1, -1)

    def padded(value, start):
        part = lax.dynamic_slice_in_dim(value, start, own_images, 1)
        return jnp.pad(part, ((0, 0), (0, 0), (0, pad - length), (0, 0)))

    mine_at = side * own_images
    other_at = (1 - side) * own_images
    hidden = padded(block_input, mine_at).astype(F32).reshape(rows, width)
    grad_own = padded(out_grad, mine_at).reshape(micro, half, width)
    grad_oth = padded(out_grad, other_at).reshape(micro, half, width)

    kept = slot_index < CAP
    place = jnp.where(kept, routes * capp + slot_index, -1)
    pick = jnp.where(kept, routes, -1)

    def lay(value, start):
        part = lax.dynamic_slice_in_dim(value, start, own_images, 1)
        part = jnp.pad(
            part, ((0, 0), (0, 0), (0, pad - length), (0, 0)), constant_values=-1
        )
        return part.reshape(micro, half, 2)

    place_own, place_oth = lay(place, mine_at), lay(place, other_at)
    place_own_rows = jnp.swapaxes(place_own, 1, 2)
    place_oth_rows = jnp.swapaxes(place_oth, 1, 2)
    grad_rows = spread_rows(
        grad_own, grad_oth, place_own_rows, place_oth_rows, experts, capp
    )
    select = lay(pick, mine_at).reshape(rows, 2)
    router_wide = jnp.pad(router, ((0, 0), (0, 128 - experts)))

    def row(vector):
        return vector.reshape(1, -1)

    qkv_one, lse_one, mix_one, after_one = attention_forward(
        hidden, row(norm_gain[0, 0]), row(row_bias[0, 0]), first_w, 0, qkv_bias_row(0),
        row(row_bias[0, 2]), length, pad, 0, micro,
    )
    after_ffn = dense_forward(
        after_one, row(norm_gain[0, 1]), row(row_bias[0, 1]), first_w, dense_at, mlp_bias_full,
        row(mlp_out_bias),
    )
    second = [
        attention_forward(
            after_ffn, row(norm_gain[1, 0]), row(row_bias[1, 0]), first_w, 1, qkv_bias_row(1),
            row(row_bias[1, 2]), length, pad, m, 1,
            (row(norm_gain[1, 1]), row(row_bias[1, 1]), router_wide, select, experts),
        )
        for m in range(micro)
    ]
    qkv_two, lse_two, mix_two, after_two, rows_own, gates, chosen = zip(*second)
    rows_oth = [swap(part) for part in rows_own]
    gate_own = jnp.stack([part[:, :2].T for part in chosen])
    gate_pair = jnp.concatenate([gate_own, swap(gate_own)], axis=1)
    ring = whole_tiles(devices, width)
    core = (lax.axis_index("dp") % 2).reshape(1)
    y_slots, r_slots, d_slots, expert_grad, ein_bias, eout_bias = mixture(
        rows_own, rows_oth, grad_rows, place_own_rows, place_oth_rows, gate_pair, expert_w,
        expert_in_bias.reshape(experts, 1, -1), expert_out_bias.reshape(experts, 1, -1), capp,
        devices,
    )
    group, one, dots = (micro, half, width), (half, width), (micro, 8, half)
    r_oth0, r_oth1, d_oth = collect(
        capp, (place_oth, d_slots, r_slots), ((one, BF), (one, BF), (dots, F32)),
        (
            (0, 0, 2, 3, "rows"), (1, 0, 2, 4, "rows"), (0, 0, 1, 5, "dots"),
            (1, 0, 1, 5, "dots"),
        ),
        "collect_first",
    )
    y_own, y_oth, r_own, d_own = collect(
        capp, (place_own, place_oth, d_slots, r_slots, y_slots),
        ((group, BF), (group, BF), (group, BF), (dots, F32)),
        (
            (0, 0, 3, 7, "rows"), (1, 0, 3, 7, "rows"), (0, 0, 2, 8, "dots"),
            (1, 0, 2, 8, "dots"), (0, 0, 4, 5, "rows"), (1, 0, 4, 5, "rows"),
            (0, 1, 4, 6, "rows"), (1, 1, 4, 6, "rows"),
        ),
        "collect_rest", (r_oth0,),
    )
    d_got = swap(d_oth)
    r_got = swap(r_oth0)
    expert_sum = PlainSum(expert_grad)
    grad_two, gate_parts, cores = [], [], []
    for m, held in enumerate((r_oth1, y_oth)):
        sent, grad_part, *small = gate_back(
            after_two[m], grad_own, held, r_own, r_got, d_own, d_got, gates[m],
            router_wide, row(norm_gain[1, 1]), row(row_bias[1, 1]), m,
            (cores[0][1],) if m else (),
        )
        r_got = swap(sent)
        grad_two.append(grad_part)
        gate_parts.append(small)
        cores.append(
            attention_core_back(
                grad_part, first_w, 1, (qkv_two[m], lse_two[m], half), length, pad, m, (sent,)
            )
        )
    y_got = r_got
    router_parts, gain_parts, shift_parts = (list(pair) for pair in zip(*gate_parts))
    two_grad, (grad_ffn, qb_two, ob_two, gain_two, shift_two) = attention_grad(
        core, grad_two, after_ffn, row(norm_gain[1, 0]), row(row_bias[1, 0]), first_w, 1, cores,
        mix_two, devices, ring, F32,
    )
    sum_two = RingSum(*two_grad) if ring else PlainSum(*two_grad)
    out_own = layer_output(after_two, y_own, y_got, (gain_two,))
    out_got = swap(out_own)
    early = (
            [
                ([gain_two], 1, 1.0, False), (gain_parts, 1, 1.0, False),
                ([shift_two], 1, 1.0, False), (shift_parts, 1, 1.0, False),
                ([ob_two], 1, 1.0, False), ([qb_two], 1, 1.0, False),
                (router_parts, experts, 1.0, False), ([eout_bias], experts, 0.5, False),
                ([ein_bias], experts, 1.0, True),
            ]
    )
    dense_grad, (grad_one, in_bias_grad, out_bias_grad, gain_ffn, shift_ffn) = dense_back(
        core, grad_ffn, after_one, row(norm_gain[0, 1]), row(row_bias[0, 1]), first_w, dense_at,
        mlp_bias_full, devices, ring, sum_two.messages + (out_own,),
    )
    last = step_all([sum_two], (gain_ffn, out_got))
    if ring:
        dense_sum = RingSum(dense_grad[0], hold(dense_grad[1], last))
    else:
        dense_sum = PlainSum(*dense_grad)
    block_output = place_images(out_own, out_got, block_input.shape, BF, last)
    step_all([dense_sum], (block_output,))
    cores = []
    for which in range(2):
        cores.append(
            attention_core_back(
                grad_one, first_w, 0, (qkv_one, lse_one, half), length, pad, which,
                sum_two.messages + dense_sum.messages + (block_output,),
            )
        )
        step_all([sum_two, dense_sum], (cores[-1][1],))
    one_grad, (grad_zero, qb_one, ob_one, gain_one, shift_one) = attention_grad(
        core, (grad_one, grad_one), hidden, row(norm_gain[0, 0]), row(row_bias[0, 0]), first_w,
        0, cores, (mix_one, mix_one), devices, False, BF,
        sum_two.messages + dense_sum.messages,
    )
    last = step_all([sum_two, dense_sum], (qb_one,))
    one_sum = PlainSum(hold(one_grad[0], expert_sum.messages + last))
    late_sum = PairSum(
        pack_rows(
            [
                ([gain_one], 1, 1.0, False), ([gain_ffn], 1, 1.0, False),
                ([shift_one], 1, 1.0, False), ([shift_ffn], 1, 1.0, False),
                ([ob_one], 1, 1.0, False), ([qb_one], 1, 1.0, False),
                ([in_bias_grad], 1, 1.0, False), ([out_bias_grad], 1, 1.0, False),
            ] + early,
            width,
        )
    )
    expert_total = expert_sum.messages[0].reshape((2, share_rows, -1))
    expert_grads = expert_outputs(expert_total, expert_in.shape, last)
    last = (expert_grads[0],)
    grad_got = swap(grad_zero)
    for turn in range(devices):
        last = step_all([sum_two, dense_sum, late_sum], last)
        if turn == 2:
            input_grad = place_images(grad_zero, grad_got, block_input.shape, F32, last)
            last = (input_grad,)

    one_done = join_sides(one_sum.result)
    joined = join_sides(
        jnp.concatenate(
            [
                sum_two.result[:, None],
                jnp.moveaxis(dense_sum.result.reshape(2, share_rows, 2, -1), 2, 0),
            ],
            axis=1,
        )
    )
    attn_grads, dense_done = [one_done, joined[0]], joined[1:]
    split_at = 3 * width // 2

    late = late_sum.value
    ff_rows = in_bias_grad.shape[1] // width
    early = late[9 + ff_rows :]
    gain_sum = jnp.concatenate([late[0:2], early[0:2]])
    shift_sum = jnp.concatenate([late[2:5], early[2:5]])
    qb_sum = jnp.stack([late[5:8], early[5:8]]).reshape(2, 2, 3, width // 2)
    qb_sum = lax.dynamic_index_in_dim(qb_sum, side, 1, keepdims=False)
    in_bias_sum = late[8 : 8 + ff_rows]
    out_bias_sum = late[8 + ff_rows]
    at = 8 + experts
    router_sum = early[8:at]
    eout_sum = early[at : at + experts]
    at += experts
    ein_rows = expert_in_bias.size // width
    ein_sum = lax.dynamic_slice_in_dim(early, at + side * ein_rows, ein_rows, 0)
    return (
        block_output,
        input_grad,
        gain_sum.reshape(norm_gain.shape),
        shift_sum.reshape(row_bias.shape),
        jnp.stack([part[:, :split_at] for part in attn_grads]).reshape(qkv_weight.shape),
        jnp.stack([qb_sum[:, 0], qb_sum[:, 2]], axis=1),
        jnp.stack([part[:, split_at:] for part in attn_grads]),
        dense_done[0],
        own_half(in_bias_sum.reshape(-1), 0),
        dense_done[1],
        out_bias_sum.reshape(-1),
        router_sum.T,
        expert_grads[0],
        ein_sum.reshape(expert_in_bias.shape),
        expert_grads[1],
        eout_sum.reshape(experts, width),
    )


def solution(mesh):
    return jax.shard_map(
        local,
        mesh=mesh,
        in_specs=(
            P(None, "dp", None, None), P(), P(), P(None, "dp", None, "tensor"),
            P(None, None, "tensor"), P(None, "dp", "tensor"), P("dp", "tensor"), P("tensor"),
            P("dp", "tensor"), P(), P(), P("dp", None, "tensor"), P(None, "tensor"),
            P("dp", None, "tensor"), P(), P(None, "dp", None, None), P(None, "dp", None, None),
            P(None, "dp", None, None),
        ),
        out_specs=(
            P(None, "dp", None, None), P(None, "dp", None, None), P(), P(),
            P(None, "dp", None, "tensor"), P(None, None, "tensor"), P(None, "dp", "tensor"),
            P("dp", "tensor"), P("tensor"), P("dp", "tensor"), P(), P(),
            P("dp", None, "tensor"), P(None, "tensor"), P("dp", None, "tensor"), P(),
        ),
        check_vma=False,
    )
```

```python
import functools

import jax
import jax.numpy as jnp
from jax import lax
from jax.experimental import pallas as pl
from jax.experimental.pallas import tpu as pltpu
from jax.sharding import PartitionSpec as P

HD = 64
CAP = 295
NORM_EPS = 1e-06
EXACT = lax.Precision.HIGHEST
BF = jnp.bfloat16
F32 = jnp.float32
VMEM_LIMIT = 58 * 1024 * 1024
FF_BLOCK = 512
EXPERT_BLOCK = 1536
ROW_PAD = 16
GELU_SLOPE = 0.7978845608028654
GELU_CUBE = 0.044715


def round_up(value, unit):
    return -(-value // unit) * unit


def mm(left, right):
    return jnp.dot(left, right, preferred_element_type=F32)


def mm_bt(left, right):
    return lax.dot_general(left, right, (((1,), (1,)), ((), ())), preferred_element_type=F32)


def mm_at(left, right):
    return lax.dot_general(left, right, (((0,), (0,)), ((), ())), preferred_element_type=F32)


def norm_parts(hidden):
    center = jnp.mean(hidden, axis=-1, keepdims=True)
    centred = hidden - center
    spread = jnp.mean(centred * centred, axis=-1, keepdims=True)
    scale = lax.rsqrt(spread + NORM_EPS)
    return centred * scale, scale


def norm_pull(unit, scale, gain, incoming):
    wide = incoming * gain
    mean_wide = jnp.mean(wide, axis=-1, keepdims=True)
    mean_dot = jnp.mean(wide * unit, axis=-1, keepdims=True)
    hidden_grad = scale * (wide - mean_wide - unit * mean_dot)
    gain_grad = jnp.sum(incoming * unit, axis=0, keepdims=True)
    shift_grad = jnp.sum(incoming, axis=0, keepdims=True)
    return hidden_grad, gain_grad, shift_grad


def gelu_pair(preact):
    square = preact * preact
    inner = GELU_SLOPE * preact * (1.0 + GELU_CUBE * square)
    bend = jnp.tanh(inner)
    half = 0.5 * (1.0 + bend)
    active = preact * half
    slope = half + 0.5 * preact * (1.0 - bend * bend) * (
        GELU_SLOPE * (1.0 + 3.0 * GELU_CUBE * square)
    )
    return active, slope


def gelu_value(preact):
    square = preact * preact
    inner = GELU_SLOPE * preact * (1.0 + GELU_CUBE * square)
    return 0.5 * preact * (1.0 + jnp.tanh(inner))


def call(kernel, grid, in_specs, out_specs, out_shape, scratch, flops, traffic, name,
         after=(), prefetch=0, aliases=None):
    taken = prefetch + len(in_specs)
    skipped = len(after)

    def body(*refs):
        kernel(*refs[:taken], *refs[taken + skipped :])

    made = pl.pallas_call(
        body,
        grid_spec=pltpu.PrefetchScalarGridSpec(
            num_scalar_prefetch=prefetch,
            grid=grid,
            in_specs=list(in_specs) + [pl.BlockSpec(memory_space=pl.ANY)] * skipped,
            out_specs=out_specs,
            scratch_shapes=scratch,
        ),
        out_shape=out_shape,
        input_output_aliases=aliases or {},
        name=name,
        compiler_params=pltpu.CompilerParams(
            vmem_limit_bytes=VMEM_LIMIT,
            dimension_semantics=("arbitrary",) * len(grid),
        ),
        cost_estimate=pl.CostEstimate(
            flops=int(flops), bytes_accessed=int(traffic), transcendentals=0
        ),
    )
    return lambda *args: made(*args, *after)


def whole_tiles(devices, width):
    return (width // devices) % ROW_PAD == 0


def grad_shapes(devices, width, columns, split):
    if not whole_tiles(devices, width):
        return [(2, width, columns)]
    if split:
        return [(devices // 2, 2, width // devices, columns)] * 2
    return [(devices, 2, width // devices, columns)]


def grad_block(shape, columns, index):
    block = shape[:-1] + (columns,)
    zeros = (0,) * (len(shape) - 1)
    return pl.BlockSpec(block, lambda *at: zeros + (index(*at),))


def put_grad(refs, core_ref, part, cols, value):
    ref = refs[0]
    if len(refs) == 2:
        pieces = value.reshape(ref.shape[0], 2, ref.shape[2], value.shape[1])
        core = core_ref[0]

        @pl.when(core == 0)
        def _():
            refs[0][:, part, :, cols] = pieces[:, 0]
            refs[1][:, part, :, cols] = pieces[:, 1]

        @pl.when(core != 0)
        def _():
            refs[0][:, part, :, cols] = pieces[:, 1]
            refs[1][:, part, :, cols] = pieces[:, 0]
    elif len(ref.shape) == 3:
        ref[part, :, cols] = value
    else:
        ref[:, part, :, cols] = value.reshape(ref.shape[0], ref.shape[2], value.shape[1])


def flat_rows(value):
    return value.reshape(-1, value.shape[-1])


def weight_spec(weights, sides, columns, index):
    devices, _, rows, _ = weights.shape
    return pl.BlockSpec(
        (devices, sides, rows, columns), index, pipeline_mode=pl.Buffered(1)
    )


def whole(shape):
    zeros = (0,) * len(shape)
    return pl.BlockSpec(shape, lambda *_: zeros, pipeline_mode=pl.Buffered(1))


def rows_of(block, width):
    return pl.BlockSpec((block, width), lambda step, *_: (step, 0))


def half_of(value, block, which):
    at = which if value.shape[0] > block else 0
    rest = (0,) * (value.ndim - 1)
    return pl.BlockSpec((block,) + value.shape[1:], lambda *_: (at,) + rest)


def attn_fwd_kernel(
    length, pad, heads, router_on,
    h_ref, g_ref, b_ref, w_ref, qb_ref, ob_ref, *rest,
):
    if router_on:
        g2_ref, b2_ref, rt_ref, sel_ref = rest[:4]
        qkv_ref, lse_ref, o_ref, a_ref, rb_ref, gp_ref, wt_ref = rest[4:]
    else:
        qkv_ref, lse_ref, o_ref, a_ref = rest
    width = h_ref.shape[1]
    images = h_ref.shape[0] // pad
    hidden = h_ref[...]
    unit, _ = norm_parts(hidden)
    normed = (unit * g_ref[...] + b_ref[...]).astype(BF)
    third = width // 2
    for t in range(2):
        cols = slice(t * 3 * third, (t + 1) * 3 * third)
        matrix = flat_rows(w_ref[:, t, :, : 3 * third])
        qkv_ref[:, cols] = (mm(normed, matrix) + qb_ref[:, cols]).astype(BF)
    pairs = heads // 2
    lane = lax.broadcasted_iota(jnp.int32, (pad, 2 * HD), 1)
    key_row = lax.broadcasted_iota(jnp.int32, (pad, pad), 0)

    def pair_step(step, carry):
        image = step // pairs
        pair = step % pairs
        rows = pl.ds(pl.multiple_of(image * pad, ROW_PAD), pad)

        def col(part):
            side = pair // (pairs // 2)
            at = (side * 3 + part) * (width // 2) + (pair % (pairs // 2)) * 2 * HD
            return pl.ds(pl.multiple_of(at, 2 * HD), 2 * HD)

        place = pl.ds(pl.multiple_of(pair * 2 * HD, 2 * HD), 2 * HD)

        query = qkv_ref[rows, col(0)] * HD ** (-0.5)
        key = qkv_ref[rows, col(1)]
        value = qkv_ref[rows, col(2)]
        mixed = []
        for half in range(2):
            mine = (lane >= HD) if half else (lane < HD)
            scores = mm_bt(key, jnp.where(mine, query, 0).astype(BF))
            scores = jnp.where(key_row < length, scores, -1e30)
            top = jnp.max(scores, axis=0, keepdims=True)
            weights = jnp.exp(scores - top)
            total = jnp.sum(weights, axis=0, keepdims=True)
            probs = (weights * (1.0 / total)).astype(BF)
            mixed.append(mm_at(probs, value))
            lse_ref[image, pl.ds(pair * 2 + half, 1), :] = top + jnp.log(total)
        o_ref[rows, place] = jnp.where(lane < HD, mixed[0], mixed[1]).astype(BF)
        return carry

    lax.fori_loop(0, images * pairs, pair_step, 0, unroll=6)
    out_matrix = jnp.concatenate(
        [flat_rows(w_ref[:, t, :, 3 * third :]) for t in range(2)], axis=1
    )
    after = hidden + mm_bt(o_ref[...], out_matrix) + ob_ref[...]
    a_ref[...] = after
    if router_on:
        unit2, _ = norm_parts(after)
        normed2 = unit2 * g2_ref[...] + b2_ref[...]
        rb_ref[...] = normed2.astype(BF)
        logits = jnp.dot(normed2, rt_ref[...], precision=EXACT, preferred_element_type=F32)
        lanes = lax.broadcasted_iota(jnp.int32, logits.shape, 1)
        live = lanes < router_on
        logits = jnp.where(live, logits, -1e30)
        gates = jnp.exp(logits - jnp.max(logits, axis=-1, keepdims=True))
        gates = gates / jnp.sum(gates, axis=-1, keepdims=True)
        gates = jnp.where(live, gates, 0.0)
        gp_ref[...] = gates
        first = jnp.sum(jnp.where(lanes == sel_ref[:, 0:1], gates, 0.0), axis=-1, keepdims=True)
        second = jnp.sum(jnp.where(lanes == sel_ref[:, 1:2], gates, 0.0), axis=-1, keepdims=True)
        wt_ref[...] = jnp.where(lanes == 0, first, jnp.where(lanes == 1, second, 0.0))


def attention_forward(
    hidden, gain, shift, weights, layer, qkv_bias, out_bias, length, pad, start, count,
    router=None,
):
    micro = 2
    rows, width = hidden.shape
    heads = width // HD
    block = rows // micro
    lse_rows = round_up(heads, 8)
    images = block // pad
    made = count * block
    in_specs = [
        pl.BlockSpec((block, width), lambda step: (start + step, 0)),
        whole((1, width)), whole((1, width)),
        weight_spec(weights, 2, 2 * width, lambda *_: (0, 0, 0, layer)),
        whole((1, 3 * width)), whole((1, width)),
    ]
    args = [hidden, gain, shift, weights, qkv_bias, out_bias]
    out_specs = [
        rows_of(block, 3 * width),
        pl.BlockSpec((images, lse_rows, pad), lambda step: (step, 0, 0)),
        rows_of(block, width),
        rows_of(block, width),
    ]
    out_shape = [
        jax.ShapeDtypeStruct((made, 3 * width), BF),
        jax.ShapeDtypeStruct((count * images, lse_rows, pad), F32),
        jax.ShapeDtypeStruct((made, width), BF),
        jax.ShapeDtypeStruct((made, width), F32),
    ]
    router_on = 0
    if router is not None:
        gain2, shift2, router_wide, select, router_on = router
        lanes = router_wide.shape[1]
        in_specs += [
            whole((1, width)), whole((1, width)), whole((width, lanes)),
            pl.BlockSpec((block, 2), lambda step: (start + step, 0)),
        ]
        args += [gain2, shift2, router_wide, select]
        out_specs += [rows_of(block, width), rows_of(block, lanes), rows_of(block, lanes)]
        out_shape += [
            jax.ShapeDtypeStruct((made, width), BF),
            jax.ShapeDtypeStruct((made, lanes), F32),
            jax.ShapeDtypeStruct((made, lanes), F32),
        ]
    return call(
        functools.partial(attn_fwd_kernel, length, pad, heads, router_on),
        (count,), in_specs, out_specs, out_shape, [],
        8.0 * made * width * width + 16.0 * made * pad * width, 12.0e6, "attn_fwd",
    )(*args)


def attn_core_kernel(
    length, pad, heads, da_ref, wo_ref, qkv_ref, lse_ref, dqkv_ref, low_ref, grad_sc,
):
    width = da_ref.shape[1]
    images = da_ref.shape[0] // pad
    pairs = heads // 2
    low = da_ref[...].astype(BF)
    low_ref[...] = low
    out_matrix = jnp.concatenate([flat_rows(wo_ref[:, t]) for t in range(2)], axis=1)
    grad_sc[...] = mm(low, out_matrix).astype(BF)
    lane = lax.broadcasted_iota(jnp.int32, (pad, 2 * HD), 1)
    key_row = lax.broadcasted_iota(jnp.int32, (pad, pad), 0)

    def pair_step(step, carry):
        image = step // pairs
        pair = step % pairs
        rows = pl.ds(pl.multiple_of(image * pad, ROW_PAD), pad)

        def col(part):
            side = pair // (pairs // 2)
            at = (side * 3 + part) * (width // 2) + (pair % (pairs // 2)) * 2 * HD
            return pl.ds(pl.multiple_of(at, 2 * HD), 2 * HD)

        place = pl.ds(pl.multiple_of(pair * 2 * HD, 2 * HD), 2 * HD)

        query = (qkv_ref[rows, col(0)] * HD ** (-0.5)).astype(BF)
        key = qkv_ref[rows, col(1)]
        value = qkv_ref[rows, col(2)]
        mixed = grad_sc[rows, place]
        key_turned = key.T
        parts = []
        for half in range(2):
            mine = (lane >= HD) if half else (lane < HD)
            scores = mm_bt(key, jnp.where(mine, query, 0).astype(BF))
            total = lse_ref[image, pl.ds(pair * 2 + half, 1), :]
            probs = jnp.where(key_row < length, jnp.exp(scores - total), 0.0)
            probs_grad = mm_bt(value, jnp.where(mine, mixed, 0).astype(BF))
            product = probs * probs_grad
            delta = jnp.sum(product, axis=0, keepdims=True)
            score_grad = (product - probs * delta).astype(BF)
            parts.append((
                mm(key_turned, score_grad) * HD ** (-0.5),
                mm(score_grad, query),
                mm(probs.astype(BF), mixed),
            ))
        turned = lax.broadcasted_iota(jnp.int32, (2 * HD, pad), 0)
        query_grad = jnp.where(turned < HD, parts[0][0], parts[1][0])
        dqkv_ref[rows, col(0)] = query_grad.T.astype(BF)
        for part in range(1, 3):
            dqkv_ref[rows, col(part)] = jnp.where(
                lane < HD, parts[0][part], parts[1][part]
            ).astype(BF)
        return carry

    lax.fori_loop(0, images * pairs, pair_step, 0, unroll=6)


def attention_core_back(incoming, weights, layer, stored, length, pad, which, after=()):
    qkv, lse, block = stored
    width = incoming.shape[1]
    heads = width // HD
    images = block // pad
    return call(
        functools.partial(attn_core_kernel, length, pad, heads),
        (1,),
        [
            half_of(incoming, block, which),
            weight_spec(weights, 2, width // 2, lambda *_: (0, 0, 0, 4 * layer + 3)),
            half_of(qkv, block, which),
            half_of(lse, images, which),
        ],
        [whole((block, 3 * width)), whole((block, width))],
        [
            jax.ShapeDtypeStruct((block, 3 * width), BF),
            jax.ShapeDtypeStruct((block, width), BF),
        ],
        [pltpu.VMEM((block, width), BF)],
        2.0 * block * width * width + 20.0 * block * pad * width * 4, 8.0e6, "attn_core",
        after,
    )(incoming, weights, qkv, lse)


def attn_grad_kernel(
    core_ref, da0_ref, da1_ref, h_ref, g_ref, b_ref, w_ref, dq0_ref, dq1_ref,
    low0_ref, low1_ref, o0_ref, o1_ref, *rest,
):
    dw_refs = rest[: len(rest) - 7]
    dh_ref, dqb_ref, dob_ref, dg_ref, db_ref, n_sc, acc = rest[len(rest) - 7 :]
    step = pl.program_id(0)
    block = dq0_ref.shape[0]
    wide = dq0_ref.shape[1]
    gain = g_ref[...]
    half = (slice(0, block), slice(block, 2 * block))

    @pl.when(step == 0)
    def _():
        unit, _ = norm_parts(h_ref[...])
        n_sc[...] = (unit * gain + b_ref[...]).astype(BF)
        acc[...] = jnp.zeros_like(acc)
        dob_ref[...] = jnp.sum(low0_ref[...].astype(F32), axis=0, keepdims=True) + jnp.sum(
            low1_ref[...].astype(F32), axis=0, keepdims=True
        )

    matrix = flat_rows(w_ref[:, 0, :, :wide])
    piece = sums = mix = None
    sides = ((dq0_ref, low0_ref, o0_ref), (dq1_ref, low1_ref, o1_ref))
    for side, (dq_ref, low_ref, o_ref) in enumerate(sides):
        grads = dq_ref[...]
        acc[half[side], :] += mm_bt(grads, matrix)
        outer = mm_at(n_sc[half[side], :], grads)
        total = jnp.sum(grads.astype(F32), axis=0, keepdims=True)
        out = mm_at(low_ref[...], o_ref[...])
        piece = outer if side == 0 else piece + outer
        sums = total if side == 0 else sums + total
        mix = out if side == 0 else mix + out
    put_grad(dw_refs, core_ref, 0, slice(0, wide), piece.astype(BF))
    put_grad(dw_refs, core_ref, 0, slice(wide, w_ref.shape[3]), mix.astype(BF))
    dqb_ref[...] = sums

    @pl.when(step == pl.num_programs(0) - 1)
    def _():
        unit, scale = norm_parts(h_ref[...])
        for side, da_ref in enumerate((da0_ref, da1_ref)):
            hidden_grad, gain_grad, shift_grad = norm_pull(
                unit[half[side]], scale[half[side]], gain, acc[half[side], :]
            )
            dh_ref[half[side], :] = (da_ref[...] + hidden_grad).astype(dh_ref.dtype)
            if side == 0:
                dg_ref[...] = gain_grad
                db_ref[...] = shift_grad
            else:
                dg_ref[...] += gain_grad
                db_ref[...] += shift_grad


def attention_grad(
    core, incoming, hidden, gain, shift, weights, layer, cores, mixed, devices, split, kind,
    after=(),
):
    rows, width = hidden.shape
    shapes = grad_shapes(devices, width, 2 * width, split)
    block = rows // 2
    short = jax.ShapeDtypeStruct((1, width), F32)
    third = width // 2

    def side_block(shape):
        if len(shape) == 3:
            return pl.BlockSpec((1,) + shape[1:], lambda t, *_: (t, 0, 0))
        return pl.BlockSpec(
            (shape[0], 1) + shape[2:], lambda t, *_: (0, t, 0, 0)
        )

    def columns_of(value, which, columns):
        at = which if value.shape[0] > block else 0
        return pl.BlockSpec((block, columns), lambda t, *_: (at, t))

    made = call(
        attn_grad_kernel, (2,),
        [
            half_of(incoming[0], block, 0), half_of(incoming[1], block, 1),
            whole((rows, width)), whole((1, width)), whole((1, width)),
            pl.BlockSpec(
                (weights.shape[0], 1, weights.shape[2], 2 * width),
                lambda t, *_: (0, t, 0, layer),
            ),
            columns_of(cores[0][0], 0, 3 * third), columns_of(cores[1][0], 0, 3 * third),
            whole((block, width)), whole((block, width)),
            columns_of(mixed[0], 0, third), columns_of(mixed[1], 1, third),
        ],
        [side_block(shape) for shape in shapes] + [
            whole((rows, width)), pl.BlockSpec((1, 3 * third), lambda t, *_: (0, t)),
            whole((1, width)), whole((1, width)), whole((1, width)),
        ],
        [jax.ShapeDtypeStruct(shape, BF) for shape in shapes] + [
            jax.ShapeDtypeStruct((rows, width), kind),
            jax.ShapeDtypeStruct((1, 3 * width), F32),
            short, short, short,
        ],
        [pltpu.VMEM((rows, width), BF), pltpu.VMEM((rows, width), F32)],
        14.0 * rows * width * width, 25.0e6, "attn_grad", after, prefetch=1,
    )(core, *incoming, hidden, gain, shift, weights, cores[0][0], cores[1][0], cores[0][1],
      cores[1][1], *mixed)
    return made[: len(shapes)], made[len(shapes) :]


def dense_fwd_kernel(a_ref, g_ref, b_ref, win_ref, wout_ref, bin_ref, bout_ref, x_ref, m_sc, acc):
    step = pl.program_id(0)

    @pl.when(step == 0)
    def _():
        unit, _ = norm_parts(a_ref[...])
        m_sc[...] = (unit * g_ref[...] + b_ref[...]).astype(BF)
        acc[...] = a_ref[...] + bout_ref[...]

    preact = mm(m_sc[...], flat_rows(win_ref[...])) + bin_ref[...]
    active = gelu_value(preact).astype(BF)
    acc[...] += mm_bt(active, flat_rows(wout_ref[...]))

    @pl.when(step == pl.num_programs(0) - 1)
    def _():
        x_ref[...] = acc[...]


def dense_specs(weights, at, ff):
    devices, _, rows, _ = weights.shape
    steps = ff // 2 // FF_BLOCK
    block = (devices, 1, rows, FF_BLOCK)
    start = at // FF_BLOCK
    return [
        pl.BlockSpec(block, lambda c, *_: (0, c // steps, 0, start + c % steps)),
        pl.BlockSpec(block, lambda c, *_: (0, c // steps, 0, start + steps + c % steps)),
        pl.BlockSpec((1, FF_BLOCK), lambda c, *_: (0, c)),
    ]


def dense_forward(hidden, gain, shift, weights, at, in_bias, out_bias):
    rows, width = hidden.shape
    ff = in_bias.shape[1]
    return call(
        dense_fwd_kernel, (ff // FF_BLOCK,),
        [whole((rows, width)), whole((1, width)), whole((1, width))]
        + dense_specs(weights, at, ff) + [whole((1, width))],
        whole((rows, width)),
        jax.ShapeDtypeStruct((rows, width), F32),
        [pltpu.VMEM((rows, width), BF), pltpu.VMEM((rows, width), F32)],
        4.0 * rows * width * ff, 15.0e6, "dense_fwd",
    )(hidden, gain, shift, weights, weights, in_bias, out_bias)


def dense_bwd_kernel(
    core_ref, dx_ref, a_ref, g_ref, b_ref, win_ref, wout_ref, bin_ref, *rest,
):
    dw_refs = rest[: len(rest) - 8]
    da_ref, dbin_ref, dbout_ref, dg_ref, db_ref, m_sc, low_sc, acc = rest[len(rest) - 8 :]
    step = pl.program_id(0)

    @pl.when(step == 0)
    def _():
        unit, _ = norm_parts(a_ref[...])
        m_sc[...] = (unit * g_ref[...] + b_ref[...]).astype(BF)
        low = dx_ref[...].astype(BF)
        low_sc[...] = low
        dbout_ref[...] = jnp.sum(low.astype(F32), axis=0, keepdims=True)
        acc[...] = jnp.zeros_like(acc)

    normed = m_sc[...]
    low = low_sc[...]
    in_matrix = flat_rows(win_ref[...])
    preact = mm(normed, in_matrix) + bin_ref[...]
    active, slope = gelu_pair(preact)
    preact_grad = (slope * mm(low, flat_rows(wout_ref[...]))).astype(BF)
    dbin_ref[...] = jnp.sum(preact_grad.astype(F32), axis=0, keepdims=True)
    every = slice(None)
    put_grad(dw_refs, core_ref, 1, every, mm_at(low, active.astype(BF)).astype(BF))
    put_grad(dw_refs, core_ref, 0, every, mm_at(normed, preact_grad).astype(BF))
    acc[...] += mm_bt(preact_grad, in_matrix)

    @pl.when(step == pl.num_programs(0) - 1)
    def _():
        unit, scale = norm_parts(a_ref[...])
        hidden_grad, gain_grad, shift_grad = norm_pull(unit, scale, g_ref[...], acc[...])
        da_ref[...] = dx_ref[...] + hidden_grad
        dg_ref[...] = gain_grad
        db_ref[...] = shift_grad


def dense_back(core, incoming, hidden, gain, shift, weights, at, in_bias, devices, split,
               after=()):
    rows, width = hidden.shape
    ff = in_bias.shape[1]
    shapes = grad_shapes(devices, width, ff, split)
    short = jax.ShapeDtypeStruct((1, width), F32)
    made = call(
        dense_bwd_kernel, (ff // FF_BLOCK,),
        [whole((rows, width)), whole((rows, width)), whole((1, width)), whole((1, width))]
        + dense_specs(weights, at, ff),
        [grad_block(shape, FF_BLOCK, lambda c, *_: c) for shape in shapes] + [
            whole((rows, width)), pl.BlockSpec((1, FF_BLOCK), lambda c, *_: (0, c)),
            whole((1, width)), whole((1, width)), whole((1, width)),
        ],
        [jax.ShapeDtypeStruct(shape, BF) for shape in shapes] + [
            jax.ShapeDtypeStruct((rows, width), F32), jax.ShapeDtypeStruct((1, ff), F32),
            short, short, short,
        ],
        [
            pltpu.VMEM((rows, width), BF), pltpu.VMEM((rows, width), BF),
            pltpu.VMEM((rows, width), F32),
        ],
        10.0 * rows * width * ff, 35.0e6, "dense_bwd", after, prefetch=1,
    )(core, incoming, hidden, gain, shift, weights, weights, in_bias)
    return made[: len(shapes)], made[len(shapes) :]


def pick_rows(place_ref, m, expert, capp):
    half = place_ref.shape[2]
    ids = lax.broadcasted_iota(jnp.int32, (capp, half), 0) + expert * capp
    return place_ref[m, 0:1, :] == ids, place_ref[m, 1:2, :] == ids


def as_pick(hit):
    return jnp.where(hit, 1.0, 0.0).astype(BF)


def spread_kernel(capp, own_ref, oth_ref, po_ref, pt_ref, out_ref):
    expert = pl.program_id(0)
    for m in range(own_ref.shape[0]):
        total = None
        for ref, place_ref in ((own_ref, po_ref), (oth_ref, pt_ref)):
            hit0, hit1 = pick_rows(place_ref, m, expert, capp)
            part = mm(as_pick(hit0 | hit1), ref[m])
            total = part if total is None else total + part
        out_ref[0, m * capp : (m + 1) * capp, :] = total.astype(BF)


def spread_rows(own, oth, place_own, place_oth, experts, capp):
    micro, half, width = own.shape
    slots = micro * capp
    (out,) = call(
        functools.partial(spread_kernel, capp), (experts,),
        [whole(own.shape), whole(oth.shape), whole(place_own.shape), whole(place_oth.shape)],
        [pl.BlockSpec((1, slots, width), lambda e: (e, 0, 0))],
        [jax.ShapeDtypeStruct((experts, slots, width), BF)],
        [], 4.0 * experts * slots * half * width, 9.0e6, "spread",
    )(own, oth, place_own, place_oth)
    return out


def moe_kernel(
    capp,
    rb_own0, rb_own1, rb_oth0, rb_oth1, og_ref, po_ref, pt_ref, w_ref,
    win_ref, wout_ref, bin_ref, bout_ref,
    y_ref, r_ref, d_ref, dw_ref, dbin_ref, dbout_ref,
    b_sc, dy_sc, w_sc, y_acc, r_acc,
):
    micro = 2
    expert = pl.program_id(0)
    chunk = pl.program_id(1)
    last_chunk = chunk == pl.num_programs(1) - 1
    rb_all = ((rb_own0, rb_oth0), (rb_own1, rb_oth1))

    @pl.when(chunk == 0)
    def _():
        for m in range(micro):
            slots = slice(m * capp, (m + 1) * capp)
            rows = gate = None
            for side, place_ref in enumerate((po_ref, pt_ref)):
                hit0, hit1 = pick_rows(place_ref, m, expert, capp)
                part = mm(as_pick(hit0 | hit1), rb_all[m][side][...])
                weight = jnp.sum(
                    jnp.where(hit0, w_ref[m, 2 * side : 2 * side + 1, :], 0.0)
                    + jnp.where(hit1, w_ref[m, 2 * side + 1 : 2 * side + 2, :], 0.0),
                    axis=-1, keepdims=True,
                )
                rows = part if side == 0 else rows + part
                gate = weight if side == 0 else gate + weight
            b_sc[slots, :] = rows.astype(BF)
            dy_sc[slots, :] = (og_ref[0, slots, :].astype(F32) * gate).astype(BF)
            w_sc[slots, :] = jnp.broadcast_to(gate, (capp, w_sc.shape[1]))

    tokens = b_sc[...]
    low = dy_sc[...]
    preact = mm(tokens, win_ref[...]) + bin_ref[0]
    active, slope = gelu_pair(preact)
    active = active.astype(BF)
    preact_grad = (slope * mm(low, wout_ref[...])).astype(BF)
    dbin_ref[0] = jnp.sum(preact_grad.astype(F32), axis=0, keepdims=True)
    result = mm_bt(active, wout_ref[...])
    rows_grad = mm_bt(preact_grad, win_ref[...])
    every = slice(None)
    put_grad((dw_ref,), None, 1, every, mm_at(low, active).astype(BF))
    put_grad((dw_ref,), None, 0, every, mm_at(tokens, preact_grad).astype(BF))

    @pl.when(chunk == 0)
    def _():
        y_acc[...] = jnp.zeros_like(y_acc)
        r_acc[...] = jnp.zeros_like(r_acc)

    @pl.when(jnp.logical_not(last_chunk))
    def _():
        y_acc[...] += result
        r_acc[...] += rows_grad

    @pl.when(last_chunk)
    def _():
        dbout_ref[0] = jnp.sum(dy_sc[...].astype(F32), axis=0, keepdims=True)
        total = y_acc[...] + result + 0.5 * bout_ref[0]
        dots = jnp.sum(og_ref[0].astype(F32) * total, axis=-1, keepdims=True)
        high = dots.astype(BF)
        rest = dots - high.astype(F32)
        mid = rest.astype(BF)
        tiny = (rest - mid.astype(F32)).astype(BF)
        lanes = lax.broadcasted_iota(jnp.int32, d_ref.shape[1:], 1)
        zero = jnp.zeros(d_ref.shape[1:], BF)
        d_ref[0] = jnp.where(
            lanes == expert, high,
            jnp.where(lanes == 8 + expert, mid, jnp.where(lanes == 16 + expert, tiny, zero)),
        )
        y_ref[0] = (w_sc[:, 0:1] * total).astype(BF)
        r_ref[0] = (r_acc[...] + rows_grad).astype(BF)


def mixture(rows_own, rows_oth, grad_rows, place_own, place_oth, gates, weights, in_bias,
            out_bias, capp, devices):
    half, width = rows_own[0].shape
    experts, slots, _ = grad_rows.shape
    ff = in_bias.shape[2]
    block = EXPERT_BLOCK
    steps = ff // block
    blocks = experts * steps
    w_block = (width, block)
    flat = (half, width)
    (shape,) = grad_shapes(devices, width, experts * ff, False)
    by_expert = pl.BlockSpec((1, slots, width), lambda e, c: (e, 0, 0))
    return call(
        functools.partial(moe_kernel, capp),
        (experts, steps),
        [
            whole(flat), whole(flat), whole(flat), whole(flat), by_expert,
            whole(place_own.shape), whole(place_oth.shape), whole(gates.shape),
            pl.BlockSpec(w_block, lambda e, c: (0, e * steps + c)),
            pl.BlockSpec(w_block, lambda e, c: (0, blocks + e * steps + c)),
            pl.BlockSpec((1, 1, block), lambda e, c: (e, 0, c)),
            pl.BlockSpec((1, 1, width), lambda e, c: (e, 0, 0)),
        ],
        [
            by_expert, by_expert, pl.BlockSpec((1, slots, 128), lambda e, c: (e, 0, 0)),
            grad_block(shape, block, lambda e, c: e * steps + c),
            pl.BlockSpec((1, 1, block), lambda e, c: (e, 0, c)),
            pl.BlockSpec((1, 1, width), lambda e, c: (e, 0, 0)),
        ],
        [
            jax.ShapeDtypeStruct((experts, slots, width), BF),
            jax.ShapeDtypeStruct((experts, slots, width), BF),
            jax.ShapeDtypeStruct((experts, slots, 128), BF),
            jax.ShapeDtypeStruct(shape, BF),
            jax.ShapeDtypeStruct((experts, 1, ff), F32),
            jax.ShapeDtypeStruct((experts, 1, width), F32),
        ],
        [
            pltpu.VMEM((slots, width), BF), pltpu.VMEM((slots, width), BF),
            pltpu.VMEM((slots, 128), F32),
            pltpu.VMEM((slots, width), F32), pltpu.VMEM((slots, width), F32),
        ],
        12.0 * slots * experts * width * ff + 4.0 * experts * slots * half * width,
        60.0e6, "experts",
    )(*rows_own, *rows_oth, grad_rows, place_own, place_oth, gates, weights, weights,
      in_bias, out_bias)


def collect_kernel(capp, jobs, *refs):
    picks = {}
    for m, place, source, out, kind in jobs:
        rows_ref, out_ref = refs[source], refs[out]
        experts = rows_ref.shape[0]
        half = refs[place].shape[1]
        if (m, place) not in picks:
            hits = []
            for expert in range(experts):
                ids = lax.broadcasted_iota(jnp.int32, (half, capp), 1) + expert * capp
                hit = (refs[place][m, :, 0:1] == ids) | (refs[place][m, :, 1:2] == ids)
                hits.append(as_pick(hit))
            picks[m, place] = hits
        total = None
        for expert, pick in enumerate(picks[m, place]):
            rows = rows_ref[expert, m * capp : (m + 1) * capp, :]
            if kind == "dots":
                part = lax.dot_general(
                    rows, pick, (((0,), (1,)), ((), ())), preferred_element_type=F32
                )
            else:
                part = mm(pick, rows)
            total = part if total is None else total + part
        if kind == "dots":
            total = total[0:8] + total[8:16] + total[16:24]
        if len(out_ref.shape) == 3:
            out_ref[m] = total.astype(out_ref.dtype)
        else:
            out_ref[...] = total.astype(out_ref.dtype)


def collect(capp, arrays, outs, jobs, name, after=()):
    experts, slots, width = arrays[-1].shape
    return call(
        functools.partial(collect_kernel, capp, tuple(jobs)), (1,),
        [whole(value.shape) for value in arrays], [whole(shape) for shape, _ in outs],
        [jax.ShapeDtypeStruct(shape, kind) for shape, kind in outs], [],
        2.0 * len(jobs) * arrays[0].shape[1] * experts * capp * width, 8.0e6, name, after,
    )(*arrays)


def gate_bwd_kernel(
    a_ref, og_ref, held_ref, ro_ref, rr_ref, do_ref, dr_ref, gp_ref, rt_ref, g_ref, b_ref,
    sent_ref, da_ref, drt_ref, dg_ref, db_ref,
):
    after = a_ref[...]
    incoming = og_ref[0].astype(F32)
    sent_ref[...] = held_ref[...]
    gates = gp_ref[...]
    found = do_ref[0] + dr_ref[0]
    spread = jnp.where(
        lax.broadcasted_iota(jnp.int32, (found.shape[0], gates.shape[1]), 0)
        == lax.broadcasted_iota(jnp.int32, (found.shape[0], gates.shape[1]), 1),
        1.0, 0.0,
    )
    gate_grad = lax.dot_general(
        found, spread, (((0,), (0,)), ((), ())), precision=EXACT, preferred_element_type=F32
    )
    logit_grad = gates * (gate_grad - jnp.sum(gates * gate_grad, axis=-1, keepdims=True))
    unit, scale = norm_parts(after)
    normed = unit * g_ref[...] + b_ref[...]
    drt_ref[...] = lax.dot_general(
        logit_grad, normed, (((0,), (0,)), ((), ())), precision=EXACT, preferred_element_type=F32
    )
    normed_grad = ro_ref[0].astype(F32) + rr_ref[...].astype(F32)
    for expert in range(rt_ref.shape[0]):
        normed_grad += logit_grad[:, expert : expert + 1] * rt_ref[expert : expert + 1, :]
    hidden_grad, gain_grad, shift_grad = norm_pull(unit, scale, g_ref[...], normed_grad)
    da_ref[...] = incoming + hidden_grad
    dg_ref[...] = gain_grad
    db_ref[...] = shift_grad


def gate_back(after, incoming, held, r_own, r_got, d_own, d_got, gates, router, gain, shift,
              which, behind=()):
    block, width = after.shape
    lanes = gates.shape[1]
    one = pl.BlockSpec((1, block, width), lambda *_: (which, 0, 0))
    dots = pl.BlockSpec((1, 8, block), lambda *_: (which, 0, 0))
    flat = whole((block, width))
    low = whole((block, lanes))
    return call(
        gate_bwd_kernel, (1,),
        [
            flat, one, whole(held.shape), one, flat, dots, dots, low,
            whole(router.shape), whole((1, width)), whole((1, width)),
        ],
        [whole(held.shape), flat, whole((lanes, width)), whole((1, width)), whole((1, width))],
        [
            jax.ShapeDtypeStruct(held.shape, BF),
            jax.ShapeDtypeStruct((block, width), F32),
            jax.ShapeDtypeStruct((lanes, width), F32),
            jax.ShapeDtypeStruct((1, width), F32),
            jax.ShapeDtypeStruct((1, width), F32),
        ],
        [], 4.0 * block * width * lanes, 7.0e6, "gate_bwd", behind,
    )(after, incoming, held, r_own, r_got, d_own, d_got, gates, router, gain, shift)


def swap(value):
    return lax.ppermute(value, "tensor", [(0, 1), (1, 0)])


def in_order(mine, other, axis):
    first = lax.axis_index("tensor") == 0
    return jnp.stack([jnp.where(first, mine, other), jnp.where(first, other, mine)], axis=axis)


def gather_rows(share):
    return lax.all_gather(share, "dp", axis=0, tiled=True)


def ring_chip(place, chips):
    half = chips // 2
    even = 2 * place
    odd = 2 * (chips - 1 - place) + 1
    if isinstance(place, int):
        return even if place < half else odd
    return jnp.where(place < half, even, odd)


def ring_add(kind, refs):
    def chunk(grads, given):
        return grads[0].astype(F32) + given[0].astype(F32)

    if kind == 0:
        grads, given, ahead, behind = refs
        total = chunk(grads, given).astype(BF)
        ahead[...] = total[0]
        behind[...] = total[1]
    elif kind == 3:
        grads, given, got_a, got_b, out = refs
        out[...] = chunk(grads, given) + (got_a[...].astype(F32) + got_b[...].astype(F32))
    elif kind == 4:
        one, two, out = refs
        out[...] = one[...] + two[...]
    else:
        grads_a, given_a, grads_b, given_b, got_a, got_b, ahead, behind = refs
        one, two = chunk(grads_a, given_a), chunk(grads_b, given_b)
        if kind == 1:
            ahead[0] = (one[0] + got_a[...].astype(F32)).astype(BF)
            ahead[1] = one[1].astype(BF)
            behind[0] = two[0].astype(BF)
            behind[1] = (two[1] + got_b[...].astype(F32)).astype(BF)
        else:
            ahead[...] = (one + got_a[...].astype(F32)).astype(BF)
            behind[...] = (two + got_b[...].astype(F32)).astype(BF)


def step_kernel(plans, _, *refs):
    taken = sum(ins for _, ins, _ in plans)
    at, out_at = 0, taken
    for kind, ins, outs in plans:
        ring_add(kind, refs[at : at + ins] + refs[out_at : out_at + outs])
        at += ins
        out_at += outs


def step_all(chains, after=()):
    live = [chain for chain in chains if not chain.finished()]
    if not live:
        return tuple(after)
    stages = [chain.stage(index) for index, chain in enumerate(live)]
    places = jnp.stack([place for stage in stages for place in stage[1]]).astype(jnp.int32)
    sums = call(
        functools.partial(
            step_kernel, tuple((stage[0], len(stage[2]), len(stage[4])) for stage in stages)
        ),
        (1,), [spec for stage in stages for spec in stage[2]],
        [whole(out.shape) for stage in stages for out in stage[4]],
        [out for stage in stages for out in stage[4]], [], 0, 2.0e6, "ring_add", after,
        prefetch=1,
    )(places, *[value for stage in stages for value in stage[3]])
    at = 0
    for chain, stage in zip(live, stages):
        chain.take(sums[at : at + len(stage[4])])
        at += len(stage[4])
    return tuple(sums[:1])


class RingSum:
    def __init__(self, kept, sent):
        count = lax.axis_size("dp")
        self.chips = count // 2
        self.ring = [ring_chip(place, self.chips) for place in range(self.chips)]
        chip = lax.axis_index("dp") // 2
        self.here = jnp.where(chip % 2 == 0, chip // 2, self.chips - 1 - chip // 2)
        self.kept = kept
        self.away = self.chips // 2
        self.messages = (sent,)
        self.given = lax.ppermute(sent, "dp", [(at, at ^ 1) for at in range(count)])
        self.got = ()
        self.result = None

    def send(self, value, step):
        pairs = [
            (self.ring[at] * 2 + side, self.ring[(at + step) % self.chips] * 2 + side)
            for at in range(self.chips)
            for side in range(2)
        ]
        return lax.ppermute(value, "dp", pairs)

    def finished(self):
        return self.result is not None

    def stage(self, index):
        away = self.away
        chips = [
            ring_chip((self.here + far) % self.chips, self.chips)
            for far in (away, self.chips - away)
        ]
        shape = self.kept.shape[1:]

        def chunk_specs(which):
            slot = 2 * index + which
            return [pl.BlockSpec((1,) + shape, lambda _, at: (at[slot], 0, 0, 0))] * 2

        far = self.chips // 2
        kind = 3 if away == 0 else 0 if away == far else 1 if away == far - 1 else 2
        two_ways = kind in (1, 2)
        in_specs = chunk_specs(0) + (chunk_specs(1) if two_ways else [])
        in_specs += [whole(got.shape) for got in self.got]
        args = [self.kept, self.given] * (2 if two_ways else 1) + list(self.got)
        out = shape if kind else shape[1:]
        outs = [jax.ShapeDtypeStruct(out, F32 if kind == 3 else BF)] * (1 if kind == 3 else 2)
        return kind, chips, in_specs, args, outs

    def take(self, sums):
        if self.away == 0:
            self.result = sums[0]
            self.messages = ()
            return
        self.away -= 1
        self.messages = tuple(sums)
        self.got = (self.send(sums[0], 1), self.send(sums[1], -1))


class PlainSum:
    def __init__(self, grad):
        axis = 1 if grad.ndim == 3 else 0
        done = lax.psum_scatter(grad, "dp", scatter_dimension=axis, tiled=True)
        self.messages = (done,)
        self.result = done.reshape((2,) + done.shape[-2:]).astype(F32)

    def finished(self):
        return True


def hold_kernel(value_ref, out_ref):
    return


def hold(value, after):
    anywhere = pl.BlockSpec(memory_space=pl.ANY)
    return call(
        hold_kernel, (1,), [anywhere], anywhere, jax.ShapeDtypeStruct(value.shape, value.dtype),
        [], 0, 1.0e3, "hold", after, aliases={0: 0},
    )(value)


def expert_out_kernel(sum_ref, in_ref, out_ref):
    experts, ff = in_ref.shape[1], in_ref.shape[2]
    for part, ref in enumerate((in_ref, out_ref)):
        for expert in range(experts):
            ref[:, expert, :] = sum_ref[part, :, expert * ff : (expert + 1) * ff].astype(F32)


def expert_outputs(total, shape, after):
    return call(
        expert_out_kernel, (1,), [whole(total.shape)], [whole(shape)] * 2,
        [jax.ShapeDtypeStruct(shape, F32)] * 2, [], 0, 4.0e6, "expert_out", after,
    )(total)


class PairSum:
    def __init__(self, value):
        self.count = lax.axis_size("dp")
        self.value = value
        self.reach = 1
        self.send()

    def send(self):
        self.messages = (self.value,)
        if self.reach < self.count:
            pairs = [(at, at ^ self.reach) for at in range(self.count)]
            self.got = lax.ppermute(self.value, "dp", pairs)
        elif self.reach == self.count:
            self.got = swap(self.value)
        else:
            self.got = None
            self.messages = ()
        self.reach *= 2

    def finished(self):
        return self.got is None

    def stage(self, index):
        zero = jnp.zeros((), jnp.int32)
        shape = self.value.shape
        return (
            4, [zero, zero], [whole(shape)] * 2, [self.value, self.got],
            [jax.ShapeDtypeStruct(shape, F32)],
        )

    def take(self, sums):
        (self.value,) = sums
        self.send()


def pack_kernel(plan, side_ref, *refs):
    out_ref = refs[-1]
    width = out_ref.shape[1]
    out_ref[...] = jnp.zeros_like(out_ref)
    at = 0
    for inputs, rows, factor, sided in plan:
        total = None
        for which in inputs:
            ref = refs[which]
            value = ref[...].reshape(-1, ref.shape[-1])[:rows]
            total = value if total is None else total + value
        total = total * factor if factor != 1.0 else total
        parts = total.shape[1] // width
        for row in range(rows):
            for part in range(parts):
                piece = total[row : row + 1, part * width : (part + 1) * width]
                place = at + row * parts + part
                if sided:
                    place = place + side_ref[0] * (rows * parts)
                out_ref[pl.ds(place, 1), :] = piece
        at += rows * parts * (2 if sided else 1)


def pack_rows(groups, width):
    arrays, plan, total = [], [], 0
    for values, rows, factor, sided in groups:
        plan.append((tuple(range(len(arrays), len(arrays) + len(values))), rows, factor, sided))
        arrays += values
        total += rows * (values[0].shape[-1] // width) * (2 if sided else 1)
    shape = (round_up(total, 8), width)
    side = lax.axis_index("tensor").reshape(1)
    (out,) = call(
        functools.partial(pack_kernel, tuple(plan)), (1,),
        [whole(value.shape) for value in arrays], [whole(shape)],
        [jax.ShapeDtypeStruct(shape, F32)], [], 0, 3.0e5, "pack", (), prefetch=1,
    )(side, *arrays)
    return out


def out_kernel(a0_ref, a1_ref, y_ref, got_ref, out_ref):
    for m, a_ref in enumerate((a0_ref, a1_ref)):
        total = a_ref[...] + (y_ref[m].astype(F32) + got_ref[m].astype(F32))
        out_ref[m] = total.astype(BF)


def layer_output(hidden, y_own, y_got, after):
    shape = y_own.shape
    (out,) = call(
        out_kernel, (1,),
        [whole(hidden[0].shape)] * 2 + [whole(shape)] * 2, [whole(shape)],
        [jax.ShapeDtypeStruct(shape, BF)], [], 0, 8.0e6, "layer_output", after,
    )(*hidden, y_own, y_got)
    return out


def place_kernel(side_ref, own_ref, got_ref, out_ref):
    images, length = own_ref.shape[1], out_ref.shape[2]
    side = side_ref[0]
    for image in range(images):
        kept = own_ref[:, image, :length, :].astype(out_ref.dtype)
        out_ref[:, side * images + image] = kept
        other = got_ref[:, image, :length, :].astype(out_ref.dtype)
        out_ref[:, (1 - side) * images + image] = other


def place_images(own, got, shape, kind, after):
    micro, images, length, width = shape
    padded = (micro, images // 2, own.size // (micro * (images // 2) * width), width)
    side = lax.axis_index("tensor").reshape(1)
    (out,) = call(
        place_kernel, (micro,),
        [pl.BlockSpec((1,) + padded[1:], lambda m, *_: (m, 0, 0, 0))] * 2,
        [pl.BlockSpec((1,) + shape[1:], lambda m, *_: (m, 0, 0, 0))],
        [jax.ShapeDtypeStruct(shape, kind)], [], 0, 8.0e6, "place", after, prefetch=1,
    )(side, own.reshape(padded), got.reshape(padded))
    return out


def join_sides(mine_first):
    mine = lax.axis_index("tensor")
    kept = lax.dynamic_index_in_dim(mine_first, mine, 0, keepdims=False)
    sent = lax.dynamic_index_in_dim(mine_first, 1 - mine, 0, keepdims=False)
    return kept + swap(sent.astype(BF)).astype(F32)


def own_half(value, axis):
    size = value.shape[axis] // 2
    return lax.dynamic_slice_in_dim(value, lax.axis_index("tensor") * size, size, axis)


def local(
    block_input, norm_gain, row_bias, qkv_weight, qkv_bias, out_weight, mlp_in, mlp_in_bias,
    mlp_out, mlp_out_bias, router, expert_in, expert_in_bias, expert_out, expert_out_bias,
    routes, slot_index, out_grad,
):
    micro, images, length, width = block_input.shape
    experts = router.shape[1]
    share_rows = mlp_in.shape[0]
    own_images = images // 2
    pad = round_up(length, ROW_PAD)
    half = own_images * pad
    rows = micro * half
    capp = round_up(CAP, ROW_PAD)
    side = lax.axis_index("tensor")

    def attn_share(layer):
        return jnp.concatenate(
            [qkv_weight[layer].reshape(share_rows, -1), out_weight[layer]], axis=1
        )

    devices = lax.axis_size("dp")
    first_mine = jnp.concatenate([attn_share(0), attn_share(1), mlp_in, mlp_out], axis=1)
    first_w = lax.all_gather(
        in_order(first_mine, swap(first_mine), 0), "dp", axis=0, tiled=False
    )
    if not whole_tiles(devices, width):
        first_w = jnp.moveaxis(first_w, 0, 1).reshape(1, 2, width, -1)
    dense_at = 4 * width
    expert_w = gather_rows(
        jnp.concatenate(
            [expert_in.reshape(share_rows, -1), expert_out.reshape(share_rows, -1)], axis=1
        )
    )

    biases = jnp.concatenate([qkv_bias.reshape(-1), mlp_in_bias])
    bias_pair = in_order(biases, swap(biases), 0)
    qkv_bias_pair = bias_pair[:, : qkv_bias.size].reshape((2,) + qkv_bias.shape)
    mlp_bias_full = bias_pair[:, qkv_bias.size :].reshape(1, -1)

    def qkv_bias_row(layer):
        pair = qkv_bias_pair[:, layer]
        zero = jnp.zeros_like(pair[:, 0])
        return jnp.concatenate([pair[:, 0], zero, pair[:, 1]], axis=1).reshape(1, -1)

    def padded(value, start):
        part = lax.dynamic_slice_in_dim(value, start, own_images, 1)
        return jnp.pad(part, ((0, 0), (0, 0), (0, pad - length), (0, 0)))

    mine_at = side * own_images
    other_at = (1 - side) * own_images
    hidden = padded(block_input, mine_at).astype(F32).reshape(rows, width)
    grad_own = padded(out_grad, mine_at).reshape(micro, half, width)
    grad_oth = padded(out_grad, other_at).reshape(micro, half, width)

    kept = slot_index < CAP
    place = jnp.where(kept, routes * capp + slot_index, -1)
    pick = jnp.where(kept, routes, -1)

    def lay(value, start):
        part = lax.dynamic_slice_in_dim(value, start, own_images, 1)
        part = jnp.pad(
            part, ((0, 0), (0, 0), (0, pad - length), (0, 0)), constant_values=-1
        )
        return part.reshape(micro, half, 2)

    place_own, place_oth = lay(place, mine_at), lay(place, other_at)
    place_own_rows = jnp.swapaxes(place_own, 1, 2)
    place_oth_rows = jnp.swapaxes(place_oth, 1, 2)
    grad_rows = spread_rows(
        grad_own, grad_oth, place_own_rows, place_oth_rows, experts, capp
    )
    select = lay(pick, mine_at).reshape(rows, 2)
    router_wide = jnp.pad(router, ((0, 0), (0, 128 - experts)))

    def row(vector):
        return vector.reshape(1, -1)

    qkv_one, lse_one, mix_one, after_one = attention_forward(
        hidden, row(norm_gain[0, 0]), row(row_bias[0, 0]), first_w, 0, qkv_bias_row(0),
        row(row_bias[0, 2]), length, pad, 0, micro,
    )
    after_ffn = dense_forward(
        after_one, row(norm_gain[0, 1]), row(row_bias[0, 1]), first_w, dense_at, mlp_bias_full,
        row(mlp_out_bias),
    )
    second = [
        attention_forward(
            after_ffn, row(norm_gain[1, 0]), row(row_bias[1, 0]), first_w, 1, qkv_bias_row(1),
            row(row_bias[1, 2]), length, pad, m, 1,
            (row(norm_gain[1, 1]), row(row_bias[1, 1]), router_wide, select, experts),
        )
        for m in range(micro)
    ]
    qkv_two, lse_two, mix_two, after_two, rows_own, gates, chosen = zip(*second)
    rows_oth = [swap(part) for part in rows_own]
    gate_own = jnp.stack([part[:, :2].T for part in chosen])
    gate_pair = jnp.concatenate([gate_own, swap(gate_own)], axis=1)
    ring = whole_tiles(devices, width)
    core = (lax.axis_index("dp") % 2).reshape(1)
    y_slots, r_slots, d_slots, expert_grad, ein_bias, eout_bias = mixture(
        rows_own, rows_oth, grad_rows, place_own_rows, place_oth_rows, gate_pair, expert_w,
        expert_in_bias.reshape(experts, 1, -1), expert_out_bias.reshape(experts, 1, -1), capp,
        devices,
    )
    group, one, dots = (micro, half, width), (half, width), (micro, 8, half)
    r_oth0, r_oth1, d_oth = collect(
        capp, (place_oth, d_slots, r_slots), ((one, BF), (one, BF), (dots, F32)),
        (
            (0, 0, 2, 3, "rows"), (1, 0, 2, 4, "rows"), (0, 0, 1, 5, "dots"),
            (1, 0, 1, 5, "dots"),
        ),
        "collect_first",
    )
    y_own, y_oth, r_own, d_own = collect(
        capp, (place_own, place_oth, d_slots, r_slots, y_slots),
        ((group, BF), (group, BF), (group, BF), (dots, F32)),
        (
            (0, 0, 3, 7, "rows"), (1, 0, 3, 7, "rows"), (0, 0, 2, 8, "dots"),
            (1, 0, 2, 8, "dots"), (0, 0, 4, 5, "rows"), (1, 0, 4, 5, "rows"),
            (0, 1, 4, 6, "rows"), (1, 1, 4, 6, "rows"),
        ),
        "collect_rest", (r_oth0,),
    )
    d_got = swap(d_oth)
    r_got = swap(r_oth0)
    expert_sum = PlainSum(expert_grad)
    grad_two, gate_parts, cores = [], [], []
    for m, held in enumerate((r_oth1, y_oth)):
        sent, grad_part, *small = gate_back(
            after_two[m], grad_own, held, r_own, r_got, d_own, d_got, gates[m],
            router.T, row(norm_gain[1, 1]), row(row_bias[1, 1]), m,
            (cores[0][1],) if m else (),
        )
        r_got = swap(sent)
        grad_two.append(grad_part)
        gate_parts.append(small)
        cores.append(
            attention_core_back(
                grad_part, first_w, 1, (qkv_two[m], lse_two[m], half), length, pad, m, (sent,)
            )
        )
    y_got = r_got
    router_parts, gain_parts, shift_parts = (list(pair) for pair in zip(*gate_parts))
    two_grad, (grad_ffn, qb_two, ob_two, gain_two, shift_two) = attention_grad(
        core, grad_two, after_ffn, row(norm_gain[1, 0]), row(row_bias[1, 0]), first_w, 1, cores,
        mix_two, devices, ring, F32,
    )
    sum_two = RingSum(*two_grad) if ring else PlainSum(*two_grad)
    out_own = layer_output(after_two, y_own, y_got, (gain_two,))
    out_got = swap(out_own)
    early = (
            [
                ([gain_two], 1, 1.0, False), (gain_parts, 1, 1.0, False),
                ([shift_two], 1, 1.0, False), (shift_parts, 1, 1.0, False),
                ([ob_two], 1, 1.0, False), ([qb_two], 1, 1.0, False),
                (router_parts, experts, 1.0, False), ([eout_bias], experts, 0.5, False),
                ([ein_bias], experts, 1.0, True),
            ]
    )
    dense_grad, (grad_one, in_bias_grad, out_bias_grad, gain_ffn, shift_ffn) = dense_back(
        core, grad_ffn, after_one, row(norm_gain[0, 1]), row(row_bias[0, 1]), first_w, dense_at,
        mlp_bias_full, devices, ring, sum_two.messages + (out_own,),
    )
    last = step_all([sum_two], (gain_ffn, out_got))
    if ring:
        dense_sum = RingSum(dense_grad[0], hold(dense_grad[1], last))
    else:
        dense_sum = PlainSum(*dense_grad)
    block_output = place_images(out_own, out_got, block_input.shape, BF, last)
    step_all([dense_sum], (block_output,))
    cores = []
    for which in range(2):
        cores.append(
            attention_core_back(
                grad_one, first_w, 0, (qkv_one, lse_one, half), length, pad, which,
                sum_two.messages + dense_sum.messages + (block_output,),
            )
        )
        step_all([sum_two, dense_sum], (cores[-1][1],))
    one_grad, (grad_zero, qb_one, ob_one, gain_one, shift_one) = attention_grad(
        core, (grad_one, grad_one), hidden, row(norm_gain[0, 0]), row(row_bias[0, 0]), first_w,
        0, cores, (mix_one, mix_one), devices, False, BF,
        sum_two.messages + dense_sum.messages,
    )
    last = step_all([sum_two, dense_sum], (qb_one,))
    one_sum = PlainSum(hold(one_grad[0], expert_sum.messages + last))
    late_sum = PairSum(
        pack_rows(
            [
                ([gain_one], 1, 1.0, False), ([gain_ffn], 1, 1.0, False),
                ([shift_one], 1, 1.0, False), ([shift_ffn], 1, 1.0, False),
                ([ob_one], 1, 1.0, False), ([qb_one], 1, 1.0, False),
                ([in_bias_grad], 1, 1.0, False), ([out_bias_grad], 1, 1.0, False),
            ] + early,
            width,
        )
    )
    expert_total = expert_sum.messages[0].reshape((2, share_rows, -1))
    expert_grads = expert_outputs(expert_total, expert_in.shape, last)
    last = (expert_grads[0],)
    grad_got = swap(grad_zero)
    for turn in range(devices):
        last = step_all([sum_two, dense_sum, late_sum], last)
        if turn == 2:
            input_grad = place_images(grad_zero, grad_got, block_input.shape, F32, last)
            last = (input_grad,)

    one_done = join_sides(one_sum.result)
    joined = join_sides(
        jnp.concatenate(
            [
                sum_two.result[:, None],
                jnp.moveaxis(dense_sum.result.reshape(2, share_rows, 2, -1), 2, 0),
            ],
            axis=1,
        )
    )
    attn_grads, dense_done = [one_done, joined[0]], joined[1:]
    split_at = 3 * width // 2

    late = late_sum.value
    ff_rows = in_bias_grad.shape[1] // width
    early = late[9 + ff_rows :]
    gain_sum = jnp.concatenate([late[0:2], early[0:2]])
    shift_sum = jnp.concatenate([late[2:5], early[2:5]])
    qb_sum = jnp.stack([late[5:8], early[5:8]]).reshape(2, 2, 3, width // 2)
    qb_sum = lax.dynamic_index_in_dim(qb_sum, side, 1, keepdims=False)
    in_bias_sum = late[8 : 8 + ff_rows]
    out_bias_sum = late[8 + ff_rows]
    at = 8 + experts
    router_sum = early[8:at]
    eout_sum = early[at : at + experts]
    at += experts
    ein_rows = expert_in_bias.size // width
    ein_sum = lax.dynamic_slice_in_dim(early, at + side * ein_rows, ein_rows, 0)
    return (
        block_output,
        input_grad,
        gain_sum.reshape(norm_gain.shape),
        shift_sum.reshape(row_bias.shape),
        jnp.stack([part[:, :split_at] for part in attn_grads]).reshape(qkv_weight.shape),
        jnp.stack([qb_sum[:, 0], qb_sum[:, 2]], axis=1),
        jnp.stack([part[:, split_at:] for part in attn_grads]),
        dense_done[0],
        own_half(in_bias_sum.reshape(-1), 0),
        dense_done[1],
        out_bias_sum.reshape(-1),
        router_sum.T,
        expert_grads[0],
        ein_sum.reshape(expert_in_bias.shape),
        expert_grads[1],
        eout_sum.reshape(experts, width),
    )


def solution(mesh):
    return jax.shard_map(
        local,
        mesh=mesh,
        in_specs=(
            P(None, "dp", None, None), P(), P(), P(None, "dp", None, "tensor"),
            P(None, None, "tensor"), P(None, "dp", "tensor"), P("dp", "tensor"), P("tensor"),
            P("dp", "tensor"), P(), P(), P("dp", None, "tensor"), P(None, "tensor"),
            P("dp", None, "tensor"), P(), P(None, "dp", None, None), P(None, "dp", None, None),
            P(None, "dp", None, None),
        ),
        out_specs=(
            P(None, "dp", None, None), P(None, "dp", None, None), P(), P(),
            P(None, "dp", None, "tensor"), P(None, None, "tensor"), P(None, "dp", "tensor"),
            P("dp", "tensor"), P("tensor"), P("dp", "tensor"), P(), P(),
            P("dp", None, "tensor"), P(None, "tensor"), P("dp", None, "tensor"), P(),
        ),
        check_vma=False,
    )
```
